32 devices in a mesh: dp: 16 (over z, y, core), seq: 2 (over x).
Axes of the slice: x: 2, y: 2, z: 4, core: 2. Of those that a mesh axis runs over, the one named last changes fastest.
Arguments:
- tokens: bfloat16 [16384, 1024], P(('dp', 'seq')), may hold values from -6 to 6
- segments: int32 [16, 1024], P('dp'), may hold values from 0 to 2, as said below
- input_gain: bfloat16 [1024], P(('dp', 'seq')), may hold values from 0.5 to 1.5
- mixer_in: bfloat16 [1024, 3352], P('dp', 'seq'), may hold values from -0.1875 to 0.1875
- conv_weight: bfloat16 [1792, 4], P(('dp', 'seq')), may hold values from -3 to 3
- conv_bias: bfloat16 [1792], P(('dp', 'seq')), may hold values from -3 to 3
- step_bias: float32 [24], replicated, may hold values from -4.5 to -2.5
- decay_log: float32 [24], replicated, may hold values from -4 to 0
- skip_gain: float32 [24], replicated, may hold values from 0.5 to 1.5
- mixer_gain: bfloat16 [1536], P(('dp', 'seq')), may hold values from 0.5 to 1.5
- mixer_out: bfloat16 [1536, 1024], P('dp', 'seq'), may hold values from -0.15625 to 0.15625
- w_query: bfloat16 [1024, 512], P('dp', 'seq'), may hold values from -0.1875 to 0.1875
- w_key: bfloat16 [1024, 128], P('dp', 'seq'), may hold values from -0.1875 to 0.1875
- w_value: bfloat16 [1024, 128], P('dp', 'seq'), may hold values from -0.1875 to 0.1875
- w_output: bfloat16 [512, 1024], P('dp', 'seq'), may hold values from -3 to 3
- hidden_gain: bfloat16 [1024], P(('dp', 'seq')), may hold values from 0.5 to 1.5
- w_gate: bfloat16 [1024, 2048], P('dp', 'seq'), may hold values from -0.1875 to 0.1875
- w_up: bfloat16 [1024, 2048], P('dp', 'seq'), may hold values from -0.1875 to 0.1875
- w_down: bfloat16 [2048, 1024], P('dp', 'seq'), may hold values from -0.125 to 0.125
- cotangent: bfloat16 [16384, 1024], P(('dp', 'seq')), may hold values from -6 to 6
Outputs:
- output: bfloat16 [16384, 1024], P(('dp', 'seq'))
- grad_tokens: float32 [16384, 1024], P(('dp', 'seq'))
- grad_input_gain: float32 [1024], P(('dp', 'seq'))
- grad_mixer_in: float32 [1024, 3352], P('dp', 'seq')
- grad_conv_weight: float32 [1792, 4], P(('dp', 'seq'))
- grad_conv_bias: float32 [1792], P(('dp', 'seq'))
- grad_step_bias: float32 [24], replicated
- grad_decay_log: float32 [24], replicated
- grad_skip_gain: float32 [24], replicated
- grad_mixer_gain: float32 [1536], P(('dp', 'seq'))
- grad_mixer_out: float32 [1536, 1024], P('dp', 'seq')
- grad_w_query: float32 [1024, 512], P('dp', 'seq')
- grad_w_key: float32 [1024, 128], P('dp', 'seq')
- grad_w_value: float32 [1024, 128], P('dp', 'seq')
- grad_w_output: float32 [512, 1024], P('dp', 'seq')
- grad_hidden_gain: float32 [1024], P(('dp', 'seq'))
- grad_w_gate: float32 [1024, 2048], P('dp', 'seq')
- grad_w_up: float32 [1024, 2048], P('dp', 'seq')
- grad_w_down: float32 [2048, 1024], P('dp', 'seq')
The draws below stay inside these ranges and needn't reach their ends.
Inputs may be any that keep to these rules, and one draw needn't show every extreme that they name: `segments`: each sequence holds three documents numbered 0, 1, 2 in order; the first and the last each have from 512 - max(64, 2) to 511 tokens.
All inputs are finite; a program needn't handle non-finite values.
Results may differ from the reference program's by a relative error of at most 0.02.
Values may be sent and summed in bfloat16 or wider, within the bound.
No kernel may reach another device: no remote copies, remote signals or barrier semaphores. Data moves between devices by JAX's collectives and lax.ppermute only.
A program may use at most 256 MiB of HBM per device.

```python
import jax
import jax.numpy as jnp
from jax import lax

D = 1024
FF = 2048
HEADS = 8
KV_HEADS = 2
HEAD_DIM = 64
SSM_HEADS = 24
SSM_DIM = 64
STATE = 128
CONV = 4
INNER = 1536
CHANNELS = 1792
PROJ = 3352
LENGTH = 1024
ROWS = 512
SEQS = 16
TOKENS = 16384


def draw_segments(key, part):
    key = jax.random.fold_in(key, 11)
    head_key, tail_key = jax.random.split(key)
    lowest = ROWS - max(ROWS // 8, 2)
    first_end = jax.random.randint(head_key, (SEQS, 1), lowest, ROWS)
    last_len = jax.random.randint(tail_key, (SEQS, 1), lowest, ROWS)
    index = jnp.arange(LENGTH, dtype=jnp.int32)[None, :]
    return (index >= first_end).astype(jnp.int32) + (index >= LENGTH - last_len).astype(jnp.int32)


def shard_levels(key, shape, shards, low, top_value):
    loudness, own = 1.0, jax.random.fold_in(key, 6)
    for axis_at, shards_of in shards:
        heights = jnp.exp(jax.random.uniform(jax.random.fold_in(own, axis_at), (shards_of,), jnp.float32, low / len(shards), top_value / len(shards)))
        loudness = loudness * jnp.repeat(heights, shape[axis_at] // shards_of).reshape([-1 if axis == axis_at else 1 for axis in range(len(shape))])
    return loudness


def scatter_about(own_key, shape, deviation, bound, cuts=(), kind=jnp.bfloat16):
    values = jax.random.normal(own_key, shape, jnp.float32) * deviation
    if len(cuts) > 0:
        values = shard_levels(own_key, shape, cuts, -0.22, 0.18) * values
    return jnp.clip(values, min=-bound, max=bound).astype(kind)


def setup_inputs(seed: int = 0) -> dict:
    splits = jax.random.split(jax.random.key(seed), 21)
    return {
        "tokens": scatter_about(splits[0], (TOKENS, D), 1.0, 6.0, ((0, 32),)),
        "segments": draw_segments(jax.random.fold_in(splits[20], 71), 0),
        "input_gain": jnp.clip(1.0 + 0.1 * jax.random.normal(splits[2], (D,), jnp.float32), 0.5, 1.5).astype(jnp.bfloat16),
        "mixer_in": scatter_about(splits[3], (D, PROJ), D ** -0.5, 0.1875, ((0, 16), (1, 2))),
        "conv_weight": scatter_about(splits[4], (CHANNELS, CONV), CONV ** -0.5, 3.0, ((0, 32),)),
        "conv_bias": scatter_about(splits[5], (CHANNELS,), 0.5, 3.0, ((0, 32),)),
        "step_bias": jnp.clip(jax.random.uniform(splits[6], (SSM_HEADS,), jnp.float32, -4.5, -2.5), -4.5, -2.5),
        "decay_log": jnp.clip(jax.random.uniform(splits[7], (SSM_HEADS,), jnp.float32, -4.0, 0.0), -4.0, 0.0),
        "skip_gain": jnp.clip(jax.random.uniform(splits[8], (SSM_HEADS,), jnp.float32, 0.5, 1.5), 0.5, 1.5),
        "mixer_gain": jnp.clip(1.0 + 0.1 * jax.random.normal(splits[9], (INNER,), jnp.float32), 0.5, 1.5).astype(jnp.bfloat16),
        "mixer_out": scatter_about(splits[10], (INNER, D), INNER ** -0.5, 0.15625, ((0, 16), (1, 2))),
        "w_query": scatter_about(splits[11], (D, HEADS * HEAD_DIM), D ** -0.5, 0.1875, ((0, 16), (1, 2))),
        "w_key": scatter_about(splits[12], (D, KV_HEADS * HEAD_DIM), D ** -0.5, 0.1875, ((0, 16), (1, 2))),
        "w_value": scatter_about(splits[13], (D, KV_HEADS * HEAD_DIM), D ** -0.5, 0.1875, ((0, 16), (1, 2))),
        "w_output": scatter_about(splits[14], (HEADS * HEAD_DIM, D), (HEADS * HEAD_DIM // 128) ** -0.5, 3.0, ((0, 16), (1, 2))),
        "hidden_gain": jnp.clip(1.0 + 0.1 * jax.random.normal(splits[15], (D,), jnp.float32), 0.5, 1.5).astype(jnp.bfloat16),
        "w_gate": scatter_about(splits[16], (D, FF), D ** -0.5, 0.1875, ((0, 16), (1, 2))),
        "w_up": scatter_about(splits[17], (D, FF), D ** -0.5, 0.1875, ((0, 16), (1, 2))),
        "w_down": scatter_about(splits[18], (FF, D), FF ** -0.5, 0.125, ((0, 16), (1, 2))),
        "cotangent": scatter_about(splits[19], (TOKENS, D), 1.0, 6.0, ((0, 32),)),
    }


EPS = 1e-05
THETA = 100000000000.0
HIGH = lax.Precision.HIGHEST

@jax.custom_vjp
def low(v):
    return lax.optimization_barrier(v.astype(jnp.bfloat16)).astype(jnp.float32)

@jax.custom_vjp
def low_back(v):
    return v

def low_keep(v):
    return (low(v), None)

def low_pass(kept, grad):
    return (grad,)

def back_keep(v):
    return (v, None)

def back_low(kept, grad):
    return (low(grad),)
low.defvjp(low_keep, low_pass)
low_back.defvjp(back_keep, back_low)

def matmul(left, right):
    return jnp.dot(left, right, precision=HIGH, preferred_element_type=jnp.float32)

def rms_scale(values, weight):
    return values * lax.rsqrt(lax.optimization_barrier(jnp.mean(values * values, axis=-1, keepdims=True)) + EPS) * weight

def rotate(values, places, sign):
    half = values.shape[-1] // 2
    freq = THETA ** (-jnp.arange(half, dtype=jnp.float32) / half)
    angle = places.astype(jnp.float32)[:, None] * freq[None, :]
    cosine = jnp.cos(angle)[:, None, :]
    sine = sign * jnp.sin(angle)[:, None, :]
    first = values[..., :half]
    second = values[..., half:]
    return jnp.concatenate([first * cosine - second * sine, second * cosine + first * sine], axis=-1)

def doc_places(seg_row):
    index = jnp.arange(seg_row.shape[0], dtype=jnp.int32)
    change = jnp.concatenate([jnp.ones((1,), bool), seg_row[1:] != seg_row[:-1]])
    starts = lax.cummax(jnp.where(change, index, 0), axis=0)
    return index - starts

def conv_mix(extended, weight, bias, seg_ext):
    count = extended.shape[0] - (CONV - 1)
    owner = seg_ext[CONV - 1:]
    total = jnp.zeros((count, extended.shape[1]), jnp.float32) + bias[None, :]
    for offset in range(CONV):
        window = extended[offset:offset + count]
        same = (seg_ext[offset:offset + count] == owner)[:, None]
        total = total + jnp.where(same, window * weight[None, :, offset], 0.0)
    return jax.nn.silu(total)

def decay_terms(step_raw, step_bias, decay_log):
    step_size = jax.nn.softplus(step_raw + step_bias[None, :])
    return (step_size, jnp.cumsum(-step_size * jnp.exp(decay_log)[None, :], axis=0))

def block_state(inner, state_in, step_raw, step_bias, decay_log, seg_rows, seg_prev):
    step_size, cumul = decay_terms(step_raw, step_bias, decay_log)
    last_seg = seg_rows[-1]
    tail = jnp.where((seg_rows == last_seg)[:, None], jnp.exp(cumul[-1][None, :] - cumul), 0.0) * step_size
    weighted = inner * tail[:, :, None]
    fresh_state = jnp.einsum('shp,sn->hpn', weighted, state_in, precision=HIGH)
    carried = jnp.where(last_seg == seg_prev, jnp.exp(cumul[-1]), 0.0)
    return (carried, fresh_state)

def block_mix(inner, state_in, state_out, step_raw, gate_z, step_bias, decay_log, skip_gain, mixer_gain, start_state, seg_rows, seg_prev):
    step_size, cumul = decay_terms(step_raw, step_bias, decay_log)
    count = seg_rows.shape[0]
    index = jnp.arange(count)
    allowed = (seg_rows[:, None] == seg_rows[None, :]) & (index[None, :] <= index[:, None])
    gap = cumul.T[:, :, None] - cumul.T[:, None, :]
    kernel = jnp.where(allowed[None], jnp.exp(jnp.where(allowed[None], gap, 0.0)), 0.0)
    intersection = jnp.dot(state_out, state_in.T, precision=HIGH)
    weights_mat = kernel * intersection[None] * step_size.T[:, None, :]
    local_part = jnp.einsum('hts,shp->thp', weights_mat, inner, precision=HIGH)
    entry = jnp.where((seg_rows == seg_prev)[:, None], jnp.exp(cumul), 0.0)
    incoming = jnp.einsum('tn,hpn->thp', state_out, start_state, precision=HIGH) * entry[:, :, None]
    mixed = local_part + incoming + skip_gain[None, :, None] * inner
    gated = mixed.reshape(count, -1) * jax.nn.silu(gate_z)
    return rms_scale(gated, mixer_gain)

def sequence_mixer(inner, state_in, state_out, step_raw, gate_z, seg_row, step_bias, decay_log, skip_gain, mixer_gain):
    blocks = LENGTH // ROWS
    earlier = jnp.concatenate([jnp.full((1,), -1, jnp.int32), seg_row[:-1]])
    pieces = (inner.reshape(blocks, ROWS, SSM_HEADS, SSM_DIM), state_in.reshape(blocks, ROWS, STATE), state_out.reshape(blocks, ROWS, STATE), step_raw.reshape(blocks, ROWS, SSM_HEADS), gate_z.reshape(blocks, ROWS, INNER), seg_row.reshape(blocks, ROWS), earlier[::ROWS])

    def advance(state_now, piece):
        inner_block, in_block, out_block, raw_block, gate_block, seg_block, prev_seg = piece
        normed = block_mix(inner_block, in_block, out_block, raw_block, gate_block, step_bias, decay_log, skip_gain, mixer_gain, state_now, seg_block, prev_seg)
        carried, fresh_state = block_state(inner_block, in_block, raw_block, step_bias, decay_log, seg_block, prev_seg)
        return (carried[:, None, None] * state_now + fresh_state, normed)
    initial = jnp.zeros((SSM_HEADS, SSM_DIM, STATE), jnp.float32)
    final_state, normed = lax.scan(jax.checkpoint(advance), initial, pieces)
    return normed.reshape(LENGTH, INNER)

def attention(query_rot, key_rot, value_proj, seg_row):
    group_size = HEADS // KV_HEADS
    grouped = query_rot.reshape(LENGTH, KV_HEADS, group_size, HEAD_DIM)
    index = jnp.arange(LENGTH)
    allowed = (seg_row[:, None] == seg_row[None, :]) & (index[None, :] <= index[:, None])
    scores = jnp.einsum('tkgd,skd->kgts', grouped, key_rot, precision=HIGH) * HEAD_DIM ** (-0.5)
    scores = low_back(jnp.where(allowed[None, None], scores, -1e+30))
    probs = low(jax.nn.softmax(scores, axis=-1))
    attended = jnp.einsum('kgts,skd->tkgd', probs, value_proj, precision=HIGH)
    return attended.reshape(LENGTH, HEADS * HEAD_DIM)

def layer(hidden_in, seg_row, weights):
    input_gain, mixer_in, conv_weight, conv_bias, step_bias, decay_log, skip_gain, mixer_gain, mixer_out, w_query, w_key, w_value, w_output, hidden_gain, w_gate, w_up, w_down = weights
    normed = low(rms_scale(hidden_in, input_gain))
    projected = low_back(matmul(normed, mixer_in))
    gate_z = projected[:, :INNER]
    conv_in = low(projected[:, INNER:INNER + CHANNELS])
    step_raw = projected[:, INNER + CHANNELS:]
    padded = jnp.concatenate([jnp.zeros((CONV - 1, CHANNELS), jnp.float32), conv_in])
    seg_pad = jnp.concatenate([jnp.full((CONV - 1,), -1, jnp.int32), seg_row])
    mixed_in = low(conv_mix(padded, conv_weight, conv_bias, seg_pad))
    inner = mixed_in[:, :INNER].reshape(LENGTH, SSM_HEADS, SSM_DIM)
    state_in = mixed_in[:, INNER:INNER + STATE]
    state_out = mixed_in[:, INNER + STATE:]
    mixed_norm = low(sequence_mixer(inner, state_in, state_out, step_raw, gate_z, seg_row, step_bias, decay_log, skip_gain, mixer_gain))
    mamba_part = low_back(matmul(mixed_norm, mixer_out))
    places = doc_places(seg_row)
    query = low_back(matmul(normed, w_query)).reshape(LENGTH, HEADS, HEAD_DIM)
    key_proj = low_back(matmul(normed, w_key)).reshape(LENGTH, KV_HEADS, HEAD_DIM)
    value_proj = low(low_back(matmul(normed, w_value))).reshape(LENGTH, KV_HEADS, HEAD_DIM)
    query_rot = low(rotate(query, places, 1.0))
    key_rot = low(rotate(key_proj, places, 1.0))
    attended = low(low_back(attention(query_rot, key_rot, value_proj, seg_row)))
    attn_part = low_back(matmul(attended, w_output))
    hidden_mid = hidden_in + attn_part + mamba_part
    normed_two = low(rms_scale(hidden_mid, hidden_gain))
    gate_part = low_back(matmul(normed_two, w_gate))
    up_part = low_back(matmul(normed_two, w_up))
    activated = low(jax.nn.silu(gate_part) * up_part)
    return hidden_mid + low_back(matmul(activated, w_down))

def reference(tokens, segments, input_gain, mixer_in, conv_weight, conv_bias, step_bias, decay_log, skip_gain, mixer_gain, mixer_out, w_query, w_key, w_value, w_output, hidden_gain, w_gate, w_up, w_down, cotangent):
    weights = (input_gain.astype(jnp.float32), mixer_in.astype(jnp.float32), conv_weight.astype(jnp.float32), conv_bias.astype(jnp.float32), step_bias.astype(jnp.float32), decay_log.astype(jnp.float32), skip_gain.astype(jnp.float32), mixer_gain.astype(jnp.float32), mixer_out.astype(jnp.float32), w_query.astype(jnp.float32), w_key.astype(jnp.float32), w_value.astype(jnp.float32), w_output.astype(jnp.float32), hidden_gain.astype(jnp.float32), w_gate.astype(jnp.float32), w_up.astype(jnp.float32), w_down.astype(jnp.float32))
    inputs = tokens.astype(jnp.float32).reshape(SEQS, LENGTH, D)
    checked = jax.checkpoint(layer)

    def forward(values, params):
        return lax.map(lambda pair: checked(pair[0], pair[1], params), (values, segments))
    outputs, pullback = jax.vjp(forward, inputs, weights)
    grad_in, grads = pullback(cotangent.astype(jnp.float32).reshape(SEQS, LENGTH, D))
    return (outputs.reshape(TOKENS, D).astype(jnp.bfloat16), grad_in.reshape(TOKENS, D), grads[0], grads[1], grads[2], grads[3], grads[4], grads[5], grads[6], grads[7], grads[8], grads[9], grads[10], grads[11], grads[12], grads[13], grads[14], grads[15], grads[16])
```

```python
import jax
import jax.numpy as jnp
from jax import lax
from jax.experimental import pallas as pl
from jax.experimental.pallas import tpu as pltpu
from jax.sharding import PartitionSpec as P

HEADS = 8
KV_HEADS = 2
HEAD_DIM = 64
SSM_HEADS = 24
SSM_DIM = 64
STATE = 128
CONV = 4
INNER = 1536
CHANNELS = 1792


EPS = 1e-05
THETA = 100000000000.0
HIGH = lax.Precision.HIGHEST


def entering(value, axis, combine, identity):
    length, index = (lax.axis_size(axis), lax.axis_index(axis))
    everything = jax.tree.map(
        lambda part, kind: lax.all_gather(part.astype(kind), axis),
        value,
        (jnp.bfloat16, jnp.bfloat16),
    )
    start = jax.tree.map(
        lambda part, zero: jnp.broadcast_to(jnp.asarray(zero, part.dtype), part.shape),
        value,
        identity,
    )

    def turn(k, before):
        reached = k < index
        new = combine(
            before, jax.tree.map(lambda part, own: part[k].astype(own.dtype), everything, value)
        )
        return jax.tree.map(lambda a, b: jnp.where(reached, a, b), new, before)

    return lax.fori_loop(0, length, turn, start)


def entering_2(value, axis, join, neutral):
    count = lax.axis_size(axis)
    place = lax.axis_index(axis)
    ahead = count - 1 - place
    gathered = jax.tree.map(
        lambda a, kind: lax.all_gather(a.astype(kind), axis),
        value,
        jax.tree.map(lambda a: jnp.bfloat16 if a.dtype == jnp.float32 else a.dtype, value),
    )
    state = jax.tree.map(lambda a, e: jnp.zeros_like(a) + jnp.asarray(e, a.dtype), value, neutral)

    def one(turn, state):
        source = count - 1 - turn
        return join(
            state,
            jax.tree.map(
                lambda a, own: lax.dynamic_index_in_dim(a, source, 0, False).astype(own.dtype),
                gathered,
                value,
            ),
        )

    return lax.fori_loop(0, ahead, one, state)


def rms_scale(values, weight):
    return values * lax.rsqrt(jnp.mean(values * values, axis=-1, keepdims=True) + EPS) * weight


def rotate(values, places, sign):
    half = values.shape[-1] // 2
    freq = THETA ** (-jnp.arange(half, dtype=jnp.float32) / half)
    angle = places.astype(jnp.float32)[:, None] * freq[None, :]
    cosine = jnp.cos(angle)[:, None, :]
    sine = sign * jnp.sin(angle)[:, None, :]
    first = values[..., :half]
    second = values[..., half:]
    return jnp.concatenate(
        [first * cosine - second * sine, second * cosine + first * sine], axis=-1
    )


def doc_places(seg_row):
    index = jnp.arange(seg_row.shape[0], dtype=jnp.int32)
    change = jnp.concatenate([jnp.ones((1,), bool), seg_row[1:] != seg_row[:-1]])
    starts = lax.cummax(jnp.where(change, index, 0), axis=0)
    return index - starts


def conv_mix(extended, weight, bias, seg_ext):
    count = extended.shape[0] - (CONV - 1)
    owner = seg_ext[CONV - 1 :]
    total = jnp.zeros((count, extended.shape[1]), jnp.float32) + bias[None, :]
    for offset in range(CONV):
        window = extended[offset : offset + count]
        same = (seg_ext[offset : offset + count] == owner)[:, None]
        total = total + jnp.where(same, window * weight[None, :, offset], 0.0)
    return jax.nn.silu(total)


def decay_terms(step_raw, step_bias, decay_log):
    step_size = jax.nn.softplus(step_raw + step_bias[None, :])
    return (step_size, jnp.cumsum(-step_size * jnp.exp(decay_log)[None, :], axis=0))


def block_state(inner, state_in, step_raw, step_bias, decay_log, seg_rows, seg_prev):
    step_size, cumul = decay_terms(step_raw, step_bias, decay_log)
    last_seg = seg_rows[-1]
    tail = (
        jnp.where((seg_rows == last_seg)[:, None], jnp.exp(cumul[-1][None, :] - cumul), 0.0)
        * step_size
    )
    weighted = inner * tail[:, :, None]
    fresh_state = jnp.einsum("shp,sn->hpn", weighted, state_in, precision=HIGH)
    carried = jnp.where(last_seg == seg_prev, jnp.exp(cumul[-1]), 0.0)
    return (carried, fresh_state)


def block_mix(
    inner,
    state_in,
    state_out,
    step_raw,
    gate_z,
    step_bias,
    decay_log,
    skip_gain,
    mixer_gain,
    start_state,
    seg_rows,
    seg_prev,
):
    step_size, cumul = decay_terms(step_raw, step_bias, decay_log)
    count = seg_rows.shape[0]
    index = jnp.arange(count)
    allowed = (seg_rows[:, None] == seg_rows[None, :]) & (index[None, :] <= index[:, None])
    gap = cumul.T[:, :, None] - cumul.T[:, None, :]
    kernel = jnp.where(allowed[None], jnp.exp(jnp.where(allowed[None], gap, 0.0)), 0.0)
    intersection = jnp.dot(state_out, state_in.T, precision=HIGH)
    weights_mat = kernel * intersection[None] * step_size.T[:, None, :]
    local_part = jnp.einsum("hts,shp->thp", weights_mat, inner, precision=HIGH)
    entry = jnp.where((seg_rows == seg_prev)[:, None], jnp.exp(cumul), 0.0)
    incoming = jnp.einsum("tn,hpn->thp", state_out, start_state, precision=HIGH) * entry[:, :, None]
    mixed = local_part + incoming + skip_gain[None, :, None] * inner
    gated = mixed.reshape(count, -1) * jax.nn.silu(gate_z)
    return rms_scale(gated, mixer_gain)


def dot_plain(left, right):
    return jnp.dot(left, right, preferred_element_type=jnp.float32)


def dot_right_t(left, right):
    return lax.dot_general(
        left, right, (((1,), (1,)), ((), ())), preferred_element_type=jnp.float32
    )


def dot_left_t(left, right):
    return lax.dot_general(
        left, right, (((0,), (0,)), ((), ())), preferred_element_type=jnp.float32
    )


def chain_forward(earlier, later):
    return (earlier[0] * later[0], later[0][:, None, None] * earlier[1] + later[1])


def chain_backward(earlier, later):
    return (earlier[0] * later[0], later[1] + later[0][:, None, None] * earlier[1])


def ffn_backward_grads(act_grad, gate_part, up_part, sigmoid_gate):
    up_grad_low = (act_grad * gate_part * sigmoid_gate).astype(jnp.bfloat16)
    gate_grad_low = (
        act_grad * up_part * sigmoid_gate * (1.0 + gate_part * (1.0 - sigmoid_gate))
    ).astype(jnp.bfloat16)
    return (gate_grad_low, up_grad_low)


def shards_general(
    tokens,
    segments,
    input_gain,
    mixer_in,
    conv_weight,
    conv_bias,
    step_bias,
    decay_log,
    skip_gain,
    mixer_gain,
    mixer_out,
    w_query,
    w_key,
    w_value,
    w_output,
    hidden_gain,
    w_gate,
    w_up,
    w_down,
    cotangent,
):
    sectioned = (
        lax.all_gather(input_gain, "seq", axis=0, tiled=True),
        lax.all_gather(mixer_in, "seq", axis=1, tiled=True),
        lax.all_gather(conv_weight, "seq", axis=0, tiled=True),
        lax.all_gather(conv_bias, "seq", axis=0, tiled=True),
        lax.all_gather(mixer_gain, "seq", axis=0, tiled=True),
        lax.all_gather(mixer_out, "seq", axis=1, tiled=True),
        lax.all_gather(w_query, "seq", axis=1, tiled=True),
        lax.all_gather(w_key, "seq", axis=1, tiled=True),
        lax.all_gather(w_value, "seq", axis=1, tiled=True),
        lax.all_gather(w_output, "seq", axis=1, tiled=True),
        lax.all_gather(hidden_gain, "seq", axis=0, tiled=True),
        lax.all_gather(w_gate, "seq", axis=1, tiled=True),
        lax.all_gather(w_up, "seq", axis=1, tiled=True),
        lax.all_gather(w_down, "seq", axis=1, tiled=True),
    )
    whole = (
        lax.all_gather(sectioned[0], "dp", axis=0, tiled=True),
        lax.all_gather(sectioned[1], "dp", axis=0, tiled=True),
        lax.all_gather(sectioned[2], "dp", axis=0, tiled=True),
        lax.all_gather(sectioned[3], "dp", axis=0, tiled=True),
        lax.all_gather(sectioned[4], "dp", axis=0, tiled=True),
        lax.all_gather(sectioned[5], "dp", axis=0, tiled=True),
        lax.all_gather(sectioned[6], "dp", axis=0, tiled=True),
        lax.all_gather(sectioned[7], "dp", axis=0, tiled=True),
        lax.all_gather(sectioned[8], "dp", axis=0, tiled=True),
        lax.all_gather(sectioned[9], "dp", axis=0, tiled=True),
        lax.all_gather(sectioned[10], "dp", axis=0, tiled=True),
        lax.all_gather(sectioned[11], "dp", axis=0, tiled=True),
        lax.all_gather(sectioned[12], "dp", axis=0, tiled=True),
        lax.all_gather(sectioned[13], "dp", axis=0, tiled=True),
    )
    (
        full_input_gain,
        full_mixer_in,
        full_conv_weight,
        full_conv_bias,
        full_mixer_gain,
        full_mixer_out,
        full_query,
        full_key,
        full_value,
        full_output,
        full_hidden_gain,
        full_gate,
        full_up,
        full_down,
    ) = whole
    row_count = tokens.shape[0]
    seg_all = segments[0]
    seq_length = seg_all.shape[0]
    seq_count = lax.axis_size("seq")
    seq_rank = lax.axis_index("seq")
    row_start = seq_rank * row_count
    places_all = doc_places(seg_all)
    seg_rows = lax.dynamic_slice_in_dim(seg_all, row_start, row_count)
    places = lax.dynamic_slice_in_dim(places_all, row_start, row_count)
    padded_seg = jnp.concatenate([jnp.full((CONV - 1,), -1, jnp.int32), seg_all])
    seg_ext = lax.dynamic_slice_in_dim(padded_seg, row_start, row_count + CONV - 1)
    seg_prev = seg_ext[CONV - 2]
    rim_start = jnp.maximum(seq_rank - 1, 0) * (CONV - 1)
    hidden_in = tokens.astype(jnp.float32)
    normed, norm_pull = jax.vjp(rms_scale, hidden_in, full_input_gain.astype(jnp.float32))
    normed_low = normed.astype(jnp.bfloat16)
    projected = dot_plain(normed_low, full_mixer_in)
    gate_z = projected[:, :INNER]
    conv_low = projected[:, INNER : INNER + CHANNELS].astype(jnp.bfloat16)
    step_raw = projected[:, INNER + CHANNELS :]
    group_size = HEADS // KV_HEADS
    score_scale = HEAD_DIM ** (-0.5)
    query = dot_plain(normed_low, full_query).reshape(row_count, HEADS, HEAD_DIM)
    key_proj = dot_plain(normed_low, full_key).reshape(row_count, KV_HEADS, HEAD_DIM)
    value_low = dot_plain(normed_low, full_value).astype(jnp.bfloat16)
    query_low = rotate(query, places, 1.0).astype(jnp.bfloat16)
    key_low = (
        rotate(key_proj, places, 1.0).astype(jnp.bfloat16).reshape(row_count, KV_HEADS * HEAD_DIM)
    )
    tail_low = conv_low[row_count - CONV + 1 :]
    keys_all, values_all, tails_all = (
        lax.all_gather(key_low, "seq", axis=0, tiled=True),
        lax.all_gather(value_low, "seq", axis=0, tiled=True),
        lax.all_gather(tail_low, "seq", axis=0, tiled=True),
    )
    rim_rows = jnp.where(
        seq_rank > 0,
        lax.dynamic_slice_in_dim(tails_all, rim_start, CONV - 1),
        jnp.zeros_like(tail_low),
    )
    extended = jnp.concatenate([rim_rows, conv_low]).astype(jnp.float32)

    def conv_piece(ext_rows, taps, shift_bias):
        return conv_mix(ext_rows, taps, shift_bias, seg_ext)

    conv_out, conv_pull = jax.vjp(
        conv_piece,
        extended,
        full_conv_weight.astype(jnp.float32),
        full_conv_bias.astype(jnp.float32),
    )
    mixed_in = conv_out.astype(jnp.bfloat16).astype(jnp.float32)
    inner = mixed_in[:, :INNER].reshape(row_count, SSM_HEADS, SSM_DIM)
    state_in = mixed_in[:, INNER : INNER + STATE]
    state_out = mixed_in[:, INNER + STATE :]

    def state_piece(inner_vals, in_vals, raw_vals, bias_vals, decay_vals):
        return block_state(inner_vals, in_vals, raw_vals, bias_vals, decay_vals, seg_rows, seg_prev)

    (carried, fresh_state), state_pull = jax.vjp(
        state_piece, inner, state_in, step_raw, step_bias, decay_log
    )
    start_state = entering(
        (carried, fresh_state),
        "seq",
        chain_forward,
        (jnp.ones_like(carried), jnp.zeros_like(fresh_state)),
    )[1]

    def mixer_piece(
        inner_vals,
        in_vals,
        out_vals,
        raw_vals,
        gate_vals,
        bias_vals,
        decay_vals,
        skip_vals,
        gain_vals,
        start_vals,
    ):
        return block_mix(
            inner_vals,
            in_vals,
            out_vals,
            raw_vals,
            gate_vals,
            bias_vals,
            decay_vals,
            skip_vals,
            gain_vals,
            start_vals,
            seg_rows,
            seg_prev,
        )

    mixed_norm, mixer_pull = jax.vjp(
        mixer_piece,
        inner,
        state_in,
        state_out,
        step_raw,
        gate_z,
        step_bias,
        decay_log,
        skip_gain,
        full_mixer_gain.astype(jnp.float32),
        start_state,
    )
    mixed_low = mixed_norm.astype(jnp.bfloat16)
    mamba_part = dot_plain(mixed_low, full_mixer_out)
    grouped = query_low.reshape(row_count, KV_HEADS, group_size, HEAD_DIM)
    keys_three = keys_all.reshape(seq_length, KV_HEADS, HEAD_DIM)
    values_three = values_all.reshape(seq_length, KV_HEADS, HEAD_DIM)
    query_index = row_start + jnp.arange(row_count)
    key_index = jnp.arange(seq_length)
    allowed = (seg_rows[:, None] == seg_all[None, :]) & (key_index[None, :] <= query_index[:, None])
    scores = (
        jnp.einsum("tkgd,skd->kgts", grouped, keys_three, preferred_element_type=jnp.float32)
        * score_scale
    )
    scores = jnp.where(allowed[None, None], scores, -1e30)
    log_total = jax.nn.logsumexp(scores, axis=-1, keepdims=True)
    probs = jnp.exp(scores - log_total)
    probs_low = probs.astype(jnp.bfloat16)
    attended = jnp.einsum(
        "kgts,skd->tkgd", probs_low, values_three, preferred_element_type=jnp.float32
    )
    attended_low = attended.reshape(row_count, HEADS * HEAD_DIM).astype(jnp.bfloat16)
    attn_part = dot_plain(attended_low, full_output)
    hidden_mid = hidden_in + attn_part + mamba_part
    normed_two, norm_two_pull = jax.vjp(rms_scale, hidden_mid, full_hidden_gain.astype(jnp.float32))
    normed_two_low = normed_two.astype(jnp.bfloat16)
    gate_part = dot_plain(normed_two_low, full_gate)
    up_part = dot_plain(normed_two_low, full_up)
    sigmoid_gate = jax.nn.sigmoid(gate_part)
    activated_low = (gate_part * sigmoid_gate * up_part).astype(jnp.bfloat16)
    output = (hidden_mid + dot_plain(activated_low, full_down)).astype(jnp.bfloat16)
    back_sectioned = (
        lax.all_gather(mixer_in, "seq", axis=1, tiled=True),
        lax.all_gather(mixer_out, "seq", axis=1, tiled=True),
        lax.all_gather(w_query, "seq", axis=1, tiled=True),
        lax.all_gather(w_key, "seq", axis=1, tiled=True),
        lax.all_gather(w_value, "seq", axis=1, tiled=True),
        lax.all_gather(w_output, "seq", axis=1, tiled=True),
        lax.all_gather(w_gate, "seq", axis=1, tiled=True),
        lax.all_gather(w_up, "seq", axis=1, tiled=True),
        lax.all_gather(w_down, "seq", axis=1, tiled=True),
    )
    back_whole = (
        lax.all_gather(back_sectioned[0], "dp", axis=0, tiled=True),
        lax.all_gather(back_sectioned[1], "dp", axis=0, tiled=True),
        lax.all_gather(back_sectioned[2], "dp", axis=0, tiled=True),
        lax.all_gather(back_sectioned[3], "dp", axis=0, tiled=True),
        lax.all_gather(back_sectioned[4], "dp", axis=0, tiled=True),
        lax.all_gather(back_sectioned[5], "dp", axis=0, tiled=True),
        lax.all_gather(back_sectioned[6], "dp", axis=0, tiled=True),
        lax.all_gather(back_sectioned[7], "dp", axis=0, tiled=True),
        lax.all_gather(back_sectioned[8], "dp", axis=0, tiled=True),
    )
    (
        back_mixer_in,
        back_mixer_out,
        back_query,
        back_key,
        back_value,
        back_output,
        back_gate,
        back_up,
        back_down,
    ) = back_whole
    act_grad = dot_right_t(cotangent, back_down)
    grad_down_part = dot_left_t(activated_low, cotangent)
    gate_grad_low, up_grad_low = ffn_backward_grads(act_grad, gate_part, up_part, sigmoid_gate)
    grad_gate_part = dot_left_t(normed_two_low, gate_grad_low)
    grad_up_part = dot_left_t(normed_two_low, up_grad_low)
    normed_two_grad = dot_right_t(gate_grad_low, back_gate) + dot_right_t(up_grad_low, back_up)
    hidden_part, hidden_gain_grad = norm_two_pull(normed_two_grad)
    hidden_grad = cotangent.astype(jnp.float32) + hidden_part
    branch_low = hidden_grad.astype(jnp.bfloat16)
    grad_mixer_out_full = dot_left_t(mixed_low, branch_low)
    norm_grad = dot_right_t(branch_low, back_mixer_out)
    (
        inner_grad_mix,
        in_grad_mix,
        out_grad,
        raw_grad_mix,
        gate_z_grad,
        bias_grad_mix,
        decay_grad_mix,
        skip_grad,
        mixer_gain_grad,
        start_grad,
    ) = mixer_pull(norm_grad)
    later_grad = entering_2(
        (carried, start_grad),
        "seq",
        chain_backward,
        (jnp.ones_like(carried), jnp.zeros_like(start_grad)),
    )[1]
    carried_grad = jnp.sum(later_grad * start_state, axis=(1, 2))
    inner_grad_st, in_grad_st, raw_grad_st, bias_grad_st, decay_grad_st = state_pull(
        (carried_grad, later_grad)
    )
    mixed_grad = jnp.concatenate(
        [
            (inner_grad_mix + inner_grad_st).reshape(row_count, INNER),
            in_grad_mix + in_grad_st,
            out_grad,
        ],
        axis=1,
    )
    ext_grad, conv_weight_grad, conv_bias_grad = conv_pull(mixed_grad)
    rim_send = jnp.where(seq_rank > 0, ext_grad[: CONV - 1], 0.0)
    rim_terms = lax.dynamic_update_slice_in_dim(
        jnp.zeros((seq_count * (CONV - 1), CHANNELS), jnp.float32), rim_send, rim_start, 0
    )
    grad_output_full = dot_left_t(attended_low, branch_low)
    attended_grad = (
        dot_right_t(branch_low, back_output)
        .astype(jnp.bfloat16)
        .reshape(row_count, KV_HEADS, group_size, HEAD_DIM)
    )
    prob_grad = jnp.einsum(
        "tkgd,skd->kgts", attended_grad, values_three, preferred_element_type=jnp.float32
    )
    inner_total = jnp.sum(probs * prob_grad, axis=-1, keepdims=True)
    score_grad = (probs * (prob_grad - inner_total)).astype(jnp.bfloat16)
    query_rot_grad = (
        jnp.einsum("kgts,skd->tkgd", score_grad, keys_three, preferred_element_type=jnp.float32)
        * score_scale
    )
    key_grad_all = (
        jnp.einsum("kgts,tkgd->skd", score_grad, grouped, preferred_element_type=jnp.float32)
        * score_scale
    )
    value_grad_all = jnp.einsum(
        "kgts,tkgd->skd", probs_low, attended_grad, preferred_element_type=jnp.float32
    )
    key_rot_grad, value_grad, rim_grad = (
        lax.psum_scatter(
            key_grad_all.reshape(seq_length, KV_HEADS * HEAD_DIM).astype(jnp.bfloat16),
            "seq",
            scatter_dimension=0,
            tiled=True,
        ).astype(jnp.float32),
        lax.psum_scatter(
            value_grad_all.reshape(seq_length, KV_HEADS * HEAD_DIM).astype(jnp.bfloat16),
            "seq",
            scatter_dimension=0,
            tiled=True,
        ).astype(jnp.float32),
        lax.psum_scatter(
            rim_terms.astype(jnp.bfloat16), "seq", scatter_dimension=0, tiled=True
        ).astype(jnp.float32),
    )
    conv_grad = ext_grad[CONV - 1 :] + jnp.concatenate(
        [jnp.zeros((row_count - CONV + 1, CHANNELS), jnp.float32), rim_grad]
    )
    proj_grad_low = jnp.concatenate(
        [gate_z_grad, conv_grad, raw_grad_mix + raw_grad_st], axis=1
    ).astype(jnp.bfloat16)
    grad_mixer_in_full = dot_left_t(normed_low, proj_grad_low)
    normed_grad = dot_right_t(proj_grad_low, back_mixer_in)
    query_grad_low = (
        rotate(query_rot_grad.reshape(row_count, HEADS, HEAD_DIM), places, -1.0)
        .reshape(row_count, HEADS * HEAD_DIM)
        .astype(jnp.bfloat16)
    )
    key_grad_low = (
        rotate(key_rot_grad.reshape(row_count, KV_HEADS, HEAD_DIM), places, -1.0)
        .reshape(row_count, KV_HEADS * HEAD_DIM)
        .astype(jnp.bfloat16)
    )
    value_grad_low = value_grad.astype(jnp.bfloat16)
    grad_query_full = dot_left_t(normed_low, query_grad_low)
    grad_key_full = dot_left_t(normed_low, key_grad_low)
    grad_value_full = dot_left_t(normed_low, value_grad_low)
    normed_grad = (
        normed_grad
        + dot_right_t(query_grad_low, back_query)
        + dot_right_t(key_grad_low, back_key)
        + dot_right_t(value_grad_low, back_value)
    )
    input_part, input_gain_grad = norm_pull(normed_grad)
    token_grad = hidden_grad + input_part
    reduced = (
        lax.psum_scatter(
            input_gain_grad.astype(jnp.bfloat16), "dp", scatter_dimension=0, tiled=True
        ).astype(jnp.float32),
        lax.psum_scatter(
            grad_mixer_in_full.astype(jnp.bfloat16), "dp", scatter_dimension=0, tiled=True
        ).astype(jnp.float32),
        lax.psum_scatter(
            conv_weight_grad.astype(jnp.bfloat16), "dp", scatter_dimension=0, tiled=True
        ).astype(jnp.float32),
        lax.psum_scatter(
            conv_bias_grad.astype(jnp.bfloat16), "dp", scatter_dimension=0, tiled=True
        ).astype(jnp.float32),
        lax.psum_scatter(
            mixer_gain_grad.astype(jnp.bfloat16), "dp", scatter_dimension=0, tiled=True
        ).astype(jnp.float32),
        lax.psum_scatter(
            grad_mixer_out_full.astype(jnp.bfloat16), "dp", scatter_dimension=0, tiled=True
        ).astype(jnp.float32),
        lax.psum_scatter(
            grad_query_full.astype(jnp.bfloat16), "dp", scatter_dimension=0, tiled=True
        ).astype(jnp.float32),
        lax.psum_scatter(
            grad_key_full.astype(jnp.bfloat16), "dp", scatter_dimension=0, tiled=True
        ).astype(jnp.float32),
        lax.psum_scatter(
            grad_value_full.astype(jnp.bfloat16), "dp", scatter_dimension=0, tiled=True
        ).astype(jnp.float32),
        lax.psum_scatter(
            grad_output_full.astype(jnp.bfloat16), "dp", scatter_dimension=0, tiled=True
        ).astype(jnp.float32),
        lax.psum_scatter(
            hidden_gain_grad.astype(jnp.bfloat16), "dp", scatter_dimension=0, tiled=True
        ).astype(jnp.float32),
        lax.psum_scatter(
            grad_gate_part.astype(jnp.bfloat16), "dp", scatter_dimension=0, tiled=True
        ).astype(jnp.float32),
        lax.psum_scatter(
            grad_up_part.astype(jnp.bfloat16), "dp", scatter_dimension=0, tiled=True
        ).astype(jnp.float32),
        lax.psum_scatter(
            grad_down_part.astype(jnp.bfloat16), "dp", scatter_dimension=0, tiled=True
        ).astype(jnp.float32),
    )
    shares = (
        lax.psum_scatter(
            reduced[0].astype(jnp.bfloat16), "seq", scatter_dimension=0, tiled=True
        ).astype(jnp.float32),
        lax.psum_scatter(
            reduced[1].astype(jnp.bfloat16), "seq", scatter_dimension=1, tiled=True
        ).astype(jnp.float32),
        lax.psum_scatter(
            reduced[2].astype(jnp.bfloat16), "seq", scatter_dimension=0, tiled=True
        ).astype(jnp.float32),
        lax.psum_scatter(
            reduced[3].astype(jnp.bfloat16), "seq", scatter_dimension=0, tiled=True
        ).astype(jnp.float32),
        lax.psum_scatter(
            reduced[4].astype(jnp.bfloat16), "seq", scatter_dimension=0, tiled=True
        ).astype(jnp.float32),
        lax.psum_scatter(
            reduced[5].astype(jnp.bfloat16), "seq", scatter_dimension=1, tiled=True
        ).astype(jnp.float32),
        lax.psum_scatter(
            reduced[6].astype(jnp.bfloat16), "seq", scatter_dimension=1, tiled=True
        ).astype(jnp.float32),
        lax.psum_scatter(
            reduced[7].astype(jnp.bfloat16), "seq", scatter_dimension=1, tiled=True
        ).astype(jnp.float32),
        lax.psum_scatter(
            reduced[8].astype(jnp.bfloat16), "seq", scatter_dimension=1, tiled=True
        ).astype(jnp.float32),
        lax.psum_scatter(
            reduced[9].astype(jnp.bfloat16), "seq", scatter_dimension=1, tiled=True
        ).astype(jnp.float32),
        lax.psum_scatter(
            reduced[10].astype(jnp.bfloat16), "seq", scatter_dimension=0, tiled=True
        ).astype(jnp.float32),
        lax.psum_scatter(
            reduced[11].astype(jnp.bfloat16), "seq", scatter_dimension=1, tiled=True
        ).astype(jnp.float32),
        lax.psum_scatter(
            reduced[12].astype(jnp.bfloat16), "seq", scatter_dimension=1, tiled=True
        ).astype(jnp.float32),
        lax.psum_scatter(
            reduced[13].astype(jnp.bfloat16), "seq", scatter_dimension=1, tiled=True
        ).astype(jnp.float32),
    )
    bias_total, decay_total, skip_total = lax.psum(
        (bias_grad_mix + bias_grad_st, decay_grad_mix + decay_grad_st, skip_grad), ("dp", "seq")
    )
    return (
        output,
        token_grad,
        shares[0],
        shares[1],
        shares[2],
        shares[3],
        bias_total,
        decay_total,
        skip_total,
        shares[4],
        shares[5],
        shares[6],
        shares[7],
        shares[8],
        shares[9],
        shares[10],
        shares[11],
        shares[12],
        shares[13],
    )


def ring(value, axis, stride, size):
    count = lax.axis_size(axis)
    pairs = []
    for place in range(count):
        own = place // stride % size
        pairs.append((place, place + ((own + 1) % size - own) * stride))
    return lax.ppermute(value, axis, pairs)


def own_place(axis, stride, size):
    return lax.axis_index(axis) // stride % size


def in_order(parts, own, dim):
    size = len(parts)
    if size == 2:
        return jnp.where(
            own == 0,
            jnp.concatenate(parts, axis=dim),
            jnp.concatenate(parts[::-1], axis=dim),
        )
    ahead = [parts[-k % size] for k in range(size)] * 2
    width = parts[0].shape[dim]
    return lax.dynamic_slice_in_dim(
        jnp.concatenate(ahead, axis=dim), (size - own) % size * width, size * width, dim
    )


def gather_stage(value, axis, stride, size, dim):
    parts = [value]
    for _ in range(size - 1):
        parts.append(ring(parts[-1], axis, stride, size))
    return in_order(parts, own_place(axis, stride, size), dim)


def dp_factors():
    count = lax.axis_size("dp")
    core = 2
    row = 4 if count > 16 else 2
    return core, row, count // (core * row)


def gather_weight(piece, seq_last):
    core, row, far = dp_factors()
    rows, columns = piece.shape
    value = piece.reshape(1, 1, 1, rows, columns)
    value = gather_stage(value, "dp", core * row, far, 0)
    if seq_last:
        value = gather_stage(value, "dp", core, row, 1)
        value = gather_stage(value, "seq", 1, lax.axis_size("seq"), 4)
    else:
        value = gather_stage(value, "seq", 1, lax.axis_size("seq"), 4)
        value = gather_stage(value, "dp", core, row, 1)
    value = gather_stage(value, "dp", 1, core, 2)
    return value.reshape(far * row * core, rows, value.shape[-1])


def pick(value, index, size, dim):
    width = value.shape[dim] // size
    if size == 2:
        return jnp.where(
            index == 0,
            lax.slice_in_dim(value, 0, width, axis=dim),
            lax.slice_in_dim(value, width, 2 * width, axis=dim),
        )
    return lax.dynamic_slice_in_dim(value, index * width, width, dim)


def scatter_stage(value, axis, stride, size, dim):
    own = own_place(axis, stride, size)
    moving = pick(value, (own + size - 1) % size, size, dim).astype(jnp.bfloat16)
    for step in range(2, size + 1):
        moving = ring(moving, axis, stride, size)
        mine = pick(value, (own + size - step) % size, size, dim)
        total = mine.astype(jnp.float32) + moving.astype(jnp.float32)
        moving = total.astype(jnp.bfloat16)
    return total


def scatter_weight(grad, seq_first):
    core, row, far = dp_factors()
    rows = grad.shape[0] // (core * row * far)
    value = grad.reshape(far, row, core, rows, grad.shape[1])
    value = scatter_stage(value, "dp", 1, core, 2).astype(jnp.bfloat16)
    if seq_first:
        value = scatter_stage(value, "seq", 1, lax.axis_size("seq"), 4).astype(jnp.bfloat16)
        value = scatter_stage(value, "dp", core, row, 1).astype(jnp.bfloat16)
    else:
        value = scatter_stage(value, "dp", core, row, 1).astype(jnp.bfloat16)
        value = scatter_stage(value, "seq", 1, lax.axis_size("seq"), 4).astype(jnp.bfloat16)
    value = scatter_stage(value, "dp", core * row, far, 0)
    return value.reshape(rows, value.shape[-1])


def scatter_small(parts):
    core, row, far = dp_factors()
    seq = lax.axis_size("seq")
    value = parts.reshape(far, row, core, seq, parts.shape[-1])
    for axis, stride, size, dim in (
        ("dp", 1, core, 2),
        ("seq", 1, seq, 3),
        ("dp", core, row, 1),
        ("dp", core * row, far, 0),
    ):
        own = own_place(axis, stride, size)
        moving = pick(value, (own + size - 1) % size, size, dim)
        for step in range(2, size + 1):
            moving = ring(moving, axis, stride, size) + pick(
                value, (own + size - step) % size, size, dim
            )
        value = moving
    return value.reshape(-1)


CHUNK = 64
PAIR = 128


def dot_high(left, right):
    return jnp.dot(left, right, precision=HIGH, preferred_element_type=jnp.float32)


def first_lanes(rows):
    return lax.broadcasted_iota(jnp.int32, (rows, PAIR), 1) < PAIR // 2


def turn(value, cosine, sine):
    half = HEAD_DIM // 2
    lane = lax.broadcasted_iota(jnp.int32, value.shape, 1)
    other = jnp.where(
        lane % HEAD_DIM < half,
        pltpu.roll(value, PAIR - half, 1),
        pltpu.roll(value, half, 1),
    )
    return value * cosine + other * sine


def twice(value):
    rolled = pltpu.roll(value, PAIR // 2, 1)
    low_half = first_lanes(value.shape[0])
    return jnp.where(low_half, value, rolled), jnp.where(low_half, rolled, value)


def stacked(pairs):
    low_half = first_lanes(pairs[0].shape[0])
    parts = []
    for pair in pairs:
        parts.append(jnp.where(low_half, pair, 0.0))
        parts.append(jnp.where(low_half, 0.0, pair))
    return jnp.concatenate(parts, axis=0).astype(jnp.bfloat16)


def softmax_block(queries, keys, seg_col, seg_row, first_row):
    rows, wide = seg_col.shape[0], keys.shape[0]
    scores = dot_right_t(queries, keys) * HEAD_DIM ** (-0.5)
    query_at = lax.broadcasted_iota(jnp.int32, (rows, wide), 0) + first_row
    key_at = lax.broadcasted_iota(jnp.int32, (rows, wide), 1)
    allowed = (seg_col == seg_row[:, :wide]) & (key_at <= query_at)
    offset = jnp.where(allowed, 0.0, -1e30)
    scores = scores + jnp.concatenate([offset] * (queries.shape[0] // rows), axis=0)
    scores = jnp.exp(scores - jnp.max(scores, axis=1, keepdims=True))
    return scores / jnp.sum(scores, axis=1, keepdims=True)


def attention_forward(part_ref, cos_ref, sin_ref, seg_col_ref, seg_row_ref, turned_ref, out_ref):
    count, row_count = part_ref.shape[0], out_ref.shape[0]
    halo = count - row_count
    block = min(row_count, 128)
    cosine, sine = cos_ref[...], sin_ref[...]
    seg_row = seg_row_ref[...]
    group = HEADS // KV_HEADS * HEAD_DIM
    for kv_head in range(KV_HEADS):
        base = kv_head * (group + 2 * HEAD_DIM)
        for at in range(base, base + group, PAIR):
            turned_ref[:, at : at + PAIR] = turn(part_ref[:, at : at + PAIR], cosine, sine).astype(
                jnp.bfloat16
            )
        at = base + group
        both = part_ref[:, at : at + PAIR]
        both = jnp.where(first_lanes(count), turn(both, cosine, sine), both).astype(jnp.bfloat16)
        turned_ref[:, at : at + PAIR] = both
        keys, values = twice(both.astype(jnp.float32))
        keys, values = keys.astype(jnp.bfloat16), values.astype(jnp.bfloat16)
        for start in range(0, row_count, block):
            first = halo + start
            queries = stacked(
                [
                    turned_ref[first : first + block, at : at + PAIR].astype(jnp.float32)
                    for at in range(base, base + group, PAIR)
                ]
            )
            wide = first + block
            probs = softmax_block(
                queries, keys[:wide], seg_col_ref[first : first + block], seg_row, first
            ).astype(jnp.bfloat16)
            result = dot_plain(probs, values[:wide])
            low_half = first_lanes(block)
            for k in range(group // PAIR):
                pair = jnp.where(
                    low_half,
                    result[2 * k * block : (2 * k + 1) * block],
                    result[(2 * k + 1) * block : (2 * k + 2) * block],
                )
                at = kv_head * group + k * PAIR
                out_ref[start : start + block, at : at + PAIR] = pair.astype(jnp.bfloat16)


def attention_backward(
    turned_ref, grad_ref, cos_ref, sin_ref, seg_col_ref, seg_row_ref, out_ref, key_ref, value_ref
):
    count, row_count = turned_ref.shape[0], grad_ref.shape[0]
    halo = count - row_count
    block = min(row_count, 128)
    cosine, sine = cos_ref[...], sin_ref[...]
    seg_row = seg_row_ref[...]
    group = HEADS // KV_HEADS * HEAD_DIM
    scale = HEAD_DIM ** (-0.5)
    for kv_head in range(KV_HEADS):
        base = kv_head * (group + 2 * HEAD_DIM)
        at = base + group
        keys, values = twice(turned_ref[:, at : at + PAIR].astype(jnp.float32))
        keys, values = keys.astype(jnp.bfloat16), values.astype(jnp.bfloat16)
        key_ref[...] = jnp.zeros_like(key_ref)
        value_ref[...] = jnp.zeros_like(value_ref)
        for start in range(0, row_count, block):
            first = halo + start
            queries = stacked(
                [
                    turned_ref[first : first + block, at : at + PAIR].astype(jnp.float32)
                    for at in range(base, base + group, PAIR)
                ]
            )
            grads = stacked(
                [
                    grad_ref[
                        start : start + block, kv_head * group + at : kv_head * group + at + PAIR
                    ].astype(jnp.float32)
                    for at in range(0, group, PAIR)
                ]
            )
            wide = first + block
            probs = softmax_block(
                queries, keys[:wide], seg_col_ref[first : first + block], seg_row, first
            )
            prob_grad = dot_right_t(grads, values[:wide])
            mean = jnp.sum(probs * prob_grad, axis=1, keepdims=True)
            score_grad = (probs * (prob_grad - mean)).astype(jnp.bfloat16)
            result = dot_plain(score_grad, keys[:wide]) * scale
            key_ref[:wide] += dot_left_t(score_grad, queries)
            value_ref[:wide] += dot_left_t(probs.astype(jnp.bfloat16), grads)
            low_half = first_lanes(block)
            for k in range(group // PAIR):
                pair = jnp.where(
                    low_half,
                    result[2 * k * block : (2 * k + 1) * block],
                    result[(2 * k + 1) * block : (2 * k + 2) * block],
                )
                pair = turn(
                    pair, cosine[first : first + block], -sine[first : first + block]
                )
                out_ref[first : first + block, base + k * PAIR : base + (k + 1) * PAIR] = (
                    pair.astype(jnp.bfloat16)
                )
        key_grad, value_grad = key_ref[...], value_ref[...]
        key_grad = (key_grad + pltpu.roll(key_grad, PAIR // 2, 1)) * scale
        value_grad = value_grad + pltpu.roll(value_grad, PAIR // 2, 1)
        both = jnp.where(first_lanes(count), turn(key_grad, cosine, -sine), value_grad)
        out_ref[:, at : at + PAIR] = both.astype(jnp.bfloat16)
        out_ref[:halo, base : base + group] = jnp.zeros((halo, group), jnp.bfloat16)


def load_conv(proj_ref, conv_ref):
    count = proj_ref.shape[0]
    conv_ref[:8] = jnp.zeros((8, CHANNELS), jnp.float32)
    conv_ref[8 : count + 8] = (
        proj_ref[:, INNER : INNER + CHANNELS].astype(jnp.bfloat16).astype(jnp.float32)
    )


def conv_chunk(conv_ref, seg_ref, taps_ref, base):
    rows = conv_ref[pl.ds(base, CHUNK + 8), :]
    segs = seg_ref[pl.ds(base, CHUNK + 8), :]
    own = segs[8:]
    total = jnp.broadcast_to(taps_ref[CONV : CONV + 1, :], (CHUNK, CHANNELS))
    for offset in range(CONV):
        at = 8 - (CONV - 1) + offset
        same = segs[at : at + CHUNK] == own
        total = total + jnp.where(same, rows[at : at + CHUNK] * taps_ref[offset : offset + 1], 0.0)
    return total, segs


def steps_of(proj_ref, heads_ref, base):
    raw = proj_ref[pl.ds(base, CHUNK), INNER + CHANNELS :] + heads_ref[0:1, :SSM_HEADS]
    step = jnp.maximum(raw, 0.0) + jnp.log1p(jnp.exp(-jnp.abs(raw)))
    rate = -step * heads_ref[1:2, :SSM_HEADS]
    early = lax.broadcasted_iota(jnp.int32, (CHUNK, CHUNK), 0)
    late = lax.broadcasted_iota(jnp.int32, (CHUNK, CHUNK), 1)
    total = dot_high((late <= early).astype(jnp.float32), rate)
    source = lax.broadcasted_iota(jnp.int32, (CHUNK, PAIR), 0)
    target = lax.broadcasted_iota(jnp.int32, (CHUNK, PAIR), 1) % CHUNK
    across = lax.dot_general(
        rate,
        (source <= target).astype(jnp.float32),
        (((0,), (0,)), ((), ())),
        precision=HIGH,
        preferred_element_type=jnp.float32,
    )
    return raw, step, rate, total, across


def chunk_masks(segs, seg_row):
    own, before, last = segs[8:], segs[7:8], segs[CHUNK + 7 :]
    at = lax.broadcasted_iota(jnp.int32, (CHUNK, PAIR), 0)
    source = lax.broadcasted_iota(jnp.int32, (CHUNK, PAIR), 1) % CHUNK
    allowed = (own == seg_row) & (source <= at)
    entry = (own == before).astype(jnp.float32)
    tail = (own == last).astype(jnp.float32)
    carry = (last == before).astype(jnp.float32)
    return allowed, entry, tail, carry


def per_pair(columns, k, low_half):
    return jnp.where(low_half, columns[:, 2 * k : 2 * k + 1], columns[:, 2 * k + 1 : 2 * k + 2])


def row_pair(rows, k, low_half):
    return jnp.where(
        low_half[:1], rows[2 * k : 2 * k + 1], rows[2 * k + 1 : 2 * k + 2]
    )


def diagonal(value, low_half):
    zero = jnp.zeros_like(value)
    return jnp.concatenate([jnp.where(low_half, value, zero), jnp.where(low_half, zero, value)])


def mixer_forward(
    proj_ref, taps_ref, heads_ref, wide_ref, seg_ref, seg_row_ref,
    out_ref, mix_ref, states_ref, conv_ref, state_ref, gated_ref,
):
    count, row_count = proj_ref.shape[0], out_ref.shape[0]
    low = jnp.bfloat16
    load_conv(proj_ref, conv_ref)
    state_ref[...] = jnp.zeros_like(state_ref)
    low_half = first_lanes(CHUNK)

    def body(c, _):
        base = pl.multiple_of(c * CHUNK, CHUNK)
        store = pl.multiple_of(jnp.maximum(c - 1, 0) * CHUNK, CHUNK)
        total, segs = conv_chunk(conv_ref, seg_ref, taps_ref, base)
        mixed = (total * jax.nn.sigmoid(total)).astype(low)
        inner = mixed[:, :INNER].astype(jnp.float32)
        state_in, state_out = mixed[:, INNER : INNER + STATE], mixed[:, INNER + STATE :]
        _, step, _, cumul, across = steps_of(proj_ref, heads_ref, base)
        allowed, entry, tail, carry = chunk_masks(segs, seg_row_ref[pl.ds(c, 1), :])
        shared = dot_right_t(state_out, jnp.concatenate([state_in, state_in]))
        shared = jnp.where(allowed, shared, 0.0)
        state = state_ref[...]
        state_low = state.astype(low)
        states_ref[pl.ds(c, 1)] = state_low[None]
        incoming = dot_plain(state_out, state_low)
        squares = jnp.zeros((CHUNK, PAIR), jnp.float32)
        fresh, kept = [], []
        for k in range(SSM_HEADS // 2):
            lanes = slice(k * PAIR, (k + 1) * PAIR)
            sums = per_pair(cumul, k, low_half)
            decay = jnp.exp(jnp.minimum(sums - row_pair(across, k, low_half), 0.0))
            weights = (decay * shared).astype(low)
            value = inner[:, lanes]
            stepped = value * per_pair(step, k, low_half)
            local = dot_plain(weights, diagonal(stepped.astype(low), low_half))
            end = sums[CHUNK - 1 :]
            mix = (
                local
                + incoming[:, lanes] * (jnp.exp(sums) * entry)
                + wide_ref[0:1, lanes] * value
            )
            fresh.append((stepped * (jnp.exp(end - sums) * tail)).astype(low))
            kept.append(jnp.exp(end) * carry)
            gate = proj_ref[pl.ds(base, CHUNK), lanes]
            gated = mix * gate * jax.nn.sigmoid(gate)
            mix_ref[pl.ds(store, CHUNK), lanes] = mix
            gated_ref[:, lanes] = gated
            squares = squares + gated * gated
        state_ref[...] = state * jnp.concatenate(kept, axis=1) + dot_left_t(
            state_in, jnp.concatenate(fresh, axis=1)
        )
        norm = lax.rsqrt(jnp.sum(squares, axis=1, keepdims=True) / INNER + EPS)
        out_ref[pl.ds(store, CHUNK), :] = (gated_ref[...] * norm * wide_ref[1:2, :]).astype(low)
        return 0

    lax.fori_loop(0, count // CHUNK, body, 0)


def mixer_backward(
    proj_ref, mix_ref, states_ref, grad_ref, taps_ref, heads_ref, wide_ref, seg_ref, seg_row_ref,
    out_ref, taps_out_ref, wide_out_ref, heads_out_ref,
    conv_ref, pre_ref, adjoint_ref, mixgrad_ref, innergrad_ref,
):
    count, row_count = proj_ref.shape[0], mix_ref.shape[0]
    low = jnp.bfloat16
    load_conv(proj_ref, conv_ref)
    adjoint_ref[...] = jnp.zeros_like(adjoint_ref)
    pre_ref[...] = jnp.zeros_like(pre_ref)
    taps_out_ref[...] = jnp.zeros_like(taps_out_ref)
    wide_out_ref[...] = jnp.zeros_like(wide_out_ref)
    heads_out_ref[...] = jnp.zeros_like(heads_out_ref)
    low_half = first_lanes(CHUNK)
    chunks = count // CHUNK

    def body(turn_at, _):
        c = chunks - 1 - turn_at
        base = pl.multiple_of(c * CHUNK, CHUNK)
        store = pl.multiple_of(jnp.maximum(c - 1, 0) * CHUNK, CHUNK)
        real = (c > 0).astype(jnp.float32)

        gate = proj_ref[pl.ds(base, CHUNK), :INNER]
        mix = mix_ref[pl.ds(store, CHUNK), :]
        norm_grad = grad_ref[pl.ds(store, CHUNK), :].astype(jnp.float32) * real
        sig = jax.nn.sigmoid(gate)
        silu = gate * sig
        gated = mix * silu
        norm = lax.rsqrt(jnp.mean(gated * gated, axis=1, keepdims=True) + EPS)
        scaled = norm_grad * wide_ref[1:2, :]
        wide_out_ref[1:2, :] += jnp.sum(norm_grad * gated * norm, axis=0, keepdims=True)
        pull = jnp.mean(gated * scaled, axis=1, keepdims=True) * (norm * norm * norm)
        gated_grad = norm * scaled - gated * pull
        mix_grad = gated_grad * silu
        mixgrad_ref[...] = mix_grad
        out_ref[pl.ds(base, CHUNK), :INNER] = (
            gated_grad * mix * (sig * (1.0 + gate * (1.0 - sig)))
        ).astype(low)

        total, segs = conv_chunk(conv_ref, seg_ref, taps_ref, base)
        sig = jax.nn.sigmoid(total)
        mixed = (total * sig).astype(low)
        slope = sig * (1.0 + total * (1.0 - sig))
        inner = mixed[:, :INNER].astype(jnp.float32)
        state_in, state_out = mixed[:, INNER : INNER + STATE], mixed[:, INNER + STATE :]
        wide_out_ref[0:1, :] += jnp.sum(mix_grad * inner, axis=0, keepdims=True)
        raw, step, rate, cumul, across = steps_of(proj_ref, heads_ref, base)
        allowed, entry, tail, carry = chunk_masks(segs, seg_row_ref[pl.ds(c, 1), :])
        twice_in = jnp.concatenate([state_in, state_in])
        shared = jnp.where(allowed, dot_right_t(state_out, twice_in), 0.0)
        state = states_ref[pl.ds(c, 1)][0]
        adjoint = adjoint_ref[...]
        adjoint_low = adjoint.astype(low)
        incoming = dot_plain(state_out, state)
        reached = dot_plain(state_in, adjoint_low)
        products = jnp.sum(adjoint * state.astype(jnp.float32), axis=0, keepdims=True)
        head_lane = lax.broadcasted_iota(jnp.int32, (CHUNK, SSM_HEADS), 1)
        head_row = lax.broadcasted_iota(jnp.int32, (SSM_HEADS, PAIR), 0)
        head_low = lax.broadcasted_iota(jnp.int32, (SSM_HEADS, PAIR), 1) < CHUNK
        last_row = lax.broadcasted_iota(jnp.int32, (CHUNK, PAIR), 0) == CHUNK - 1
        sum_grad = jnp.zeros((CHUNK, SSM_HEADS), jnp.float32)
        step_grad = jnp.zeros((CHUNK, SSM_HEADS), jnp.float32)
        columns = jnp.zeros((SSM_HEADS, PAIR), jnp.float32)
        shared_grad = jnp.zeros((CHUNK, PAIR), jnp.float32)
        leaving, fresh, kept = [], [], []
        for k in range(SSM_HEADS // 2):
            lanes = slice(k * PAIR, (k + 1) * PAIR)
            grad = mixgrad_ref[:, lanes]
            grad_low = grad.astype(low)
            sums = per_pair(cumul, k, low_half)
            decay = jnp.exp(jnp.minimum(sums - row_pair(across, k, low_half), 0.0))
            weights = decay * shared
            value = inner[:, lanes]
            steps = per_pair(step, k, low_half)
            stepped = value * steps
            end = sums[CHUNK - 1 :]
            grown = jnp.exp(sums) * entry
            faded = jnp.exp(end - sums) * tail
            passed = jnp.exp(end) * carry
            leaving.append((grad * grown).astype(low))
            fresh.append((stepped * faded).astype(low))
            kept.append(passed)
            weight_grad = dot_right_t(grad_low, diagonal(stepped.astype(low), low_half))
            local = dot_left_t(weights.astype(low), grad_low)
            local = jnp.where(low_half, local[:CHUNK], local[CHUNK:])
            shared_grad = shared_grad + weight_grad * decay
            gap_grad = weight_grad * weights
            into = reached[:, lanes] * faded
            moved = into * stepped
            at_end = jnp.sum(moved, axis=0, keepdims=True) + products[:, lanes] * passed
            sum_terms = (
                gap_grad
                + grad * incoming[:, lanes] * grown
                - moved
                + jnp.where(last_row, at_end, 0.0)
            )
            stepped_grad = into + local
            innergrad_ref[:, lanes] = stepped_grad * steps + wide_ref[0:1, lanes] * grad
            step_terms = stepped_grad * value
            for half in range(2):
                head = 2 * k + half
                chosen = low_half if half == 0 else ~low_half
                sum_grad = sum_grad + jnp.where(
                    head_lane == head,
                    jnp.sum(jnp.where(chosen, sum_terms, 0.0), axis=1, keepdims=True),
                    0.0,
                )
                step_grad = step_grad + jnp.where(
                    head_lane == head,
                    jnp.sum(jnp.where(chosen, step_terms, 0.0), axis=1, keepdims=True),
                    0.0,
                )
            column = jnp.sum(gap_grad, axis=0, keepdims=True)
            mine = ((head_row == 2 * k) & head_low) | ((head_row == 2 * k + 1) & ~head_low)
            columns = columns + jnp.where(mine, column, 0.0)
        leaving = jnp.concatenate(leaving, axis=1)
        fresh = jnp.concatenate(fresh, axis=1)
        shared_grad = jnp.where(allowed, shared_grad, 0.0).astype(low)
        out_grad = dot_right_t(leaving, state) + dot_plain(shared_grad, twice_in)
        in_grad = dot_left_t(shared_grad, state_out)
        in_grad = in_grad[:CHUNK] + in_grad[CHUNK:] + dot_right_t(fresh, adjoint_low)
        adjoint_ref[...] = adjoint * jnp.concatenate(kept, axis=1) + dot_left_t(state_out, leaving)

        place = lax.broadcasted_iota(jnp.int32, (CHUNK, PAIR), 0)
        lane = lax.broadcasted_iota(jnp.int32, (CHUNK, PAIR), 1) % CHUNK
        sum_grad = sum_grad - lax.dot_general(
            (place == lane).astype(jnp.float32),
            columns,
            (((1,), (1,)), ((), ())),
            precision=HIGH,
            preferred_element_type=jnp.float32,
        )
        early = lax.broadcasted_iota(jnp.int32, (CHUNK, CHUNK), 0)
        late = lax.broadcasted_iota(jnp.int32, (CHUNK, CHUNK), 1)
        rate_grad = dot_high((late >= early).astype(jnp.float32), sum_grad)
        raw_grad = (step_grad - rate_grad * heads_ref[1:2, :SSM_HEADS]) * jax.nn.sigmoid(raw)
        heads_out_ref[0:1, :SSM_HEADS] += jnp.sum(raw_grad, axis=0, keepdims=True)
        heads_out_ref[1:2, :SSM_HEADS] += jnp.sum(rate_grad * rate, axis=0, keepdims=True)
        out_ref[pl.ds(base, CHUNK), INNER + CHANNELS :] = raw_grad.astype(low)

        pre = jnp.concatenate([innergrad_ref[...], in_grad, out_grad], axis=1) * slope
        taps_out_ref[CONV : CONV + 1, :] += jnp.sum(pre, axis=0, keepdims=True)
        rows = conv_ref[pl.ds(base, CHUNK + 8), :]
        own = segs[8:]
        for offset in range(CONV):
            at = 8 - (CONV - 1) + offset
            same = segs[at : at + CHUNK] == own
            taps_out_ref[offset : offset + 1, :] += jnp.sum(
                jnp.where(same, pre * rows[at : at + CHUNK], 0.0), axis=0, keepdims=True
            )
        later = jnp.concatenate([pre, pre_ref[...]])
        later_segs = seg_ref[pl.ds(base + 8, CHUNK + 8), :]
        conv_grad = jnp.zeros((CHUNK, CHANNELS), jnp.float32)
        for offset in range(CONV):
            at = CONV - 1 - offset
            same = later_segs[at : at + CHUNK] == own
            conv_grad = conv_grad + jnp.where(
                same, later[at : at + CHUNK] * taps_ref[offset : offset + 1], 0.0
            )
        out_ref[pl.ds(base, CHUNK), INNER : INNER + CHANNELS] = conv_grad.astype(low)
        pre_ref[...] = pre[:8]
        return 0

    lax.fori_loop(0, chunks, body, 0)


def call(kernel, outs, scratch, flops, *args):
    size = sum(a.size * a.dtype.itemsize for a in args)
    whole = pl.BlockSpec(memory_space=pltpu.VMEM)
    return pl.pallas_call(
        kernel,
        out_shape=[jax.ShapeDtypeStruct(shape, kind) for shape, kind in outs],
        in_specs=[whole] * len(args),
        out_specs=[whole] * len(outs),
        scratch_shapes=[pltpu.VMEM(shape, jnp.float32) for shape in scratch],
        compiler_params=pltpu.CompilerParams(vmem_limit_bytes=56 * 1024 * 1024),
        cost_estimate=pl.CostEstimate(flops=flops, bytes_accessed=size, transcendentals=0),
    )(*args)


def shards_halo(
    tokens,
    segments,
    input_gain,
    mixer_in,
    conv_weight,
    conv_bias,
    step_bias,
    decay_log,
    skip_gain,
    mixer_gain,
    mixer_out,
    w_query,
    w_key,
    w_value,
    w_output,
    hidden_gain,
    w_gate,
    w_up,
    w_down,
    cotangent,
):
    row_count, width = tokens.shape
    halo = max(row_count // 8, 2)
    count = row_count + halo
    seq_rank = lax.axis_index("seq")
    dp_count = lax.axis_size("dp")
    low = jnp.bfloat16

    small = jnp.concatenate(
        [input_gain, conv_weight.reshape(-1), conv_bias, mixer_gain, hidden_gain]
    )
    per_row = w_query.shape[1] + w_key.shape[1] + w_value.shape[1]
    small = jnp.pad(small, (0, 16 * per_row - small.shape[0])).reshape(16, per_row)
    qkv_piece = jnp.concatenate([w_query, w_key, w_value], axis=1)
    qkv_rows = qkv_piece.shape[0]
    qkv = gather_weight(jnp.concatenate([qkv_piece, small]), False)
    smalls = (
        qkv[:, qkv_rows:].reshape(dp_count, 16, 2, per_row).transpose(0, 2, 1, 3)
    ).reshape(2 * dp_count, 16 * per_row)
    sizes = [
        input_gain.shape[0],
        conv_weight.size,
        conv_bias.shape[0],
        mixer_gain.shape[0],
        hidden_gain.shape[0],
    ]
    places_at = [sum(sizes[:k]) for k in range(6)]
    gains = [
        smalls[:, places_at[k] : places_at[k + 1]].reshape(-1).astype(jnp.float32)
        for k in range(5)
    ]
    full_input_gain, full_conv_weight, full_conv_bias, full_mixer_gain, full_hidden_gain = gains
    full_conv_weight = full_conv_weight.reshape(-1, CONV)
    qkv = qkv[:, :qkv_rows].reshape(width, 2 * per_row)
    half_q, half_k = w_query.shape[1], w_key.shape[1]
    full_mixer_in = gather_weight(mixer_in, True).reshape(width, -1)
    outs = gather_weight(jnp.concatenate([mixer_out, w_output]), False)
    full_mixer_out = outs[:, : mixer_out.shape[0]].reshape(-1, width)
    full_output = outs[:, mixer_out.shape[0] :].reshape(-1, width)
    gate_up = gather_weight(jnp.concatenate([w_gate, w_up], axis=1), True).reshape(width, -1)
    full_down = gather_weight(w_down, False).reshape(-1, width)

    seg_all = segments[0]
    tail = lax.ppermute(tokens[row_count - halo :], "seq", [(0, 1)])
    hidden_ext = jnp.concatenate([tail, tokens]).astype(jnp.float32)
    padded_seg = jnp.concatenate([jnp.full((halo,), -1, jnp.int32), seg_all])
    seg_ext = lax.dynamic_slice_in_dim(padded_seg, seq_rank * row_count, count)
    padded_places = jnp.concatenate([jnp.zeros((halo,), jnp.int32), doc_places(seg_all)])
    places = lax.dynamic_slice_in_dim(padded_places, seq_rank * row_count, count)
    seg_rows = seg_ext[halo:]

    normed, norm_pull = jax.vjp(rms_scale, hidden_ext, full_input_gain)
    normed_low = normed.astype(low)
    normed_own = normed_low[halo:]
    f32 = jnp.float32
    seg_col, seg_row = seg_ext[:, None], seg_ext[None, :]
    half = HEAD_DIM // 2
    lane = jnp.arange(PAIR)
    angle = places.astype(f32)[:, None] * (THETA ** (-(lane % half).astype(f32) / half))[None, :]
    cosine = jnp.cos(angle)
    sine = jnp.sin(angle) * jnp.where(lane % HEAD_DIM < half, -1.0, 1.0)[None, :]
    turned, attended_low = call(
        attention_forward,
        [((count, 2 * per_row), low), ((row_count, HEADS * HEAD_DIM), low)],
        [],
        10**10,
        dot_plain(normed_low, qkv),
        cosine,
        sine,
        seg_col,
        seg_row,
    )

    projected = dot_plain(normed_low, full_mixer_in)
    chunks = count // CHUNK
    seg_conv = jnp.concatenate([jnp.full((8,), -1, jnp.int32), seg_ext, jnp.full((8,), -9, jnp.int32)])
    seg_conv = seg_conv[:, None]
    seg_chunks = jnp.concatenate([seg_ext.reshape(chunks, CHUNK)] * 2, axis=1)
    taps = jnp.concatenate([full_conv_weight.T, full_conv_bias[None]])
    heads = jnp.stack([step_bias, jnp.exp(decay_log)])
    wide = jnp.stack([jnp.repeat(skip_gain, SSM_DIM), full_mixer_gain])
    mixed_low, mix, states = call(
        mixer_forward,
        [
            ((row_count, INNER), low),
            ((row_count, INNER), f32),
            ((chunks, STATE, INNER), low),
        ],
        [(count + 8, CHANNELS), (STATE, INNER), (CHUNK, INNER)],
        2 * 10**10,
        projected,
        taps,
        heads,
        wide,
        seg_conv,
        seg_chunks,
    )
    hidden_mid = (
        hidden_ext[halo:]
        + dot_plain(attended_low, full_output)
        + dot_plain(mixed_low, full_mixer_out)
    )
    normed_two, norm_two_pull = jax.vjp(rms_scale, hidden_mid, full_hidden_gain)
    normed_two_low = normed_two.astype(low)
    gate_up_part = dot_plain(normed_two_low, gate_up)
    half_ff = w_gate.shape[1]
    gate_part = two_halves(gate_up_part, 0, half_ff)
    up_part = two_halves(gate_up_part, 1, half_ff)
    sigmoid_gate = jax.nn.sigmoid(gate_part)
    activated_low = (gate_part * sigmoid_gate * up_part).astype(low)
    output = (hidden_mid + dot_plain(activated_low, full_down)).astype(low)

    act_grad = dot_right_t(cotangent, full_down)
    grad_down = scatter_weight(dot_left_t(activated_low, cotangent).astype(low), False)
    gate_grad_low, up_grad_low = ffn_backward_grads(act_grad, gate_part, up_part, sigmoid_gate)
    gate_up_grad = jnp.concatenate(
        [
            gate_grad_low[:, :half_ff],
            up_grad_low[:, :half_ff],
            gate_grad_low[:, half_ff:],
            up_grad_low[:, half_ff:],
        ],
        axis=1,
    )
    grad_gate_up = scatter_weight(dot_left_t(normed_two_low, gate_up_grad).astype(low), True)
    normed_two_grad = dot_right_t(gate_up_grad, gate_up)
    hidden_part, hidden_gain_grad = norm_two_pull(normed_two_grad)
    hidden_grad = cotangent.astype(jnp.float32) + hidden_part
    branch_low = hidden_grad.astype(low)
    grad_mixer_out = scatter_weight(dot_left_t(mixed_low, branch_low).astype(low), False)
    grad_output = scatter_weight(dot_left_t(attended_low, branch_low).astype(low), True)

    (qkv_grad,) = call(
        attention_backward,
        [((count, 2 * per_row), low)],
        [(count, PAIR), (count, PAIR)],
        2 * 10**10,
        turned,
        dot_right_t(branch_low, full_output).astype(low),
        cosine,
        sine,
        seg_col,
        seg_row,
    )
    grad_qkv = scatter_weight(dot_left_t(normed_low, qkv_grad).astype(low), False)

    norm_grad = dot_right_t(branch_low, full_mixer_out)
    proj_grad_low, taps_grad, wide_grad, heads_grad = call(
        mixer_backward,
        [
            ((count, INNER + CHANNELS + SSM_HEADS), low),
            ((8, CHANNELS), f32),
            ((8, INNER), f32),
            ((8, PAIR), f32),
        ],
        [
            (count + 8, CHANNELS),
            (8, CHANNELS),
            (STATE, INNER),
            (CHUNK, INNER),
            (CHUNK, INNER),
        ],
        4 * 10**10,
        projected,
        mix,
        states,
        norm_grad,
        taps,
        heads,
        wide,
        seg_conv,
        seg_chunks,
    )
    conv_weight_grad, conv_bias_grad = taps_grad[:CONV].T, taps_grad[CONV]
    mixer_gain_grad = wide_grad[1]
    skip_grad = jnp.sum(wide_grad[0].reshape(SSM_HEADS, SSM_DIM), axis=1)
    bias_grad, decay_grad = heads_grad[0, :SSM_HEADS], heads_grad[1, :SSM_HEADS]
    normed_grad = dot_right_t(proj_grad_low, full_mixer_in) + dot_right_t(qkv_grad, qkv)
    grad_mixer_in = scatter_weight(dot_left_t(normed_low, proj_grad_low).astype(low), True)
    input_part, input_gain_grad = norm_pull(normed_grad)
    returned = lax.ppermute(input_part[:halo].astype(low), "seq", [(1, 0)]).astype(jnp.float32)
    token_grad = hidden_grad + input_part[halo:]
    token_grad = token_grad.at[row_count - halo :].add(returned)

    blocks = 2 * dp_count
    shared_sums = jnp.concatenate([bias_grad, decay_grad, skip_grad])
    small_grads = jnp.concatenate(
        [
            input_gain_grad.reshape(blocks, -1),
            conv_weight_grad.reshape(blocks, -1),
            conv_bias_grad.reshape(blocks, -1),
            mixer_gain_grad.reshape(blocks, -1),
            hidden_gain_grad.reshape(blocks, -1),
            jnp.broadcast_to(shared_sums[None], (blocks, 3 * SSM_HEADS)),
        ],
        axis=1,
    )
    sums = scatter_small(small_grads)
    small_out = [sums[places_at[k] : places_at[k + 1]] for k in range(5)]
    heads_out = sums[places_at[5] :].reshape(3, SSM_HEADS)
    return (
        output,
        token_grad,
        small_out[0],
        grad_mixer_in,
        small_out[1].reshape(-1, CONV),
        small_out[2],
        heads_out[0],
        heads_out[1],
        heads_out[2],
        small_out[3],
        grad_mixer_out,
        grad_qkv[:, :half_q],
        grad_qkv[:, half_q : half_q + half_k],
        grad_qkv[:, half_q + half_k :],
        grad_output,
        small_out[4],
        grad_gate_up[:, :half_ff],
        grad_gate_up[:, half_ff:],
        grad_down,
    )


def two_halves(value, which, half):
    return jnp.concatenate(
        [
            value[:, which * half : which * half + half],
            value[:, (2 + which) * half : (3 + which) * half],
        ],
        axis=1,
    )


def solution(mesh):
    placed = (
        P(("dp", "seq"), None),
        P("dp", None),
        P(("dp", "seq")),
        P("dp", "seq"),
        P(("dp", "seq"), None),
        P(("dp", "seq")),
        P(),
        P(),
        P(),
        P(("dp", "seq")),
        P("dp", "seq"),
        P("dp", "seq"),
        P("dp", "seq"),
        P("dp", "seq"),
        P("dp", "seq"),
        P(("dp", "seq")),
        P("dp", "seq"),
        P("dp", "seq"),
        P("dp", "seq"),
        P(("dp", "seq"), None),
    )
    return jax.shard_map(
        shards_halo if mesh.shape["seq"] == 2 else shards_general,
        mesh=mesh,
        in_specs=placed,
        out_specs=(
            P(("dp", "seq"), None),
            P(("dp", "seq"), None),
            P(("dp", "seq")),
            P("dp", "seq"),
            P(("dp", "seq"), None),
            P(("dp", "seq")),
            P(),
            P(),
            P(),
            P(("dp", "seq")),
            P("dp", "seq"),
            P("dp", "seq"),
            P("dp", "seq"),
            P("dp", "seq"),
            P("dp", "seq"),
            P(("dp", "seq")),
            P("dp", "seq"),
            P("dp", "seq"),
            P("dp", "seq"),
        ),
        check_vma=False,
    )
```

```python
import functools

import jax
import jax.numpy as jnp
from jax import lax
from jax.experimental import pallas as pl
from jax.experimental.layout import Layout, with_layout_constraint
from jax.experimental.pallas import tpu as pltpu
from jax.sharding import PartitionSpec as P

HEADS = 8
KV_HEADS = 2
HEAD_DIM = 64
SSM_HEADS = 24
SSM_DIM = 64
STATE = 128
CONV = 4
INNER = 1536
CHANNELS = 1792


EPS = 1e-05
THETA = 100000000000.0
HIGH = lax.Precision.HIGHEST


def entering(value, axis, combine, identity):
    length, index = (lax.axis_size(axis), lax.axis_index(axis))
    everything = jax.tree.map(
        lambda part, kind: lax.all_gather(part.astype(kind), axis),
        value,
        (jnp.bfloat16, jnp.bfloat16),
    )
    start = jax.tree.map(
        lambda part, zero: jnp.broadcast_to(jnp.asarray(zero, part.dtype), part.shape),
        value,
        identity,
    )

    def turn(k, before):
        reached = k < index
        new = combine(
            before, jax.tree.map(lambda part, own: part[k].astype(own.dtype), everything, value)
        )
        return jax.tree.map(lambda a, b: jnp.where(reached, a, b), new, before)

    return lax.fori_loop(0, length, turn, start)


def entering_2(value, axis, join, neutral):
    count = lax.axis_size(axis)
    place = lax.axis_index(axis)
    ahead = count - 1 - place
    gathered = jax.tree.map(
        lambda a, kind: lax.all_gather(a.astype(kind), axis),
        value,
        jax.tree.map(lambda a: jnp.bfloat16 if a.dtype == jnp.float32 else a.dtype, value),
    )
    state = jax.tree.map(lambda a, e: jnp.zeros_like(a) + jnp.asarray(e, a.dtype), value, neutral)

    def one(turn, state):
        source = count - 1 - turn
        return join(
            state,
            jax.tree.map(
                lambda a, own: lax.dynamic_index_in_dim(a, source, 0, False).astype(own.dtype),
                gathered,
                value,
            ),
        )

    return lax.fori_loop(0, ahead, one, state)


def rms_scale(values, weight):
    return values * lax.rsqrt(jnp.mean(values * values, axis=-1, keepdims=True) + EPS) * weight


def rotate(values, places, sign):
    half = values.shape[-1] // 2
    freq = THETA ** (-jnp.arange(half, dtype=jnp.float32) / half)
    angle = places.astype(jnp.float32)[:, None] * freq[None, :]
    cosine = jnp.cos(angle)[:, None, :]
    sine = sign * jnp.sin(angle)[:, None, :]
    first = values[..., :half]
    second = values[..., half:]
    return jnp.concatenate(
        [first * cosine - second * sine, second * cosine + first * sine], axis=-1
    )


def doc_places(seg_row):
    index = jnp.arange(seg_row.shape[0], dtype=jnp.int32)
    change = jnp.concatenate([jnp.ones((1,), bool), seg_row[1:] != seg_row[:-1]])
    starts = lax.cummax(jnp.where(change, index, 0), axis=0)
    return index - starts


def conv_mix(extended, weight, bias, seg_ext):
    count = extended.shape[0] - (CONV - 1)
    owner = seg_ext[CONV - 1 :]
    total = jnp.zeros((count, extended.shape[1]), jnp.float32) + bias[None, :]
    for offset in range(CONV):
        window = extended[offset : offset + count]
        same = (seg_ext[offset : offset + count] == owner)[:, None]
        total = total + jnp.where(same, window * weight[None, :, offset], 0.0)
    return jax.nn.silu(total)


def decay_terms(step_raw, step_bias, decay_log):
    step_size = jax.nn.softplus(step_raw + step_bias[None, :])
    return (step_size, jnp.cumsum(-step_size * jnp.exp(decay_log)[None, :], axis=0))


def block_state(inner, state_in, step_raw, step_bias, decay_log, seg_rows, seg_prev):
    step_size, cumul = decay_terms(step_raw, step_bias, decay_log)
    last_seg = seg_rows[-1]
    tail = (
        jnp.where((seg_rows == last_seg)[:, None], jnp.exp(cumul[-1][None, :] - cumul), 0.0)
        * step_size
    )
    weighted = inner * tail[:, :, None]
    fresh_state = jnp.einsum("shp,sn->hpn", weighted, state_in, precision=HIGH)
    carried = jnp.where(last_seg == seg_prev, jnp.exp(cumul[-1]), 0.0)
    return (carried, fresh_state)


def block_mix(
    inner,
    state_in,
    state_out,
    step_raw,
    gate_z,
    step_bias,
    decay_log,
    skip_gain,
    mixer_gain,
    start_state,
    seg_rows,
    seg_prev,
):
    step_size, cumul = decay_terms(step_raw, step_bias, decay_log)
    count = seg_rows.shape[0]
    index = jnp.arange(count)
    allowed = (seg_rows[:, None] == seg_rows[None, :]) & (index[None, :] <= index[:, None])
    gap = cumul.T[:, :, None] - cumul.T[:, None, :]
    kernel = jnp.where(allowed[None], jnp.exp(jnp.where(allowed[None], gap, 0.0)), 0.0)
    intersection = jnp.dot(state_out, state_in.T, precision=HIGH)
    weights_mat = kernel * intersection[None] * step_size.T[:, None, :]
    local_part = jnp.einsum("hts,shp->thp", weights_mat, inner, precision=HIGH)
    entry = jnp.where((seg_rows == seg_prev)[:, None], jnp.exp(cumul), 0.0)
    incoming = jnp.einsum("tn,hpn->thp", state_out, start_state, precision=HIGH) * entry[:, :, None]
    mixed = local_part + incoming + skip_gain[None, :, None] * inner
    gated = mixed.reshape(count, -1) * jax.nn.silu(gate_z)
    return rms_scale(gated, mixer_gain)


def dot_plain(left, right):
    return jnp.dot(left, right, preferred_element_type=jnp.float32)


def dot_right_t(left, right):
    return lax.dot_general(
        left, right, (((1,), (1,)), ((), ())), preferred_element_type=jnp.float32
    )


def dot_left_t(left, right):
    return lax.dot_general(
        left, right, (((0,), (0,)), ((), ())), preferred_element_type=jnp.float32
    )


def chain_forward(earlier, later):
    return (earlier[0] * later[0], later[0][:, None, None] * earlier[1] + later[1])


def chain_backward(earlier, later):
    return (earlier[0] * later[0], later[1] + later[0][:, None, None] * earlier[1])


def ffn_backward_grads(act_grad, gate_part, up_part, sigmoid_gate):
    up_grad_low = (act_grad * gate_part * sigmoid_gate).astype(jnp.bfloat16)
    gate_grad_low = (
        act_grad * up_part * sigmoid_gate * (1.0 + gate_part * (1.0 - sigmoid_gate))
    ).astype(jnp.bfloat16)
    return (gate_grad_low, up_grad_low)


def shards_general(
    tokens,
    segments,
    input_gain,
    mixer_in,
    conv_weight,
    conv_bias,
    step_bias,
    decay_log,
    skip_gain,
    mixer_gain,
    mixer_out,
    w_query,
    w_key,
    w_value,
    w_output,
    hidden_gain,
    w_gate,
    w_up,
    w_down,
    cotangent,
):
    sectioned = (
        lax.all_gather(input_gain, "seq", axis=0, tiled=True),
        lax.all_gather(mixer_in, "seq", axis=1, tiled=True),
        lax.all_gather(conv_weight, "seq", axis=0, tiled=True),
        lax.all_gather(conv_bias, "seq", axis=0, tiled=True),
        lax.all_gather(mixer_gain, "seq", axis=0, tiled=True),
        lax.all_gather(mixer_out, "seq", axis=1, tiled=True),
        lax.all_gather(w_query, "seq", axis=1, tiled=True),
        lax.all_gather(w_key, "seq", axis=1, tiled=True),
        lax.all_gather(w_value, "seq", axis=1, tiled=True),
        lax.all_gather(w_output, "seq", axis=1, tiled=True),
        lax.all_gather(hidden_gain, "seq", axis=0, tiled=True),
        lax.all_gather(w_gate, "seq", axis=1, tiled=True),
        lax.all_gather(w_up, "seq", axis=1, tiled=True),
        lax.all_gather(w_down, "seq", axis=1, tiled=True),
    )
    whole = (
        lax.all_gather(sectioned[0], "dp", axis=0, tiled=True),
        lax.all_gather(sectioned[1], "dp", axis=0, tiled=True),
        lax.all_gather(sectioned[2], "dp", axis=0, tiled=True),
        lax.all_gather(sectioned[3], "dp", axis=0, tiled=True),
        lax.all_gather(sectioned[4], "dp", axis=0, tiled=True),
        lax.all_gather(sectioned[5], "dp", axis=0, tiled=True),
        lax.all_gather(sectioned[6], "dp", axis=0, tiled=True),
        lax.all_gather(sectioned[7], "dp", axis=0, tiled=True),
        lax.all_gather(sectioned[8], "dp", axis=0, tiled=True),
        lax.all_gather(sectioned[9], "dp", axis=0, tiled=True),
        lax.all_gather(sectioned[10], "dp", axis=0, tiled=True),
        lax.all_gather(sectioned[11], "dp", axis=0, tiled=True),
        lax.all_gather(sectioned[12], "dp", axis=0, tiled=True),
        lax.all_gather(sectioned[13], "dp", axis=0, tiled=True),
    )
    (
        full_input_gain,
        full_mixer_in,
        full_conv_weight,
        full_conv_bias,
        full_mixer_gain,
        full_mixer_out,
        full_query,
        full_key,
        full_value,
        full_output,
        full_hidden_gain,
        full_gate,
        full_up,
        full_down,
    ) = whole
    row_count = tokens.shape[0]
    seg_all = segments[0]
    seq_length = seg_all.shape[0]
    seq_count = lax.axis_size("seq")
    seq_rank = lax.axis_index("seq")
    row_start = seq_rank * row_count
    places_all = doc_places(seg_all)
    seg_rows = lax.dynamic_slice_in_dim(seg_all, row_start, row_count)
    places = lax.dynamic_slice_in_dim(places_all, row_start, row_count)
    padded_seg = jnp.concatenate([jnp.full((CONV - 1,), -1, jnp.int32), seg_all])
    seg_ext = lax.dynamic_slice_in_dim(padded_seg, row_start, row_count + CONV - 1)
    seg_prev = seg_ext[CONV - 2]
    rim_start = jnp.maximum(seq_rank - 1, 0) * (CONV - 1)
    hidden_in = tokens.astype(jnp.float32)
    normed, norm_pull = jax.vjp(rms_scale, hidden_in, full_input_gain.astype(jnp.float32))
    normed_low = normed.astype(jnp.bfloat16)
    projected = dot_plain(normed_low, full_mixer_in)
    gate_z = projected[:, :INNER]
    conv_low = projected[:, INNER : INNER + CHANNELS].astype(jnp.bfloat16)
    step_raw = projected[:, INNER + CHANNELS :]
    group_size = HEADS // KV_HEADS
    score_scale = HEAD_DIM ** (-0.5)
    query = dot_plain(normed_low, full_query).reshape(row_count, HEADS, HEAD_DIM)
    key_proj = dot_plain(normed_low, full_key).reshape(row_count, KV_HEADS, HEAD_DIM)
    value_low = dot_plain(normed_low, full_value).astype(jnp.bfloat16)
    query_low = rotate(query, places, 1.0).astype(jnp.bfloat16)
    key_low = (
        rotate(key_proj, places, 1.0).astype(jnp.bfloat16).reshape(row_count, KV_HEADS * HEAD_DIM)
    )
    tail_low = conv_low[row_count - CONV + 1 :]
    keys_all, values_all, tails_all = (
        lax.all_gather(key_low, "seq", axis=0, tiled=True),
        lax.all_gather(value_low, "seq", axis=0, tiled=True),
        lax.all_gather(tail_low, "seq", axis=0, tiled=True),
    )
    rim_rows = jnp.where(
        seq_rank > 0,
        lax.dynamic_slice_in_dim(tails_all, rim_start, CONV - 1),
        jnp.zeros_like(tail_low),
    )
    extended = jnp.concatenate([rim_rows, conv_low]).astype(jnp.float32)

    def conv_piece(ext_rows, taps, shift_bias):
        return conv_mix(ext_rows, taps, shift_bias, seg_ext)

    conv_out, conv_pull = jax.vjp(
        conv_piece,
        extended,
        full_conv_weight.astype(jnp.float32),
        full_conv_bias.astype(jnp.float32),
    )
    mixed_in = conv_out.astype(jnp.bfloat16).astype(jnp.float32)
    inner = mixed_in[:, :INNER].reshape(row_count, SSM_HEADS, SSM_DIM)
    state_in = mixed_in[:, INNER : INNER + STATE]
    state_out = mixed_in[:, INNER + STATE :]

    def state_piece(inner_vals, in_vals, raw_vals, bias_vals, decay_vals):
        return block_state(inner_vals, in_vals, raw_vals, bias_vals, decay_vals, seg_rows, seg_prev)

    (carried, fresh_state), state_pull = jax.vjp(
        state_piece, inner, state_in, step_raw, step_bias, decay_log
    )
    start_state = entering(
        (carried, fresh_state),
        "seq",
        chain_forward,
        (jnp.ones_like(carried), jnp.zeros_like(fresh_state)),
    )[1]

    def mixer_piece(
        inner_vals,
        in_vals,
        out_vals,
        raw_vals,
        gate_vals,
        bias_vals,
        decay_vals,
        skip_vals,
        gain_vals,
        start_vals,
    ):
        return block_mix(
            inner_vals,
            in_vals,
            out_vals,
            raw_vals,
            gate_vals,
            bias_vals,
            decay_vals,
            skip_vals,
            gain_vals,
            start_vals,
            seg_rows,
            seg_prev,
        )

    mixed_norm, mixer_pull = jax.vjp(
        mixer_piece,
        inner,
        state_in,
        state_out,
        step_raw,
        gate_z,
        step_bias,
        decay_log,
        skip_gain,
        full_mixer_gain.astype(jnp.float32),
        start_state,
    )
    mixed_low = mixed_norm.astype(jnp.bfloat16)
    mamba_part = dot_plain(mixed_low, full_mixer_out)
    grouped = query_low.reshape(row_count, KV_HEADS, group_size, HEAD_DIM)
    keys_three = keys_all.reshape(seq_length, KV_HEADS, HEAD_DIM)
    values_three = values_all.reshape(seq_length, KV_HEADS, HEAD_DIM)
    query_index = row_start + jnp.arange(row_count)
    key_index = jnp.arange(seq_length)
    allowed = (seg_rows[:, None] == seg_all[None, :]) & (key_index[None, :] <= query_index[:, None])
    scores = (
        jnp.einsum("tkgd,skd->kgts", grouped, keys_three, preferred_element_type=jnp.float32)
        * score_scale
    )
    scores = jnp.where(allowed[None, None], scores, -1e30)
    log_total = jax.nn.logsumexp(scores, axis=-1, keepdims=True)
    probs = jnp.exp(scores - log_total)
    probs_low = probs.astype(jnp.bfloat16)
    attended = jnp.einsum(
        "kgts,skd->tkgd", probs_low, values_three, preferred_element_type=jnp.float32
    )
    attended_low = attended.reshape(row_count, HEADS * HEAD_DIM).astype(jnp.bfloat16)
    attn_part = dot_plain(attended_low, full_output)
    hidden_mid = hidden_in + attn_part + mamba_part
    normed_two, norm_two_pull = jax.vjp(rms_scale, hidden_mid, full_hidden_gain.astype(jnp.float32))
    normed_two_low = normed_two.astype(jnp.bfloat16)
    gate_part = dot_plain(normed_two_low, full_gate)
    up_part = dot_plain(normed_two_low, full_up)
    sigmoid_gate = jax.nn.sigmoid(gate_part)
    activated_low = (gate_part * sigmoid_gate * up_part).astype(jnp.bfloat16)
    output = (hidden_mid + dot_plain(activated_low, full_down)).astype(jnp.bfloat16)
    back_sectioned = (
        lax.all_gather(mixer_in, "seq", axis=1, tiled=True),
        lax.all_gather(mixer_out, "seq", axis=1, tiled=True),
        lax.all_gather(w_query, "seq", axis=1, tiled=True),
        lax.all_gather(w_key, "seq", axis=1, tiled=True),
        lax.all_gather(w_value, "seq", axis=1, tiled=True),
        lax.all_gather(w_output, "seq", axis=1, tiled=True),
        lax.all_gather(w_gate, "seq", axis=1, tiled=True),
        lax.all_gather(w_up, "seq", axis=1, tiled=True),
        lax.all_gather(w_down, "seq", axis=1, tiled=True),
    )
    back_whole = (
        lax.all_gather(back_sectioned[0], "dp", axis=0, tiled=True),
        lax.all_gather(back_sectioned[1], "dp", axis=0, tiled=True),
        lax.all_gather(back_sectioned[2], "dp", axis=0, tiled=True),
        lax.all_gather(back_sectioned[3], "dp", axis=0, tiled=True),
        lax.all_gather(back_sectioned[4], "dp", axis=0, tiled=True),
        lax.all_gather(back_sectioned[5], "dp", axis=0, tiled=True),
        lax.all_gather(back_sectioned[6], "dp", axis=0, tiled=True),
        lax.all_gather(back_sectioned[7], "dp", axis=0, tiled=True),
        lax.all_gather(back_sectioned[8], "dp", axis=0, tiled=True),
    )
    (
        back_mixer_in,
        back_mixer_out,
        back_query,
        back_key,
        back_value,
        back_output,
        back_gate,
        back_up,
        back_down,
    ) = back_whole
    act_grad = dot_right_t(cotangent, back_down)
    grad_down_part = dot_left_t(activated_low, cotangent)
    gate_grad_low, up_grad_low = ffn_backward_grads(act_grad, gate_part, up_part, sigmoid_gate)
    grad_gate_part = dot_left_t(normed_two_low, gate_grad_low)
    grad_up_part = dot_left_t(normed_two_low, up_grad_low)
    normed_two_grad = dot_right_t(gate_grad_low, back_gate) + dot_right_t(up_grad_low, back_up)
    hidden_part, hidden_gain_grad = norm_two_pull(normed_two_grad)
    hidden_grad = cotangent.astype(jnp.float32) + hidden_part
    branch_low = hidden_grad.astype(jnp.bfloat16)
    grad_mixer_out_full = dot_left_t(mixed_low, branch_low)
    norm_grad = dot_right_t(branch_low, back_mixer_out)
    (
        inner_grad_mix,
        in_grad_mix,
        out_grad,
        raw_grad_mix,
        gate_z_grad,
        bias_grad_mix,
        decay_grad_mix,
        skip_grad,
        mixer_gain_grad,
        start_grad,
    ) = mixer_pull(norm_grad)
    later_grad = entering_2(
        (carried, start_grad),
        "seq",
        chain_backward,
        (jnp.ones_like(carried), jnp.zeros_like(start_grad)),
    )[1]
    carried_grad = jnp.sum(later_grad * start_state, axis=(1, 2))
    inner_grad_st, in_grad_st, raw_grad_st, bias_grad_st, decay_grad_st = state_pull(
        (carried_grad, later_grad)
    )
    mixed_grad = jnp.concatenate(
        [
            (inner_grad_mix + inner_grad_st).reshape(row_count, INNER),
            in_grad_mix + in_grad_st,
            out_grad,
        ],
        axis=1,
    )
    ext_grad, conv_weight_grad, conv_bias_grad = conv_pull(mixed_grad)
    rim_send = jnp.where(seq_rank > 0, ext_grad[: CONV - 1], 0.0)
    rim_terms = lax.dynamic_update_slice_in_dim(
        jnp.zeros((seq_count * (CONV - 1), CHANNELS), jnp.float32), rim_send, rim_start, 0
    )
    grad_output_full = dot_left_t(attended_low, branch_low)
    attended_grad = (
        dot_right_t(branch_low, back_output)
        .astype(jnp.bfloat16)
        .reshape(row_count, KV_HEADS, group_size, HEAD_DIM)
    )
    prob_grad = jnp.einsum(
        "tkgd,skd->kgts", attended_grad, values_three, preferred_element_type=jnp.float32
    )
    inner_total = jnp.sum(probs * prob_grad, axis=-1, keepdims=True)
    score_grad = (probs * (prob_grad - inner_total)).astype(jnp.bfloat16)
    query_rot_grad = (
        jnp.einsum("kgts,skd->tkgd", score_grad, keys_three, preferred_element_type=jnp.float32)
        * score_scale
    )
    key_grad_all = (
        jnp.einsum("kgts,tkgd->skd", score_grad, grouped, preferred_element_type=jnp.float32)
        * score_scale
    )
    value_grad_all = jnp.einsum(
        "kgts,tkgd->skd", probs_low, attended_grad, preferred_element_type=jnp.float32
    )
    key_rot_grad, value_grad, rim_grad = (
        lax.psum_scatter(
            key_grad_all.reshape(seq_length, KV_HEADS * HEAD_DIM).astype(jnp.bfloat16),
            "seq",
            scatter_dimension=0,
            tiled=True,
        ).astype(jnp.float32),
        lax.psum_scatter(
            value_grad_all.reshape(seq_length, KV_HEADS * HEAD_DIM).astype(jnp.bfloat16),
            "seq",
            scatter_dimension=0,
            tiled=True,
        ).astype(jnp.float32),
        lax.psum_scatter(
            rim_terms.astype(jnp.bfloat16), "seq", scatter_dimension=0, tiled=True
        ).astype(jnp.float32),
    )
    conv_grad = ext_grad[CONV - 1 :] + jnp.concatenate(
        [jnp.zeros((row_count - CONV + 1, CHANNELS), jnp.float32), rim_grad]
    )
    proj_grad_low = jnp.concatenate(
        [gate_z_grad, conv_grad, raw_grad_mix + raw_grad_st], axis=1
    ).astype(jnp.bfloat16)
    grad_mixer_in_full = dot_left_t(normed_low, proj_grad_low)
    normed_grad = dot_right_t(proj_grad_low, back_mixer_in)
    query_grad_low = (
        rotate(query_rot_grad.reshape(row_count, HEADS, HEAD_DIM), places, -1.0)
        .reshape(row_count, HEADS * HEAD_DIM)
        .astype(jnp.bfloat16)
    )
    key_grad_low = (
        rotate(key_rot_grad.reshape(row_count, KV_HEADS, HEAD_DIM), places, -1.0)
        .reshape(row_count, KV_HEADS * HEAD_DIM)
        .astype(jnp.bfloat16)
    )
    value_grad_low = value_grad.astype(jnp.bfloat16)
    grad_query_full = dot_left_t(normed_low, query_grad_low)
    grad_key_full = dot_left_t(normed_low, key_grad_low)
    grad_value_full = dot_left_t(normed_low, value_grad_low)
    normed_grad = (
        normed_grad
        + dot_right_t(query_grad_low, back_query)
        + dot_right_t(key_grad_low, back_key)
        + dot_right_t(value_grad_low, back_value)
    )
    input_part, input_gain_grad = norm_pull(normed_grad)
    token_grad = hidden_grad + input_part
    reduced = (
        lax.psum_scatter(
            input_gain_grad.astype(jnp.bfloat16), "dp", scatter_dimension=0, tiled=True
        ).astype(jnp.float32),
        lax.psum_scatter(
            grad_mixer_in_full.astype(jnp.bfloat16), "dp", scatter_dimension=0, tiled=True
        ).astype(jnp.float32),
        lax.psum_scatter(
            conv_weight_grad.astype(jnp.bfloat16), "dp", scatter_dimension=0, tiled=True
        ).astype(jnp.float32),
        lax.psum_scatter(
            conv_bias_grad.astype(jnp.bfloat16), "dp", scatter_dimension=0, tiled=True
        ).astype(jnp.float32),
        lax.psum_scatter(
            mixer_gain_grad.astype(jnp.bfloat16), "dp", scatter_dimension=0, tiled=True
        ).astype(jnp.float32),
        lax.psum_scatter(
            grad_mixer_out_full.astype(jnp.bfloat16), "dp", scatter_dimension=0, tiled=True
        ).astype(jnp.float32),
        lax.psum_scatter(
            grad_query_full.astype(jnp.bfloat16), "dp", scatter_dimension=0, tiled=True
        ).astype(jnp.float32),
        lax.psum_scatter(
            grad_key_full.astype(jnp.bfloat16), "dp", scatter_dimension=0, tiled=True
        ).astype(jnp.float32),
        lax.psum_scatter(
            grad_value_full.astype(jnp.bfloat16), "dp", scatter_dimension=0, tiled=True
        ).astype(jnp.float32),
        lax.psum_scatter(
            grad_output_full.astype(jnp.bfloat16), "dp", scatter_dimension=0, tiled=True
        ).astype(jnp.float32),
        lax.psum_scatter(
            hidden_gain_grad.astype(jnp.bfloat16), "dp", scatter_dimension=0, tiled=True
        ).astype(jnp.float32),
        lax.psum_scatter(
            grad_gate_part.astype(jnp.bfloat16), "dp", scatter_dimension=0, tiled=True
        ).astype(jnp.float32),
        lax.psum_scatter(
            grad_up_part.astype(jnp.bfloat16), "dp", scatter_dimension=0, tiled=True
        ).astype(jnp.float32),
        lax.psum_scatter(
            grad_down_part.astype(jnp.bfloat16), "dp", scatter_dimension=0, tiled=True
        ).astype(jnp.float32),
    )
    shares = (
        lax.psum_scatter(
            reduced[0].astype(jnp.bfloat16), "seq", scatter_dimension=0, tiled=True
        ).astype(jnp.float32),
        lax.psum_scatter(
            reduced[1].astype(jnp.bfloat16), "seq", scatter_dimension=1, tiled=True
        ).astype(jnp.float32),
        lax.psum_scatter(
            reduced[2].astype(jnp.bfloat16), "seq", scatter_dimension=0, tiled=True
        ).astype(jnp.float32),
        lax.psum_scatter(
            reduced[3].astype(jnp.bfloat16), "seq", scatter_dimension=0, tiled=True
        ).astype(jnp.float32),
        lax.psum_scatter(
            reduced[4].astype(jnp.bfloat16), "seq", scatter_dimension=0, tiled=True
        ).astype(jnp.float32),
        lax.psum_scatter(
            reduced[5].astype(jnp.bfloat16), "seq", scatter_dimension=1, tiled=True
        ).astype(jnp.float32),
        lax.psum_scatter(
            reduced[6].astype(jnp.bfloat16), "seq", scatter_dimension=1, tiled=True
        ).astype(jnp.float32),
        lax.psum_scatter(
            reduced[7].astype(jnp.bfloat16), "seq", scatter_dimension=1, tiled=True
        ).astype(jnp.float32),
        lax.psum_scatter(
            reduced[8].astype(jnp.bfloat16), "seq", scatter_dimension=1, tiled=True
        ).astype(jnp.float32),
        lax.psum_scatter(
            reduced[9].astype(jnp.bfloat16), "seq", scatter_dimension=1, tiled=True
        ).astype(jnp.float32),
        lax.psum_scatter(
            reduced[10].astype(jnp.bfloat16), "seq", scatter_dimension=0, tiled=True
        ).astype(jnp.float32),
        lax.psum_scatter(
            reduced[11].astype(jnp.bfloat16), "seq", scatter_dimension=1, tiled=True
        ).astype(jnp.float32),
        lax.psum_scatter(
            reduced[12].astype(jnp.bfloat16), "seq", scatter_dimension=1, tiled=True
        ).astype(jnp.float32),
        lax.psum_scatter(
            reduced[13].astype(jnp.bfloat16), "seq", scatter_dimension=1, tiled=True
        ).astype(jnp.float32),
    )
    bias_total, decay_total, skip_total = lax.psum(
        (bias_grad_mix + bias_grad_st, decay_grad_mix + decay_grad_st, skip_grad), ("dp", "seq")
    )
    return (
        output,
        token_grad,
        shares[0],
        shares[1],
        shares[2],
        shares[3],
        bias_total,
        decay_total,
        skip_total,
        shares[4],
        shares[5],
        shares[6],
        shares[7],
        shares[8],
        shares[9],
        shares[10],
        shares[11],
        shares[12],
        shares[13],
    )


def shift(value, axis, stride, size, by=1):
    count = lax.axis_size(axis)
    pairs = []
    for place in range(count):
        own = place // stride % size
        pairs.append((place, place + ((own + by) % size - own) * stride))
    return lax.ppermute(value, axis, pairs)


def own_place(axis, stride, size):
    return lax.axis_index(axis) // stride % size


def in_order(parts, own, dim):
    size = len(parts)
    if size == 2:
        return jnp.where(
            own == 0,
            jnp.concatenate(parts, axis=dim),
            jnp.concatenate(parts[::-1], axis=dim),
        )
    ahead = [parts[-k % size] for k in range(size)] * 2
    width = parts[0].shape[dim]
    return lax.dynamic_slice_in_dim(
        jnp.concatenate(ahead, axis=dim), (size - own) % size * width, size * width, dim
    )


def send_all(value, axis, stride, size):
    return [value] + [shift(value, axis, stride, size, by) for by in range(1, size)]


def join(*values):
    return lax.optimization_barrier(values)


def dp_factors():
    count = lax.axis_size("dp")
    core = 2
    row = 4 if count > 16 else 2
    return core, row, count // (core * row)


def gather_far(piece, direct):
    core, row, far = dp_factors()
    place = ("dp", core * row, far)
    value = piece.reshape(1, 1, 1, 1, *piece.shape)
    parts = [value]
    for by in range(1, far):
        parts.append(shift(value, *place, by) if direct else shift(parts[-1], *place))
    return in_order(parts, own_place(*place), 1)


def start_rings(values, places):
    core, row, far = dp_factors()
    stages = {"row": ("dp", core, row), "seq": ("seq", 1, lax.axis_size("seq"))}
    parts = []
    for value, place in zip(values, places, strict=True):
        parts.append(send_all(value, *stages[place]))
    return parts


def finish_rings(parts, places):
    core, row, far = dp_factors()
    stages = {"row": ("dp", core, row, 2), "seq": ("seq", 1, lax.axis_size("seq"), 0)}
    values = []
    for part, place in zip(parts, places, strict=True):
        axis, stride, size, dim = stages[place]
        values.append(in_order(part, own_place(axis, stride, size), dim))
    return values


NEAR = ("row", "seq")
LAST = ("seq", "row")


def exchange_cores(parts):
    return [(part, shift(part, "dp", 1, 2)) for part in parts]


def place_pieces(plan, count, core_ref, *refs):
    sources, outs = refs[:count], refs[count:]
    core = core_ref[0]
    for half, columns, out, out_rows in plan:
        width = columns.stop - columns.start
        for s in range(sources[0].shape[0]):
            for other in range(2):
                index = 1 - core if other else core
                outs[out][0, 0, index, out_rows, s * width : (s + 1) * width] = sources[
                    2 * half + other
                ][s, 0, 0, 0, :, columns]


def assemble(pairs, plan, outs):
    sources = [value for pair in pairs for value in pair]
    seq, far, row = sources[0].shape[:3]
    core = own_place("dp", 1, 2).astype(jnp.int32).reshape(1)
    size = 4 * sum(value.size for value in sources)
    results = pl.pallas_call(
        functools.partial(place_pieces, plan, len(sources)),
        grid=(far, row),
        out_shape=[
            jax.ShapeDtypeStruct((far, row, 2, rows, seq * width), jnp.bfloat16)
            for rows, width in outs
        ],
        in_specs=[pl.BlockSpec(memory_space=pltpu.SMEM)]
        + [
            pl.BlockSpec((seq, 1, 1, *value.shape[3:]), lambda f, r: (0, f, r, 0, 0, 0))
            for value in sources
        ],
        out_specs=[
            pl.BlockSpec((1, 1, 2, rows, seq * width), lambda f, r: (f, r, 0, 0, 0))
            for rows, width in outs
        ],
        compiler_params=pltpu.CompilerParams(vmem_limit_bytes=32 * 1024 * 1024),
        cost_estimate=pl.CostEstimate(flops=0, bytes_accessed=size, transcendentals=0),
    )(core, *sources)
    return [value.reshape(-1, value.shape[-1]) for value in results]


def pick(value, index, size, dim):
    width = value.shape[dim] // size
    if size == 2:
        return jnp.where(
            index == 0,
            lax.slice_in_dim(value, 0, width, axis=dim),
            lax.slice_in_dim(value, width, 2 * width, axis=dim),
        )
    return lax.dynamic_slice_in_dim(value, index * width, width, dim)


class Scatter:
    def __init__(self, value, names, kind=jnp.bfloat16):
        core, row, far = dp_factors()
        stages = {
            "core": ("dp", 1, core, 2),
            "row": ("dp", core, row, 1),
            "far": ("dp", core * row, far, 0),
            "seq": ("seq", 1, lax.axis_size("seq"), 4),
        }
        self.steps = [stages[name] for name in names]
        self.value, self.kind, self.left, self.moving = value.astype(kind), kind, 0, None

    def start(self, direct=False):
        axis, stride, size, dim = self.steps[0]
        own = own_place(axis, stride, size)
        if direct:
            self.left = 1
            self.moving = [
                shift(pick(self.value, (own + by) % size, size, dim), axis, stride, size, by)
                for by in range(1, size)
            ]
            return
        if self.left == 0:
            self.left = size - 1
            self.moving = [pick(self.value, (own + size - 1) % size, size, dim)]
        self.moving = [shift(self.moving[0], axis, stride, size)]

    def finish(self):
        axis, stride, size, dim = self.steps[0]
        self.left -= 1
        own = own_place(axis, stride, size)
        total = pick(self.value, (own + self.left) % size, size, dim).astype(jnp.float32)
        for value in self.moving:
            total = total + value.astype(jnp.float32)
        if self.left > 0:
            self.moving = [total.astype(self.kind)]
        else:
            self.steps.pop(0)
            self.value = total.astype(self.kind) if self.steps else total


class Total:
    def __init__(self, value):
        core, row, far = dp_factors()
        self.steps = [
            ("dp", 1, core),
            ("dp", core, row),
            ("seq", 1, lax.axis_size("seq")),
            ("dp", core * row, far),
        ]
        self.value = value

    def start(self):
        self.moving = send_all(self.value, *self.steps.pop(0))[1:]

    def finish(self):
        for value in self.moving:
            self.value = self.value + value


def meet(chains, *values):
    moving = [chain.moving for chain in chains]
    moving, values = join(moving, values)
    for chain, value in zip(chains, moving, strict=True):
        chain.moving = value
        chain.finish()
    return values


def start_all(chains):
    for chain in chains:
        chain.start()


def settle(chains, *values):
    sums, values = join([chain.value for chain in chains], values)
    for chain, value in zip(chains, sums, strict=True):
        chain.value = value
    return values


SEQ_FIRST = ("core", "seq", "row", "far")
ROW_FIRST = ("core", "row", "seq", "far")


CHUNK = 64
PAIR = 128
FRONT = HEADS // KV_HEADS * HEAD_DIM + 2 * HEAD_DIM
SPLIT = (INNER + CHANNELS + SSM_HEADS) // 2


def dot_high(left, right):
    return jnp.dot(left, right, precision=HIGH, preferred_element_type=jnp.float32)


def first_lanes(rows):
    return lax.broadcasted_iota(jnp.int32, (rows, PAIR), 1) < PAIR // 2


def turn(value, cosine, sine):
    half = HEAD_DIM // 2
    lane = lax.broadcasted_iota(jnp.int32, value.shape, 1)
    other = jnp.where(
        lane % HEAD_DIM < half,
        pltpu.roll(value, PAIR - half, 1),
        pltpu.roll(value, half, 1),
    )
    return value * cosine + other * sine


def twice(value):
    rolled = pltpu.roll(value, PAIR // 2, 1)
    low_half = first_lanes(value.shape[0])
    return jnp.where(low_half, value, rolled), jnp.where(low_half, rolled, value)


def stacked(pairs):
    low_half = first_lanes(pairs[0].shape[0])
    parts = []
    for pair in pairs:
        parts.append(jnp.where(low_half, pair, 0.0))
        parts.append(jnp.where(low_half, 0.0, pair))
    return jnp.concatenate(parts, axis=0).astype(jnp.bfloat16)


def softmax_block(queries, keys, seg_col, seg_row, first_row):
    rows, wide = seg_col.shape[0], keys.shape[0]
    scores = dot_right_t(queries, keys) * HEAD_DIM ** (-0.5)
    query_at = lax.broadcasted_iota(jnp.int32, (rows, wide), 0) + first_row
    key_at = lax.broadcasted_iota(jnp.int32, (rows, wide), 1)
    allowed = (seg_col == seg_row[:, :wide]) & (key_at <= query_at)
    offset = jnp.where(allowed, 0.0, -1e30)
    scores = scores + jnp.concatenate([offset] * (queries.shape[0] // rows), axis=0)
    scores = jnp.exp(scores - jnp.max(scores, axis=1, keepdims=True))
    return scores / jnp.sum(scores, axis=1, keepdims=True)


def attention_forward(*refs):
    parts, refs = refs[: 3 * KV_HEADS], refs[3 * KV_HEADS :]
    cos_ref, sin_ref, seg_col_ref, seg_row_ref, turned_ref, out_ref = refs
    count, row_count = turned_ref.shape[0], out_ref.shape[0]
    halo = count - row_count
    block = min(row_count, 128)
    cosine, sine = cos_ref[...], sin_ref[...]
    seg_row = seg_row_ref[...]
    group = HEADS // KV_HEADS * HEAD_DIM
    for kv_head in range(KV_HEADS):
        part_refs = parts[3 * kv_head : 3 * kv_head + 3]
        base = kv_head * (group + 2 * HEAD_DIM)
        for at in range(0, group, PAIR):
            turned_ref[:, base + at : base + at + PAIR] = turn(
                part_refs[at // PAIR][...], cosine, sine
            ).astype(jnp.bfloat16)
        at = base + group
        both = part_refs[2][...]
        both = jnp.where(first_lanes(count), turn(both, cosine, sine), both).astype(jnp.bfloat16)
        turned_ref[:, at : at + PAIR] = both
        keys, values = twice(both.astype(jnp.float32))
        keys, values = keys.astype(jnp.bfloat16), values.astype(jnp.bfloat16)
        for start in range(0, row_count, block):
            first = halo + start
            queries = stacked(
                [
                    turned_ref[first : first + block, at : at + PAIR].astype(jnp.float32)
                    for at in range(base, base + group, PAIR)
                ]
            )
            wide = first + block
            probs = softmax_block(
                queries, keys[:wide], seg_col_ref[first : first + block], seg_row, first
            ).astype(jnp.bfloat16)
            result = dot_plain(probs, values[:wide])
            low_half = first_lanes(block)
            for k in range(group // PAIR):
                pair = jnp.where(
                    low_half,
                    result[2 * k * block : (2 * k + 1) * block],
                    result[(2 * k + 1) * block : (2 * k + 2) * block],
                )
                at = kv_head * group + k * PAIR
                out_ref[start : start + block, at : at + PAIR] = pair.astype(jnp.bfloat16)


def attention_backward(
    turned_ref, grad_ref, cos_ref, sin_ref, seg_col_ref, seg_row_ref, out_ref, key_ref, value_ref
):
    count, row_count = turned_ref.shape[0], grad_ref.shape[0]
    halo = count - row_count
    block = min(row_count, 128)
    cosine, sine = cos_ref[...], sin_ref[...]
    seg_row = seg_row_ref[...]
    group = HEADS // KV_HEADS * HEAD_DIM
    scale = HEAD_DIM ** (-0.5)
    for kv_head in range(KV_HEADS):
        base = kv_head * (group + 2 * HEAD_DIM)
        at = base + group
        keys, values = twice(turned_ref[:, at : at + PAIR].astype(jnp.float32))
        keys, values = keys.astype(jnp.bfloat16), values.astype(jnp.bfloat16)
        key_ref[...] = jnp.zeros_like(key_ref)
        value_ref[...] = jnp.zeros_like(value_ref)
        for start in range(0, row_count, block):
            first = halo + start
            queries = stacked(
                [
                    turned_ref[first : first + block, at : at + PAIR].astype(jnp.float32)
                    for at in range(base, base + group, PAIR)
                ]
            )
            grads = stacked(
                [
                    grad_ref[
                        start : start + block, kv_head * group + at : kv_head * group + at + PAIR
                    ].astype(jnp.float32)
                    for at in range(0, group, PAIR)
                ]
            )
            wide = first + block
            probs = softmax_block(
                queries, keys[:wide], seg_col_ref[first : first + block], seg_row, first
            )
            prob_grad = dot_right_t(grads, values[:wide])
            mean = jnp.sum(probs * prob_grad, axis=1, keepdims=True)
            score_grad = (probs * (prob_grad - mean)).astype(jnp.bfloat16)
            result = dot_plain(score_grad, keys[:wide]) * scale
            key_ref[:wide] += dot_left_t(score_grad, queries)
            value_ref[:wide] += dot_left_t(probs.astype(jnp.bfloat16), grads)
            low_half = first_lanes(block)
            for k in range(group // PAIR):
                pair = jnp.where(
                    low_half,
                    result[2 * k * block : (2 * k + 1) * block],
                    result[(2 * k + 1) * block : (2 * k + 2) * block],
                )
                pair = turn(
                    pair, cosine[first : first + block], -sine[first : first + block]
                )
                out_ref[first : first + block, base + k * PAIR : base + (k + 1) * PAIR] = (
                    pair.astype(jnp.bfloat16)
                )
        key_grad, value_grad = key_ref[...], value_ref[...]
        key_grad = (key_grad + pltpu.roll(key_grad, PAIR // 2, 1)) * scale
        value_grad = value_grad + pltpu.roll(value_grad, PAIR // 2, 1)
        both = jnp.where(first_lanes(count), turn(key_grad, cosine, -sine), value_grad)
        out_ref[:, at : at + PAIR] = both.astype(jnp.bfloat16)
        out_ref[:halo, base : base + group] = jnp.zeros((halo, group), jnp.bfloat16)


def column_halves(ref):
    half = ref.shape[1] // 2
    return ref.at[:, :half], ref.at[:, half:]


def load_conv(first_ref, second_ref, conv_ref, split):
    count = first_ref.shape[0]
    early = split - INNER
    conv_ref[:8] = jnp.zeros((8, CHANNELS), jnp.float32)
    channels = jnp.concatenate(
        [
            first_ref[:, FRONT + INNER : FRONT + split],
            second_ref[:, FRONT : FRONT + CHANNELS - early],
        ],
        axis=1,
    )
    conv_ref[8 : count + 8] = channels.astype(jnp.bfloat16).astype(jnp.float32)


def conv_chunk(conv_ref, seg_ref, taps_ref, base):
    rows = conv_ref[pl.ds(base, CHUNK + 8), :]
    segs = seg_ref[pl.ds(base, CHUNK + 8), :]
    own = segs[8:]
    total = jnp.broadcast_to(taps_ref[CONV : CONV + 1, :], (CHUNK, CHANNELS))
    for offset in range(CONV):
        at = 8 - (CONV - 1) + offset
        same = segs[at : at + CHUNK] == own
        total = total + jnp.where(same, rows[at : at + CHUNK] * taps_ref[offset : offset + 1], 0.0)
    return total, segs


def steps_of(second_ref, heads_ref, base):
    raw = second_ref[pl.ds(base, CHUNK), FRONT + SPLIT - SSM_HEADS : FRONT + SPLIT]
    raw = raw + heads_ref[0:1, :SSM_HEADS]
    step = jnp.maximum(raw, 0.0) + jnp.log1p(jnp.exp(-jnp.abs(raw)))
    rate = -step * heads_ref[1:2, :SSM_HEADS]
    early = lax.broadcasted_iota(jnp.int32, (CHUNK, CHUNK), 0)
    late = lax.broadcasted_iota(jnp.int32, (CHUNK, CHUNK), 1)
    total = dot_high((late <= early).astype(jnp.float32), rate)
    source = lax.broadcasted_iota(jnp.int32, (CHUNK, PAIR), 0)
    target = lax.broadcasted_iota(jnp.int32, (CHUNK, PAIR), 1) % CHUNK
    across = lax.dot_general(
        rate,
        (source <= target).astype(jnp.float32),
        (((0,), (0,)), ((), ())),
        precision=HIGH,
        preferred_element_type=jnp.float32,
    )
    return raw, step, rate, total, across


def chunk_masks(segs, seg_row):
    own, before, last = segs[8:], segs[7:8], segs[CHUNK + 7 :]
    at = lax.broadcasted_iota(jnp.int32, (CHUNK, PAIR), 0)
    source = lax.broadcasted_iota(jnp.int32, (CHUNK, PAIR), 1) % CHUNK
    allowed = (own == seg_row) & (source <= at)
    entry = (own == before).astype(jnp.float32)
    tail = (own == last).astype(jnp.float32)
    carry = (last == before).astype(jnp.float32)
    return allowed, entry, tail, carry


def per_pair(columns, k, low_half):
    return jnp.where(low_half, columns[:, 2 * k : 2 * k + 1], columns[:, 2 * k + 1 : 2 * k + 2])


def row_pair(rows, k, low_half):
    return jnp.where(
        low_half[:1], rows[2 * k : 2 * k + 1], rows[2 * k + 1 : 2 * k + 2]
    )


def diagonal(value, low_half):
    zero = jnp.zeros_like(value)
    return jnp.concatenate([jnp.where(low_half, value, zero), jnp.where(low_half, zero, value)])


def mixer_forward(
    proj_ref, taps_ref, heads_ref, wide_ref, seg_ref, seg_row_ref,
    out_ref, mix_ref, states_ref, conv_ref, state_ref, gated_ref,
):
    first_ref, second_ref = column_halves(proj_ref)
    count, row_count = first_ref.shape[0], out_ref.shape[0]
    low = jnp.bfloat16
    load_conv(first_ref, second_ref, conv_ref, SPLIT)
    state_ref[...] = jnp.zeros_like(state_ref)
    low_half = first_lanes(CHUNK)

    def body(c, _):
        base = pl.multiple_of(c * CHUNK, CHUNK)
        store = pl.multiple_of(jnp.maximum(c - 1, 0) * CHUNK, CHUNK)
        total, segs = conv_chunk(conv_ref, seg_ref, taps_ref, base)
        mixed = (total * jax.nn.sigmoid(total)).astype(low)
        inner = mixed[:, :INNER].astype(jnp.float32)
        state_in, state_out = mixed[:, INNER : INNER + STATE], mixed[:, INNER + STATE :]
        _, step, _, cumul, across = steps_of(second_ref, heads_ref, base)
        allowed, entry, tail, carry = chunk_masks(segs, seg_row_ref[pl.ds(c, 1), :])
        shared = dot_right_t(state_out, jnp.concatenate([state_in, state_in]))
        shared = jnp.where(allowed, shared, 0.0)
        state = state_ref[...]
        state_low = state.astype(low)
        states_ref[pl.ds(c, 1)] = state_low[None]
        incoming = dot_plain(state_out, state_low)
        squares = jnp.zeros((CHUNK, PAIR), jnp.float32)
        fresh, kept = [], []
        for k in range(SSM_HEADS // 2):
            lanes = slice(k * PAIR, (k + 1) * PAIR)
            sums = per_pair(cumul, k, low_half)
            decay = jnp.exp(jnp.minimum(sums - row_pair(across, k, low_half), 0.0))
            weights = (decay * shared).astype(low)
            value = inner[:, lanes]
            stepped = value * per_pair(step, k, low_half)
            local = dot_plain(weights, diagonal(stepped.astype(low), low_half))
            end = sums[CHUNK - 1 :]
            mix = (
                local
                + incoming[:, lanes] * (jnp.exp(sums) * entry)
                + wide_ref[0:1, lanes] * value
            )
            fresh.append((stepped * (jnp.exp(end - sums) * tail)).astype(low))
            kept.append(jnp.exp(end) * carry)
            gate = first_ref[
                pl.ds(base, CHUNK), FRONT + k * PAIR : FRONT + (k + 1) * PAIR
            ]
            gated = mix * gate * jax.nn.sigmoid(gate)
            mix_ref[pl.ds(store, CHUNK), lanes] = mix
            gated_ref[:, lanes] = gated
            squares = squares + gated * gated
        state_ref[...] = state * jnp.concatenate(kept, axis=1) + dot_left_t(
            state_in, jnp.concatenate(fresh, axis=1)
        )
        norm = lax.rsqrt(jnp.sum(squares, axis=1, keepdims=True) / INNER + EPS)
        out_ref[pl.ds(store, CHUNK), :] = (gated_ref[...] * norm * wide_ref[1:2, :]).astype(low)
        return 0

    lax.fori_loop(0, count // CHUNK, body, 0)


def mixer_backward(
    proj_ref, mix_ref, states_ref, grad_ref, attention_ref, taps_ref, heads_ref, wide_ref, seg_ref, seg_row_ref,
    both_ref, sums_ref,
    conv_ref, pre_ref, adjoint_ref, mixgrad_ref, innergrad_ref,
):
    first_ref, second_ref = column_halves(proj_ref)
    out_ref, other_ref = column_halves(both_ref)
    count, row_count = first_ref.shape[0], mix_ref.shape[0]
    low = jnp.bfloat16
    load_conv(first_ref, second_ref, conv_ref, SPLIT)
    adjoint_ref[...] = jnp.zeros_like(adjoint_ref)
    pre_ref[...] = jnp.zeros_like(pre_ref)
    sums_ref[...] = jnp.zeros_like(sums_ref)
    low_half = first_lanes(CHUNK)
    chunks = count // CHUNK

    def body(turn_at, _):
        c = chunks - 1 - turn_at
        base = pl.multiple_of(c * CHUNK, CHUNK)
        store = pl.multiple_of(jnp.maximum(c - 1, 0) * CHUNK, CHUNK)
        real = (c > 0).astype(jnp.float32)

        gate = first_ref[pl.ds(base, CHUNK), FRONT : FRONT + INNER]
        mix = mix_ref[pl.ds(store, CHUNK), :]
        norm_grad = grad_ref[pl.ds(store, CHUNK), :].astype(jnp.float32) * real
        sig = jax.nn.sigmoid(gate)
        silu = gate * sig
        gated = mix * silu
        norm = lax.rsqrt(jnp.mean(gated * gated, axis=1, keepdims=True) + EPS)
        scaled = norm_grad * wide_ref[1:2, :]
        sums_ref[5:6, :INNER] += jnp.sum(norm_grad * gated * norm, axis=0, keepdims=True)
        pull = jnp.mean(gated * scaled, axis=1, keepdims=True) * (norm * norm * norm)
        gated_grad = norm * scaled - gated * pull
        mix_grad = gated_grad * silu
        mixgrad_ref[...] = mix_grad
        gate_grad = (gated_grad * mix * (sig * (1.0 + gate * (1.0 - sig)))).astype(low)

        total, segs = conv_chunk(conv_ref, seg_ref, taps_ref, base)
        sig = jax.nn.sigmoid(total)
        mixed = (total * sig).astype(low)
        slope = sig * (1.0 + total * (1.0 - sig))
        inner = mixed[:, :INNER].astype(jnp.float32)
        state_in, state_out = mixed[:, INNER : INNER + STATE], mixed[:, INNER + STATE :]
        sums_ref[6:7, :INNER] += jnp.sum(mix_grad * inner, axis=0, keepdims=True)
        raw, step, rate, cumul, across = steps_of(second_ref, heads_ref, base)
        allowed, entry, tail, carry = chunk_masks(segs, seg_row_ref[pl.ds(c, 1), :])
        twice_in = jnp.concatenate([state_in, state_in])
        shared = jnp.where(allowed, dot_right_t(state_out, twice_in), 0.0)
        state = states_ref[pl.ds(c, 1)][0]
        adjoint = adjoint_ref[...]
        adjoint_low = adjoint.astype(low)
        incoming = dot_plain(state_out, state)
        reached = dot_plain(state_in, adjoint_low)
        products = jnp.sum(adjoint * state.astype(jnp.float32), axis=0, keepdims=True)
        head_lane = lax.broadcasted_iota(jnp.int32, (CHUNK, SSM_HEADS), 1)
        head_row = lax.broadcasted_iota(jnp.int32, (SSM_HEADS, PAIR), 0)
        head_low = lax.broadcasted_iota(jnp.int32, (SSM_HEADS, PAIR), 1) < CHUNK
        last_row = lax.broadcasted_iota(jnp.int32, (CHUNK, PAIR), 0) == CHUNK - 1
        sum_grad = jnp.zeros((CHUNK, SSM_HEADS), jnp.float32)
        step_grad = jnp.zeros((CHUNK, SSM_HEADS), jnp.float32)
        columns = jnp.zeros((SSM_HEADS, PAIR), jnp.float32)
        shared_grad = jnp.zeros((CHUNK, PAIR), jnp.float32)
        leaving, fresh, kept = [], [], []
        for k in range(SSM_HEADS // 2):
            lanes = slice(k * PAIR, (k + 1) * PAIR)
            grad = mixgrad_ref[:, lanes]
            grad_low = grad.astype(low)
            sums = per_pair(cumul, k, low_half)
            decay = jnp.exp(jnp.minimum(sums - row_pair(across, k, low_half), 0.0))
            weights = decay * shared
            value = inner[:, lanes]
            steps = per_pair(step, k, low_half)
            stepped = value * steps
            end = sums[CHUNK - 1 :]
            grown = jnp.exp(sums) * entry
            faded = jnp.exp(end - sums) * tail
            passed = jnp.exp(end) * carry
            leaving.append((grad * grown).astype(low))
            fresh.append((stepped * faded).astype(low))
            kept.append(passed)
            weight_grad = dot_right_t(grad_low, diagonal(stepped.astype(low), low_half))
            local = dot_left_t(weights.astype(low), grad_low)
            local = jnp.where(low_half, local[:CHUNK], local[CHUNK:])
            shared_grad = shared_grad + weight_grad * decay
            gap_grad = weight_grad * weights
            into = reached[:, lanes] * faded
            moved = into * stepped
            at_end = jnp.sum(moved, axis=0, keepdims=True) + products[:, lanes] * passed
            sum_terms = (
                gap_grad
                + grad * incoming[:, lanes] * grown
                - moved
                + jnp.where(last_row, at_end, 0.0)
            )
            stepped_grad = into + local
            innergrad_ref[:, lanes] = stepped_grad * steps + wide_ref[0:1, lanes] * grad
            step_terms = stepped_grad * value
            for half in range(2):
                head = 2 * k + half
                chosen = low_half if half == 0 else ~low_half
                sum_grad = sum_grad + jnp.where(
                    head_lane == head,
                    jnp.sum(jnp.where(chosen, sum_terms, 0.0), axis=1, keepdims=True),
                    0.0,
                )
                step_grad = step_grad + jnp.where(
                    head_lane == head,
                    jnp.sum(jnp.where(chosen, step_terms, 0.0), axis=1, keepdims=True),
                    0.0,
                )
            column = jnp.sum(gap_grad, axis=0, keepdims=True)
            mine = ((head_row == 2 * k) & head_low) | ((head_row == 2 * k + 1) & ~head_low)
            columns = columns + jnp.where(mine, column, 0.0)
        leaving = jnp.concatenate(leaving, axis=1)
        fresh = jnp.concatenate(fresh, axis=1)
        shared_grad = jnp.where(allowed, shared_grad, 0.0).astype(low)
        out_grad = dot_right_t(leaving, state) + dot_plain(shared_grad, twice_in)
        in_grad = dot_left_t(shared_grad, state_out)
        in_grad = in_grad[:CHUNK] + in_grad[CHUNK:] + dot_right_t(fresh, adjoint_low)
        adjoint_ref[...] = adjoint * jnp.concatenate(kept, axis=1) + dot_left_t(state_out, leaving)

        place = lax.broadcasted_iota(jnp.int32, (CHUNK, PAIR), 0)
        lane = lax.broadcasted_iota(jnp.int32, (CHUNK, PAIR), 1) % CHUNK
        sum_grad = sum_grad - lax.dot_general(
            (place == lane).astype(jnp.float32),
            columns,
            (((1,), (1,)), ((), ())),
            precision=HIGH,
            preferred_element_type=jnp.float32,
        )
        early = lax.broadcasted_iota(jnp.int32, (CHUNK, CHUNK), 0)
        late = lax.broadcasted_iota(jnp.int32, (CHUNK, CHUNK), 1)
        rate_grad = dot_high((late >= early).astype(jnp.float32), sum_grad)
        raw_grad = (step_grad - rate_grad * heads_ref[1:2, :SSM_HEADS]) * jax.nn.sigmoid(raw)
        sums_ref[7:8, :SSM_HEADS] += jnp.sum(raw_grad, axis=0, keepdims=True)
        sums_ref[8:9, :SSM_HEADS] += jnp.sum(rate_grad * rate, axis=0, keepdims=True)

        pre = jnp.concatenate([innergrad_ref[...], in_grad, out_grad], axis=1) * slope
        sums_ref[CONV : CONV + 1, :] += jnp.sum(pre, axis=0, keepdims=True)
        rows = conv_ref[pl.ds(base, CHUNK + 8), :]
        own = segs[8:]
        for offset in range(CONV):
            at = 8 - (CONV - 1) + offset
            same = segs[at : at + CHUNK] == own
            sums_ref[offset : offset + 1, :] += jnp.sum(
                jnp.where(same, pre * rows[at : at + CHUNK], 0.0), axis=0, keepdims=True
            )
        later = jnp.concatenate([pre, pre_ref[...]])
        later_segs = seg_ref[pl.ds(base + 8, CHUNK + 8), :]
        conv_grad = jnp.zeros((CHUNK, CHANNELS), jnp.float32)
        for offset in range(CONV):
            at = CONV - 1 - offset
            same = later_segs[at : at + CHUNK] == own
            conv_grad = conv_grad + jnp.where(
                same, later[at : at + CHUNK] * taps_ref[offset : offset + 1], 0.0
            )
        conv_grad = conv_grad.astype(low)
        early = SPLIT - INNER
        rest = jnp.zeros((CHUNK, out_ref.shape[1] - FRONT - SPLIT), low)
        out_ref[pl.ds(base, CHUNK), :] = jnp.concatenate(
            [attention_ref[pl.ds(base, CHUNK), :FRONT], gate_grad, conv_grad[:, :early], rest],
            axis=1,
        )
        other_ref[pl.ds(base, CHUNK), :] = jnp.concatenate(
            [
                attention_ref[pl.ds(base, CHUNK), FRONT:],
                conv_grad[:, early:],
                raw_grad.astype(low),
                rest,
            ],
            axis=1,
        )
        pre_ref[...] = pre[:8]
        return 0

    lax.fori_loop(0, chunks, body, 0)


def call(kernel, outs, scratch, flops, *args, blocks=()):
    size = sum(a.size * a.dtype.itemsize for a in args)
    whole = pl.BlockSpec(memory_space=pltpu.VMEM)
    specs = [
        pl.BlockSpec((args[0].shape[0], PAIR), functools.partial(lambda at, _: (0, at), at))
        for at in blocks
    ]
    return pl.pallas_call(
        kernel,
        grid=(1,) if blocks else (),
        out_shape=[jax.ShapeDtypeStruct(shape, kind) for shape, kind in outs],
        in_specs=specs + [whole] * (len(args) - len(blocks)),
        out_specs=[whole] * len(outs),
        scratch_shapes=[pltpu.VMEM(shape, jnp.float32) for shape in scratch],
        compiler_params=pltpu.CompilerParams(vmem_limit_bytes=56 * 1024 * 1024),
        cost_estimate=pl.CostEstimate(flops=flops, bytes_accessed=size, transcendentals=0),
    )(*args)


def shards_halo(
    tokens,
    segments,
    input_gain,
    mixer_in,
    conv_weight,
    conv_bias,
    step_bias,
    decay_log,
    skip_gain,
    mixer_gain,
    mixer_out,
    w_query,
    w_key,
    w_value,
    w_output,
    hidden_gain,
    w_gate,
    w_up,
    w_down,
    cotangent,
):
    row_count, width = tokens.shape
    halo = max(row_count // 8, 2)
    count = row_count + halo
    seq_rank = lax.axis_index("seq")
    dp_count = lax.axis_size("dp")
    low = jnp.bfloat16

    small = jnp.concatenate(
        [input_gain, conv_weight.reshape(-1), conv_bias, mixer_gain, hidden_gain]
    )
    rows = w_query.shape[0]
    small = jnp.pad(small, (0, -small.shape[0] % rows)).reshape(rows, -1)
    small_width = small.shape[1]
    half_q, half_k = w_query.shape[1], w_key.shape[1]
    front = half_q + 2 * half_k
    split = mixer_in.shape[1]
    first_piece = jnp.concatenate([w_query, w_key, w_value, mixer_in, small], axis=1)
    first_piece = jnp.pad(first_piece, ((0, 0), (0, -first_piece.shape[1] % 128)))
    first_width = first_piece.shape[1]
    half_ff, half_width = w_gate.shape[1], mixer_out.shape[1]
    out_piece = jnp.concatenate([mixer_out, w_output])
    second_piece = jnp.concatenate(
        [w_gate, w_up]
        + [
            value[at : at + rows]
            for value in (out_piece, w_down)
            for at in range(0, value.shape[0], rows)
        ],
        axis=1,
    )
    first_far = gather_far(first_piece, True)
    both = slice(0, rows // 2), slice(rows // 2, rows)

    def halves(value):
        return [value[:, :, :, :, half] for half in both]

    first_near = finish_rings(start_rings(halves(first_far), NEAR), NEAR)
    second_piece, first_near = join(second_piece, first_near)
    second_far = gather_far(second_piece, False)
    first_last = finish_rings(start_rings(first_near, LAST), LAST)
    (weights_one,) = assemble(
        exchange_cores(first_last),
        [(half, slice(0, first_width), 0, both[half]) for half in range(2)],
        [(rows, first_width)],
    )
    second_far, weights_one = join(second_far, weights_one)
    second_near = start_rings(halves(second_far), NEAR)

    smalls = jnp.stack(
        [
            weights_one[:, at + front + split : at + front + split + small_width]
            for at in (0, first_width)
        ]
    )
    smalls = smalls.reshape(2, dp_count, -1)
    smalls = smalls.transpose(1, 0, 2).reshape(2 * dp_count, -1)
    sizes = [
        input_gain.shape[0],
        conv_weight.size,
        conv_bias.shape[0],
        mixer_gain.shape[0],
        hidden_gain.shape[0],
    ]
    places_at = [sum(sizes[:k]) for k in range(6)]
    gains = [
        smalls[:, places_at[k] : places_at[k + 1]].reshape(-1).astype(jnp.float32)
        for k in range(5)
    ]
    full_input_gain, full_conv_weight, full_conv_bias, full_mixer_gain, full_hidden_gain = gains
    full_conv_weight = full_conv_weight.reshape(-1, CONV)

    half_rows = rows // 2

    def half_sums(grad):
        return [
            Scatter(grad[:, :, :, :half_rows], SEQ_FIRST),
            Scatter(grad[:, :, :, half_rows:], ROW_FIRST),
        ]

    def row_major(value):
        return with_layout_constraint(value, Layout(tuple(range(value.ndim))))

    def weight_grad(left, right):
        core, row, far = dp_factors()
        grad = row_major(dot_left_t(left, right).astype(low))
        return grad.reshape(far, row, core, -1, right.shape[1])


    seg_all = segments[0]
    tail = lax.ppermute(tokens[row_count - halo :], "seq", [(0, 1)])
    hidden_ext = jnp.concatenate([tail, tokens]).astype(jnp.float32)
    padded_seg = jnp.concatenate([jnp.full((halo,), -1, jnp.int32), seg_all])
    seg_ext = lax.dynamic_slice_in_dim(padded_seg, seq_rank * row_count, count)
    padded_places = jnp.concatenate([jnp.zeros((halo,), jnp.int32), doc_places(seg_all)])
    places = lax.dynamic_slice_in_dim(padded_places, seq_rank * row_count, count)
    seg_rows = seg_ext[halo:]

    normed, norm_pull = jax.vjp(rms_scale, hidden_ext, full_input_gain)
    normed_low = normed.astype(low)
    normed_own = normed_low[halo:]
    f32 = jnp.float32
    seg_col, seg_row = seg_ext[:, None], seg_ext[None, :]
    half = HEAD_DIM // 2
    lane = jnp.arange(PAIR)
    angle = places.astype(f32)[:, None] * (THETA ** (-(lane % half).astype(f32) / half))[None, :]
    cosine = jnp.cos(angle)
    sine = jnp.sin(angle) * jnp.where(lane % HEAD_DIM < half, -1.0, 1.0)[None, :]
    projected = row_major(dot_plain(normed_low, weights_one))
    second_near, projected = join(second_near, projected)
    second_near = finish_rings(second_near, NEAR)
    base_out = 2 * half_ff
    base_down = base_out + 2 * half_width
    second_near, projected = join(
        [
            [value[..., :base_down] for value in second_near],
            [value[..., base_down:] for value in second_near],
        ],
        projected,
    )
    second_last = start_rings(second_near[0], LAST)
    blocks = [at + k for at in (0, first_width // PAIR) for k in range(front // PAIR)]
    turned, attended_low = call(
        attention_forward,
        [((count, 2 * front), low), ((row_count, HEADS * HEAD_DIM), low)],
        [],
        10**9,
        *[projected] * len(blocks),
        cosine,
        sine,
        seg_col,
        seg_row,
        blocks=blocks,
    )
    projected, attended_low = join(projected, attended_low)

    chunks = count // CHUNK
    seg_conv = jnp.concatenate(
        [jnp.full((8,), -1, jnp.int32), seg_ext, jnp.full((8,), -9, jnp.int32)]
    )
    seg_conv = seg_conv[:, None]
    seg_chunks = jnp.concatenate([seg_ext.reshape(chunks, CHUNK)] * 2, axis=1)
    taps = jnp.concatenate([full_conv_weight.T, full_conv_bias[None]])
    heads = jnp.stack([step_bias, jnp.exp(decay_log)])
    wide = jnp.stack([jnp.repeat(skip_gain, SSM_DIM), full_mixer_gain])
    mixed_low, mix, states = call(
        mixer_forward,
        [
            ((row_count, INNER), low),
            ((row_count, INNER), f32),
            ((chunks, STATE, INNER), low),
        ],
        [(count + 8, CHANNELS), (STATE, INNER), (CHUNK, INNER)],
        10**9,
        projected,
        taps,
        heads,
        wide,
        seg_conv,
        seg_chunks,
    )
    second_last, mixed_low = join(second_last, mixed_low)
    second_last = finish_rings(second_last, LAST)
    second_near[1], second_last = join(second_near[1], second_last)
    third_last = start_rings(second_near[1], LAST)
    pieces, down_pieces = [], []
    for half in range(2):
        pieces.append((half, slice(0, base_out), 0, both[half]))
        for k in range(2):
            at = k * rows + half * (rows // 2)
            columns = slice(k * half_width, (k + 1) * half_width)
            down_pieces.append((half, columns, 0, slice(at, at + rows // 2)))
            columns = slice(base_out + k * half_width, base_out + (k + 1) * half_width)
            if at < mixer_out.shape[0]:
                pieces.append((half, columns, 1, slice(at, at + rows // 2)))
            else:
                at -= mixer_out.shape[0]
                pieces.append((half, columns, 2, slice(at, at + rows // 2)))
    gate_up, full_mixer_out, full_output = assemble(
        exchange_cores(second_last),
        pieces,
        [
            (rows, base_out),
            (mixer_out.shape[0], half_width),
            (w_output.shape[0], half_width),
        ],
    )
    hidden_mid = (
        hidden_ext[halo:]
        + dot_plain(attended_low, full_output)
        + dot_plain(mixed_low, full_mixer_out)
    )
    normed_two, norm_two_pull = jax.vjp(rms_scale, hidden_mid, full_hidden_gain)
    normed_two_low = normed_two.astype(low)
    third_last, normed_two_low = join(third_last, normed_two_low)
    third_cores = exchange_cores(finish_rings(third_last, LAST))
    gate_up_part = dot_plain(normed_two_low, gate_up)
    ffn = []
    for k in range(2):
        gate_part, up_part = (
            gate_up_part[:, at : at + half_ff]
            for at in (2 * k * half_ff, (2 * k + 1) * half_ff)
        )
        sigmoid_gate = jax.nn.sigmoid(gate_part)
        ffn.append((gate_part, up_part, sigmoid_gate))
    (full_down,) = assemble(third_cores, down_pieces, [(w_down.shape[0], half_width)])
    activated_low = jnp.concatenate([(g * s * u).astype(low) for g, u, s in ffn], axis=1)
    output = (hidden_mid + dot_plain(activated_low, full_down)).astype(low)

    grad_down = weight_grad(activated_low, cotangent)
    down = Scatter(grad_down, ROW_FIRST)
    down.start()
    act_grad = dot_right_t(cotangent, full_down)
    gate_up_grad = []
    for k in range(2):
        gate_grad, up_grad = ffn_backward_grads(
            act_grad[:, k * half_ff : (k + 1) * half_ff], *ffn[k]
        )
        gate_up_grad += [gate_grad, up_grad]
    gate_up_grad = jnp.concatenate(gate_up_grad, axis=1)
    (gate_up_grad,) = meet([down], gate_up_grad)
    down.start()
    grad_gate_up = weight_grad(normed_two_low, gate_up_grad)
    grad_gate_up, gate_up_grad = join(grad_gate_up, gate_up_grad)
    ffn_sums = half_sums(grad_gate_up)
    start_all(ffn_sums)
    normed_two_grad = row_major(
        dot_right_t(gate_up_grad, gate_up)
    )
    hidden_part, hidden_gain_grad = norm_two_pull(normed_two_grad)
    hidden_grad = cotangent.astype(jnp.float32) + hidden_part
    branch_low = hidden_grad.astype(low)
    (branch_low,) = meet(ffn_sums, branch_low)
    start_all(ffn_sums)

    grad_outs = jnp.concatenate(
        [
            weight_grad(mixed_low, branch_low),
            weight_grad(attended_low, branch_low),
        ],
        axis=3,
    )
    outs = Scatter(grad_outs, ROW_FIRST)
    outs.start()
    attended_grad = dot_right_t(branch_low, full_output).astype(low)
    norm_grad = row_major(dot_right_t(branch_low, full_mixer_out))
    (qkv_grad,) = call(
        attention_backward,
        [((count, 2 * front), low)],
        [(count, PAIR), (count, PAIR)],
        10**9,
        turned,
        attended_grad,
        cosine,
        sine,
        seg_col,
        seg_row,
    )
    others = [*ffn_sums, down, outs]
    qkv_grad, norm_grad = meet(others, qkv_grad, norm_grad)
    (qkv_grad,) = settle(others, qkv_grad)
    start_all(others)
    proj_grad, small_sums = call(
        mixer_backward,
        [
            ((count, 2 * first_width), low),
            ((16, CHANNELS), f32),
        ],
        [
            (count + 8, CHANNELS),
            (8, CHANNELS),
            (STATE, INNER),
            (CHUNK, INNER),
            (CHUNK, INNER),
        ],
        10**9,
        projected,
        mix,
        states,
        norm_grad,
        qkv_grad,
        taps,
        heads,
        wide,
        seg_conv,
        seg_chunks,
    )
    (proj_grad,) = meet(others, proj_grad)
    (proj_grad,) = settle(others, proj_grad)
    start_all(others)
    grad_first = weight_grad(normed_low, proj_grad)
    grad_first, proj_grad = meet(others, grad_first, proj_grad)
    first = half_sums(grad_first)
    start_all([*first, *others])
    normed_grad = row_major(dot_right_t(proj_grad, weights_one))
    normed_grad, small_sums, hidden_gain_grad = meet(
        [*first, *others], normed_grad, small_sums, hidden_gain_grad
    )
    normed_grad, small_sums, hidden_gain_grad = settle(
        first, normed_grad, small_sums, hidden_gain_grad
    )
    start_all([*first, *others])
    input_part, input_gain_grad = norm_pull(normed_grad)
    returned = lax.ppermute(input_part[:halo].astype(low), "seq", [(1, 0)]).astype(jnp.float32)
    token_grad = hidden_grad + input_part[halo:]
    token_grad = token_grad + jnp.pad(returned, ((row_count - halo, 0), (0, 0)))

    gain_rows = jnp.stack([hidden_gain_grad, input_gain_grad])
    small = Total(small_sums + jnp.pad(gain_rows, ((9, 5), (0, CHANNELS - width))))
    meet(others)
    start_all([outs])
    small.start()
    meet([*first, small, outs])
    first.append(small)
    start_all(first)
    meet(first)
    start_all(first)
    meet(first)
    start_all(first)
    meet(first)
    first.pop()
    start_all(first)
    meet(first)
    grad_down = down.value.reshape(-1, half_width)
    grad_gate_up = jnp.concatenate(
        [chain.value.reshape(half_rows, -1) for chain in ffn_sums]
    )
    grad_outs = outs.value.reshape(-1, half_width)
    grad_mixer_out = grad_outs[: mixer_out.shape[0]]
    grad_output = grad_outs[mixer_out.shape[0] :]
    grad_first = jnp.concatenate([chain.value.reshape(half_rows, first_width) for chain in first[:2]])
    sums = small.value
    place = lax.axis_index("dp") * 2 + seq_rank

    def own_part(row, size):
        return lax.dynamic_slice(sums, (row, place * size), (1, size)).reshape(-1)

    own_taps = lax.dynamic_slice(sums, (0, place * sizes[2]), (CONV, sizes[2]))
    skip_grad = jnp.sum(sums[6, :INNER].reshape(SSM_HEADS, SSM_DIM), axis=1)
    return (
        output,
        token_grad,
        own_part(10, sizes[0]),
        grad_first[:, front : front + split],
        own_taps.T,
        own_part(CONV, sizes[2]),
        sums[7, :SSM_HEADS],
        sums[8, :SSM_HEADS],
        skip_grad,
        own_part(5, sizes[3]),
        grad_mixer_out,
        grad_first[:, :half_q],
        grad_first[:, half_q : half_q + half_k],
        grad_first[:, half_q + half_k : front],
        grad_output,
        own_part(9, sizes[4]),
        grad_gate_up[:, :half_ff],
        grad_gate_up[:, half_ff:],
        grad_down,
    )


def solution(mesh):
    placed = (
        P(("dp", "seq"), None),
        P("dp", None),
        P(("dp", "seq")),
        P("dp", "seq"),
        P(("dp", "seq"), None),
        P(("dp", "seq")),
        P(),
        P(),
        P(),
        P(("dp", "seq")),
        P("dp", "seq"),
        P("dp", "seq"),
        P("dp", "seq"),
        P("dp", "seq"),
        P("dp", "seq"),
        P(("dp", "seq")),
        P("dp", "seq"),
        P("dp", "seq"),
        P("dp", "seq"),
        P(("dp", "seq"), None),
    )
    return jax.shard_map(
        shards_halo if mesh.shape["seq"] == 2 else shards_general,
        mesh=mesh,
        in_specs=placed,
        out_specs=(
            P(("dp", "seq"), None),
            P(("dp", "seq"), None),
            P(("dp", "seq")),
            P("dp", "seq"),
            P(("dp", "seq"), None),
            P(("dp", "seq")),
            P(),
            P(),
            P(),
            P(("dp", "seq")),
            P("dp", "seq"),
            P("dp", "seq"),
            P("dp", "seq"),
            P("dp", "seq"),
            P("dp", "seq"),
            P(("dp", "seq")),
            P("dp", "seq"),
            P("dp", "seq"),
            P("dp", "seq"),
        ),
        check_vma=False,
    )
```

```python
import functools

import jax
import jax.numpy as jnp
from jax import lax
from jax.experimental import pallas as pl
from jax.experimental.layout import Layout, with_layout_constraint
from jax.experimental.pallas import tpu as pltpu
from jax.sharding import PartitionSpec as P

HEADS = 8
KV_HEADS = 2
HEAD_DIM = 64
SSM_HEADS = 24
SSM_DIM = 64
STATE = 128
CONV = 4
INNER = 1536
CHANNELS = 1792


EPS = 1e-05
THETA = 100000000000.0
HIGH = lax.Precision.HIGHEST


def entering(value, axis, combine, identity):
    length, index = (lax.axis_size(axis), lax.axis_index(axis))
    everything = jax.tree.map(
        lambda part, kind: lax.all_gather(part.astype(kind), axis),
        value,
        (jnp.bfloat16, jnp.bfloat16),
    )
    start = jax.tree.map(
        lambda part, zero: jnp.broadcast_to(jnp.asarray(zero, part.dtype), part.shape),
        value,
        identity,
    )

    def turn(k, before):
        reached = k < index
        new = combine(
            before, jax.tree.map(lambda part, own: part[k].astype(own.dtype), everything, value)
        )
        return jax.tree.map(lambda a, b: jnp.where(reached, a, b), new, before)

    return lax.fori_loop(0, length, turn, start)


def entering_2(value, axis, join, neutral):
    count = lax.axis_size(axis)
    place = lax.axis_index(axis)
    ahead = count - 1 - place
    gathered = jax.tree.map(
        lambda a, kind: lax.all_gather(a.astype(kind), axis),
        value,
        jax.tree.map(lambda a: jnp.bfloat16 if a.dtype == jnp.float32 else a.dtype, value),
    )
    state = jax.tree.map(lambda a, e: jnp.zeros_like(a) + jnp.asarray(e, a.dtype), value, neutral)

    def one(turn, state):
        source = count - 1 - turn
        return join(
            state,
            jax.tree.map(
                lambda a, own: lax.dynamic_index_in_dim(a, source, 0, False).astype(own.dtype),
                gathered,
                value,
            ),
        )

    return lax.fori_loop(0, ahead, one, state)


def rms_scale(values, weight):
    return values * lax.rsqrt(jnp.mean(values * values, axis=-1, keepdims=True) + EPS) * weight


def rotate(values, places, sign):
    half = values.shape[-1] // 2
    freq = THETA ** (-jnp.arange(half, dtype=jnp.float32) / half)
    angle = places.astype(jnp.float32)[:, None] * freq[None, :]
    cosine = jnp.cos(angle)[:, None, :]
    sine = sign * jnp.sin(angle)[:, None, :]
    first = values[..., :half]
    second = values[..., half:]
    return jnp.concatenate(
        [first * cosine - second * sine, second * cosine + first * sine], axis=-1
    )


def doc_places(seg_row):
    index = jnp.arange(seg_row.shape[0], dtype=jnp.int32)
    change = jnp.concatenate([jnp.ones((1,), bool), seg_row[1:] != seg_row[:-1]])
    starts = lax.cummax(jnp.where(change, index, 0), axis=0)
    return index - starts


def conv_mix(extended, weight, bias, seg_ext):
    count = extended.shape[0] - (CONV - 1)
    owner = seg_ext[CONV - 1 :]
    total = jnp.zeros((count, extended.shape[1]), jnp.float32) + bias[None, :]
    for offset in range(CONV):
        window = extended[offset : offset + count]
        same = (seg_ext[offset : offset + count] == owner)[:, None]
        total = total + jnp.where(same, window * weight[None, :, offset], 0.0)
    return jax.nn.silu(total)


def decay_terms(step_raw, step_bias, decay_log):
    step_size = jax.nn.softplus(step_raw + step_bias[None, :])
    return (step_size, jnp.cumsum(-step_size * jnp.exp(decay_log)[None, :], axis=0))


def block_state(inner, state_in, step_raw, step_bias, decay_log, seg_rows, seg_prev):
    step_size, cumul = decay_terms(step_raw, step_bias, decay_log)
    last_seg = seg_rows[-1]
    tail = (
        jnp.where((seg_rows == last_seg)[:, None], jnp.exp(cumul[-1][None, :] - cumul), 0.0)
        * step_size
    )
    weighted = inner * tail[:, :, None]
    fresh_state = jnp.einsum("shp,sn->hpn", weighted, state_in, precision=HIGH)
    carried = jnp.where(last_seg == seg_prev, jnp.exp(cumul[-1]), 0.0)
    return (carried, fresh_state)


def block_mix(
    inner,
    state_in,
    state_out,
    step_raw,
    gate_z,
    step_bias,
    decay_log,
    skip_gain,
    mixer_gain,
    start_state,
    seg_rows,
    seg_prev,
):
    step_size, cumul = decay_terms(step_raw, step_bias, decay_log)
    count = seg_rows.shape[0]
    index = jnp.arange(count)
    allowed = (seg_rows[:, None] == seg_rows[None, :]) & (index[None, :] <= index[:, None])
    gap = cumul.T[:, :, None] - cumul.T[:, None, :]
    kernel = jnp.where(allowed[None], jnp.exp(jnp.where(allowed[None], gap, 0.0)), 0.0)
    intersection = jnp.dot(state_out, state_in.T, precision=HIGH)
    weights_mat = kernel * intersection[None] * step_size.T[:, None, :]
    local_part = jnp.einsum("hts,shp->thp", weights_mat, inner, precision=HIGH)
    entry = jnp.where((seg_rows == seg_prev)[:, None], jnp.exp(cumul), 0.0)
    incoming = jnp.einsum("tn,hpn->thp", state_out, start_state, precision=HIGH) * entry[:, :, None]
    mixed = local_part + incoming + skip_gain[None, :, None] * inner
    gated = mixed.reshape(count, -1) * jax.nn.silu(gate_z)
    return rms_scale(gated, mixer_gain)


def dot_plain(left, right):
    return jnp.dot(left, right, preferred_element_type=jnp.float32)


def dot_right_t(left, right):
    return lax.dot_general(
        left, right, (((1,), (1,)), ((), ())), preferred_element_type=jnp.float32
    )


def dot_left_t(left, right):
    return lax.dot_general(
        left, right, (((0,), (0,)), ((), ())), preferred_element_type=jnp.float32
    )


def chain_forward(earlier, later):
    return (earlier[0] * later[0], later[0][:, None, None] * earlier[1] + later[1])


def chain_backward(earlier, later):
    return (earlier[0] * later[0], later[1] + later[0][:, None, None] * earlier[1])


def ffn_backward_grads(act_grad, gate_part, up_part, sigmoid_gate):
    up_grad_low = (act_grad * gate_part * sigmoid_gate).astype(jnp.bfloat16)
    gate_grad_low = (
        act_grad * up_part * sigmoid_gate * (1.0 + gate_part * (1.0 - sigmoid_gate))
    ).astype(jnp.bfloat16)
    return (gate_grad_low, up_grad_low)


def shards_general(
    tokens,
    segments,
    input_gain,
    mixer_in,
    conv_weight,
    conv_bias,
    step_bias,
    decay_log,
    skip_gain,
    mixer_gain,
    mixer_out,
    w_query,
    w_key,
    w_value,
    w_output,
    hidden_gain,
    w_gate,
    w_up,
    w_down,
    cotangent,
):
    sectioned = (
        lax.all_gather(input_gain, "seq", axis=0, tiled=True),
        lax.all_gather(mixer_in, "seq", axis=1, tiled=True),
        lax.all_gather(conv_weight, "seq", axis=0, tiled=True),
        lax.all_gather(conv_bias, "seq", axis=0, tiled=True),
        lax.all_gather(mixer_gain, "seq", axis=0, tiled=True),
        lax.all_gather(mixer_out, "seq", axis=1, tiled=True),
        lax.all_gather(w_query, "seq", axis=1, tiled=True),
        lax.all_gather(w_key, "seq", axis=1, tiled=True),
        lax.all_gather(w_value, "seq", axis=1, tiled=True),
        lax.all_gather(w_output, "seq", axis=1, tiled=True),
        lax.all_gather(hidden_gain, "seq", axis=0, tiled=True),
        lax.all_gather(w_gate, "seq", axis=1, tiled=True),
        lax.all_gather(w_up, "seq", axis=1, tiled=True),
        lax.all_gather(w_down, "seq", axis=1, tiled=True),
    )
    whole = (
        lax.all_gather(sectioned[0], "dp", axis=0, tiled=True),
        lax.all_gather(sectioned[1], "dp", axis=0, tiled=True),
        lax.all_gather(sectioned[2], "dp", axis=0, tiled=True),
        lax.all_gather(sectioned[3], "dp", axis=0, tiled=True),
        lax.all_gather(sectioned[4], "dp", axis=0, tiled=True),
        lax.all_gather(sectioned[5], "dp", axis=0, tiled=True),
        lax.all_gather(sectioned[6], "dp", axis=0, tiled=True),
        lax.all_gather(sectioned[7], "dp", axis=0, tiled=True),
        lax.all_gather(sectioned[8], "dp", axis=0, tiled=True),
        lax.all_gather(sectioned[9], "dp", axis=0, tiled=True),
        lax.all_gather(sectioned[10], "dp", axis=0, tiled=True),
        lax.all_gather(sectioned[11], "dp", axis=0, tiled=True),
        lax.all_gather(sectioned[12], "dp", axis=0, tiled=True),
        lax.all_gather(sectioned[13], "dp", axis=0, tiled=True),
    )
    (
        full_input_gain,
        full_mixer_in,
        full_conv_weight,
        full_conv_bias,
        full_mixer_gain,
        full_mixer_out,
        full_query,
        full_key,
        full_value,
        full_output,
        full_hidden_gain,
        full_gate,
        full_up,
        full_down,
    ) = whole
    row_count = tokens.shape[0]
    seg_all = segments[0]
    seq_length = seg_all.shape[0]
    seq_count = lax.axis_size("seq")
    seq_rank = lax.axis_index("seq")
    row_start = seq_rank * row_count
    places_all = doc_places(seg_all)
    seg_rows = lax.dynamic_slice_in_dim(seg_all, row_start, row_count)
    places = lax.dynamic_slice_in_dim(places_all, row_start, row_count)
    padded_seg = jnp.concatenate([jnp.full((CONV - 1,), -1, jnp.int32), seg_all])
    seg_ext = lax.dynamic_slice_in_dim(padded_seg, row_start, row_count + CONV - 1)
    seg_prev = seg_ext[CONV - 2]
    rim_start = jnp.maximum(seq_rank - 1, 0) * (CONV - 1)
    hidden_in = tokens.astype(jnp.float32)
    normed, norm_pull = jax.vjp(rms_scale, hidden_in, full_input_gain.astype(jnp.float32))
    normed_low = normed.astype(jnp.bfloat16)
    projected = dot_plain(normed_low, full_mixer_in)
    gate_z = projected[:, :INNER]
    conv_low = projected[:, INNER : INNER + CHANNELS].astype(jnp.bfloat16)
    step_raw = projected[:, INNER + CHANNELS :]
    group_size = HEADS // KV_HEADS
    score_scale = HEAD_DIM ** (-0.5)
    query = dot_plain(normed_low, full_query).reshape(row_count, HEADS, HEAD_DIM)
    key_proj = dot_plain(normed_low, full_key).reshape(row_count, KV_HEADS, HEAD_DIM)
    value_low = dot_plain(normed_low, full_value).astype(jnp.bfloat16)
    query_low = rotate(query, places, 1.0).astype(jnp.bfloat16)
    key_low = (
        rotate(key_proj, places, 1.0).astype(jnp.bfloat16).reshape(row_count, KV_HEADS * HEAD_DIM)
    )
    tail_low = conv_low[row_count - CONV + 1 :]
    keys_all, values_all, tails_all = (
        lax.all_gather(key_low, "seq", axis=0, tiled=True),
        lax.all_gather(value_low, "seq", axis=0, tiled=True),
        lax.all_gather(tail_low, "seq", axis=0, tiled=True),
    )
    rim_rows = jnp.where(
        seq_rank > 0,
        lax.dynamic_slice_in_dim(tails_all, rim_start, CONV - 1),
        jnp.zeros_like(tail_low),
    )
    extended = jnp.concatenate([rim_rows, conv_low]).astype(jnp.float32)

    def conv_piece(ext_rows, taps, shift_bias):
        return conv_mix(ext_rows, taps, shift_bias, seg_ext)

    conv_out, conv_pull = jax.vjp(
        conv_piece,
        extended,
        full_conv_weight.astype(jnp.float32),
        full_conv_bias.astype(jnp.float32),
    )
    mixed_in = conv_out.astype(jnp.bfloat16).astype(jnp.float32)
    inner = mixed_in[:, :INNER].reshape(row_count, SSM_HEADS, SSM_DIM)
    state_in = mixed_in[:, INNER : INNER + STATE]
    state_out = mixed_in[:, INNER + STATE :]

    def state_piece(inner_vals, in_vals, raw_vals, bias_vals, decay_vals):
        return block_state(inner_vals, in_vals, raw_vals, bias_vals, decay_vals, seg_rows, seg_prev)

    (carried, fresh_state), state_pull = jax.vjp(
        state_piece, inner, state_in, step_raw, step_bias, decay_log
    )
    start_state = entering(
        (carried, fresh_state),
        "seq",
        chain_forward,
        (jnp.ones_like(carried), jnp.zeros_like(fresh_state)),
    )[1]

    def mixer_piece(
        inner_vals,
        in_vals,
        out_vals,
        raw_vals,
        gate_vals,
        bias_vals,
        decay_vals,
        skip_vals,
        gain_vals,
        start_vals,
    ):
        return block_mix(
            inner_vals,
            in_vals,
            out_vals,
            raw_vals,
            gate_vals,
            bias_vals,
            decay_vals,
            skip_vals,
            gain_vals,
            start_vals,
            seg_rows,
            seg_prev,
        )

    mixed_norm, mixer_pull = jax.vjp(
        mixer_piece,
        inner,
        state_in,
        state_out,
        step_raw,
        gate_z,
        step_bias,
        decay_log,
        skip_gain,
        full_mixer_gain.astype(jnp.float32),
        start_state,
    )
    mixed_low = mixed_norm.astype(jnp.bfloat16)
    mamba_part = dot_plain(mixed_low, full_mixer_out)
    grouped = query_low.reshape(row_count, KV_HEADS, group_size, HEAD_DIM)
    keys_three = keys_all.reshape(seq_length, KV_HEADS, HEAD_DIM)
    values_three = values_all.reshape(seq_length, KV_HEADS, HEAD_DIM)
    query_index = row_start + jnp.arange(row_count)
    key_index = jnp.arange(seq_length)
    allowed = (seg_rows[:, None] == seg_all[None, :]) & (key_index[None, :] <= query_index[:, None])
    scores = (
        jnp.einsum("tkgd,skd->kgts", grouped, keys_three, preferred_element_type=jnp.float32)
        * score_scale
    )
    scores = jnp.where(allowed[None, None], scores, -1e30)
    log_total = jax.nn.logsumexp(scores, axis=-1, keepdims=True)
    probs = jnp.exp(scores - log_total)
    probs_low = probs.astype(jnp.bfloat16)
    attended = jnp.einsum(
        "kgts,skd->tkgd", probs_low, values_three, preferred_element_type=jnp.float32
    )
    attended_low = attended.reshape(row_count, HEADS * HEAD_DIM).astype(jnp.bfloat16)
    attn_part = dot_plain(attended_low, full_output)
    hidden_mid = hidden_in + attn_part + mamba_part
    normed_two, norm_two_pull = jax.vjp(rms_scale, hidden_mid, full_hidden_gain.astype(jnp.float32))
    normed_two_low = normed_two.astype(jnp.bfloat16)
    gate_part = dot_plain(normed_two_low, full_gate)
    up_part = dot_plain(normed_two_low, full_up)
    sigmoid_gate = jax.nn.sigmoid(gate_part)
    activated_low = (gate_part * sigmoid_gate * up_part).astype(jnp.bfloat16)
    output = (hidden_mid + dot_plain(activated_low, full_down)).astype(jnp.bfloat16)
    back_sectioned = (
        lax.all_gather(mixer_in, "seq", axis=1, tiled=True),
        lax.all_gather(mixer_out, "seq", axis=1, tiled=True),
        lax.all_gather(w_query, "seq", axis=1, tiled=True),
        lax.all_gather(w_key, "seq", axis=1, tiled=True),
        lax.all_gather(w_value, "seq", axis=1, tiled=True),
        lax.all_gather(w_output, "seq", axis=1, tiled=True),
        lax.all_gather(w_gate, "seq", axis=1, tiled=True),
        lax.all_gather(w_up, "seq", axis=1, tiled=True),
        lax.all_gather(w_down, "seq", axis=1, tiled=True),
    )
    back_whole = (
        lax.all_gather(back_sectioned[0], "dp", axis=0, tiled=True),
        lax.all_gather(back_sectioned[1], "dp", axis=0, tiled=True),
        lax.all_gather(back_sectioned[2], "dp", axis=0, tiled=True),
        lax.all_gather(back_sectioned[3], "dp", axis=0, tiled=True),
        lax.all_gather(back_sectioned[4], "dp", axis=0, tiled=True),
        lax.all_gather(back_sectioned[5], "dp", axis=0, tiled=True),
        lax.all_gather(back_sectioned[6], "dp", axis=0, tiled=True),
        lax.all_gather(back_sectioned[7], "dp", axis=0, tiled=True),
        lax.all_gather(back_sectioned[8], "dp", axis=0, tiled=True),
    )
    (
        back_mixer_in,
        back_mixer_out,
        back_query,
        back_key,
        back_value,
        back_output,
        back_gate,
        back_up,
        back_down,
    ) = back_whole
    act_grad = dot_right_t(cotangent, back_down)
    grad_down_part = dot_left_t(activated_low, cotangent)
    gate_grad_low, up_grad_low = ffn_backward_grads(act_grad, gate_part, up_part, sigmoid_gate)
    grad_gate_part = dot_left_t(normed_two_low, gate_grad_low)
    grad_up_part = dot_left_t(normed_two_low, up_grad_low)
    normed_two_grad = dot_right_t(gate_grad_low, back_gate) + dot_right_t(up_grad_low, back_up)
    hidden_part, hidden_gain_grad = norm_two_pull(normed_two_grad)
    hidden_grad = cotangent.astype(jnp.float32) + hidden_part
    branch_low = hidden_grad.astype(jnp.bfloat16)
    grad_mixer_out_full = dot_left_t(mixed_low, branch_low)
    norm_grad = dot_right_t(branch_low, back_mixer_out)
    (
        inner_grad_mix,
        in_grad_mix,
        out_grad,
        raw_grad_mix,
        gate_z_grad,
        bias_grad_mix,
        decay_grad_mix,
        skip_grad,
        mixer_gain_grad,
        start_grad,
    ) = mixer_pull(norm_grad)
    later_grad = entering_2(
        (carried, start_grad),
        "seq",
        chain_backward,
        (jnp.ones_like(carried), jnp.zeros_like(start_grad)),
    )[1]
    carried_grad = jnp.sum(later_grad * start_state, axis=(1, 2))
    inner_grad_st, in_grad_st, raw_grad_st, bias_grad_st, decay_grad_st = state_pull(
        (carried_grad, later_grad)
    )
    mixed_grad = jnp.concatenate(
        [
            (inner_grad_mix + inner_grad_st).reshape(row_count, INNER),
            in_grad_mix + in_grad_st,
            out_grad,
        ],
        axis=1,
    )
    ext_grad, conv_weight_grad, conv_bias_grad = conv_pull(mixed_grad)
    rim_send = jnp.where(seq_rank > 0, ext_grad[: CONV - 1], 0.0)
    rim_terms = lax.dynamic_update_slice_in_dim(
        jnp.zeros((seq_count * (CONV - 1), CHANNELS), jnp.float32), rim_send, rim_start, 0
    )
    grad_output_full = dot_left_t(attended_low, branch_low)
    attended_grad = (
        dot_right_t(branch_low, back_output)
        .astype(jnp.bfloat16)
        .reshape(row_count, KV_HEADS, group_size, HEAD_DIM)
    )
    prob_grad = jnp.einsum(
        "tkgd,skd->kgts", attended_grad, values_three, preferred_element_type=jnp.float32
    )
    inner_total = jnp.sum(probs * prob_grad, axis=-1, keepdims=True)
    score_grad = (probs * (prob_grad - inner_total)).astype(jnp.bfloat16)
    query_rot_grad = (
        jnp.einsum("kgts,skd->tkgd", score_grad, keys_three, preferred_element_type=jnp.float32)
        * score_scale
    )
    key_grad_all = (
        jnp.einsum("kgts,tkgd->skd", score_grad, grouped, preferred_element_type=jnp.float32)
        * score_scale
    )
    value_grad_all = jnp.einsum(
        "kgts,tkgd->skd", probs_low, attended_grad, preferred_element_type=jnp.float32
    )
    key_rot_grad, value_grad, rim_grad = (
        lax.psum_scatter(
            key_grad_all.reshape(seq_length, KV_HEADS * HEAD_DIM).astype(jnp.bfloat16),
            "seq",
            scatter_dimension=0,
            tiled=True,
        ).astype(jnp.float32),
        lax.psum_scatter(
            value_grad_all.reshape(seq_length, KV_HEADS * HEAD_DIM).astype(jnp.bfloat16),
            "seq",
            scatter_dimension=0,
            tiled=True,
        ).astype(jnp.float32),
        lax.psum_scatter(
            rim_terms.astype(jnp.bfloat16), "seq", scatter_dimension=0, tiled=True
        ).astype(jnp.float32),
    )
    conv_grad = ext_grad[CONV - 1 :] + jnp.concatenate(
        [jnp.zeros((row_count - CONV + 1, CHANNELS), jnp.float32), rim_grad]
    )
    proj_grad_low = jnp.concatenate(
        [gate_z_grad, conv_grad, raw_grad_mix + raw_grad_st], axis=1
    ).astype(jnp.bfloat16)
    grad_mixer_in_full = dot_left_t(normed_low, proj_grad_low)
    normed_grad = dot_right_t(proj_grad_low, back_mixer_in)
    query_grad_low = (
        rotate(query_rot_grad.reshape(row_count, HEADS, HEAD_DIM), places, -1.0)
        .reshape(row_count, HEADS * HEAD_DIM)
        .astype(jnp.bfloat16)
    )
    key_grad_low = (
        rotate(key_rot_grad.reshape(row_count, KV_HEADS, HEAD_DIM), places, -1.0)
        .reshape(row_count, KV_HEADS * HEAD_DIM)
        .astype(jnp.bfloat16)
    )
    value_grad_low = value_grad.astype(jnp.bfloat16)
    grad_query_full = dot_left_t(normed_low, query_grad_low)
    grad_key_full = dot_left_t(normed_low, key_grad_low)
    grad_value_full = dot_left_t(normed_low, value_grad_low)
    normed_grad = (
        normed_grad
        + dot_right_t(query_grad_low, back_query)
        + dot_right_t(key_grad_low, back_key)
        + dot_right_t(value_grad_low, back_value)
    )
    input_part, input_gain_grad = norm_pull(normed_grad)
    token_grad = hidden_grad + input_part
    reduced = (
        lax.psum_scatter(
            input_gain_grad.astype(jnp.bfloat16), "dp", scatter_dimension=0, tiled=True
        ).astype(jnp.float32),
        lax.psum_scatter(
            grad_mixer_in_full.astype(jnp.bfloat16), "dp", scatter_dimension=0, tiled=True
        ).astype(jnp.float32),
        lax.psum_scatter(
            conv_weight_grad.astype(jnp.bfloat16), "dp", scatter_dimension=0, tiled=True
        ).astype(jnp.float32),
        lax.psum_scatter(
            conv_bias_grad.astype(jnp.bfloat16), "dp", scatter_dimension=0, tiled=True
        ).astype(jnp.float32),
        lax.psum_scatter(
            mixer_gain_grad.astype(jnp.bfloat16), "dp", scatter_dimension=0, tiled=True
        ).astype(jnp.float32),
        lax.psum_scatter(
            grad_mixer_out_full.astype(jnp.bfloat16), "dp", scatter_dimension=0, tiled=True
        ).astype(jnp.float32),
        lax.psum_scatter(
            grad_query_full.astype(jnp.bfloat16), "dp", scatter_dimension=0, tiled=True
        ).astype(jnp.float32),
        lax.psum_scatter(
            grad_key_full.astype(jnp.bfloat16), "dp", scatter_dimension=0, tiled=True
        ).astype(jnp.float32),
        lax.psum_scatter(
            grad_value_full.astype(jnp.bfloat16), "dp", scatter_dimension=0, tiled=True
        ).astype(jnp.float32),
        lax.psum_scatter(
            grad_output_full.astype(jnp.bfloat16), "dp", scatter_dimension=0, tiled=True
        ).astype(jnp.float32),
        lax.psum_scatter(
            hidden_gain_grad.astype(jnp.bfloat16), "dp", scatter_dimension=0, tiled=True
        ).astype(jnp.float32),
        lax.psum_scatter(
            grad_gate_part.astype(jnp.bfloat16), "dp", scatter_dimension=0, tiled=True
        ).astype(jnp.float32),
        lax.psum_scatter(
            grad_up_part.astype(jnp.bfloat16), "dp", scatter_dimension=0, tiled=True
        ).astype(jnp.float32),
        lax.psum_scatter(
            grad_down_part.astype(jnp.bfloat16), "dp", scatter_dimension=0, tiled=True
        ).astype(jnp.float32),
    )
    shares = (
        lax.psum_scatter(
            reduced[0].astype(jnp.bfloat16), "seq", scatter_dimension=0, tiled=True
        ).astype(jnp.float32),
        lax.psum_scatter(
            reduced[1].astype(jnp.bfloat16), "seq", scatter_dimension=1, tiled=True
        ).astype(jnp.float32),
        lax.psum_scatter(
            reduced[2].astype(jnp.bfloat16), "seq", scatter_dimension=0, tiled=True
        ).astype(jnp.float32),
        lax.psum_scatter(
            reduced[3].astype(jnp.bfloat16), "seq", scatter_dimension=0, tiled=True
        ).astype(jnp.float32),
        lax.psum_scatter(
            reduced[4].astype(jnp.bfloat16), "seq", scatter_dimension=0, tiled=True
        ).astype(jnp.float32),
        lax.psum_scatter(
            reduced[5].astype(jnp.bfloat16), "seq", scatter_dimension=1, tiled=True
        ).astype(jnp.float32),
        lax.psum_scatter(
            reduced[6].astype(jnp.bfloat16), "seq", scatter_dimension=1, tiled=True
        ).astype(jnp.float32),
        lax.psum_scatter(
            reduced[7].astype(jnp.bfloat16), "seq", scatter_dimension=1, tiled=True
        ).astype(jnp.float32),
        lax.psum_scatter(
            reduced[8].astype(jnp.bfloat16), "seq", scatter_dimension=1, tiled=True
        ).astype(jnp.float32),
        lax.psum_scatter(
            reduced[9].astype(jnp.bfloat16), "seq", scatter_dimension=1, tiled=True
        ).astype(jnp.float32),
        lax.psum_scatter(
            reduced[10].astype(jnp.bfloat16), "seq", scatter_dimension=0, tiled=True
        ).astype(jnp.float32),
        lax.psum_scatter(
            reduced[11].astype(jnp.bfloat16), "seq", scatter_dimension=1, tiled=True
        ).astype(jnp.float32),
        lax.psum_scatter(
            reduced[12].astype(jnp.bfloat16), "seq", scatter_dimension=1, tiled=True
        ).astype(jnp.float32),
        lax.psum_scatter(
            reduced[13].astype(jnp.bfloat16), "seq", scatter_dimension=1, tiled=True
        ).astype(jnp.float32),
    )
    bias_total, decay_total, skip_total = lax.psum(
        (bias_grad_mix + bias_grad_st, decay_grad_mix + decay_grad_st, skip_grad), ("dp", "seq")
    )
    return (
        output,
        token_grad,
        shares[0],
        shares[1],
        shares[2],
        shares[3],
        bias_total,
        decay_total,
        skip_total,
        shares[4],
        shares[5],
        shares[6],
        shares[7],
        shares[8],
        shares[9],
        shares[10],
        shares[11],
        shares[12],
        shares[13],
    )


def shift(value, axis, stride, size, by=1):
    count = lax.axis_size(axis)
    pairs = []
    for place in range(count):
        own = place // stride % size
        pairs.append((place, place + ((own + by) % size - own) * stride))
    return lax.ppermute(value, axis, pairs)


def own_place(axis, stride, size):
    return lax.axis_index(axis) // stride % size


def in_order(parts, own, dim):
    size = len(parts)
    if size == 2:
        return jnp.where(
            own == 0,
            jnp.concatenate(parts, axis=dim),
            jnp.concatenate(parts[::-1], axis=dim),
        )
    ahead = [parts[-k % size] for k in range(size)] * 2
    width = parts[0].shape[dim]
    return lax.dynamic_slice_in_dim(
        jnp.concatenate(ahead, axis=dim), (size - own) % size * width, size * width, dim
    )


def send_all(value, axis, stride, size):
    return [value] + [shift(value, axis, stride, size, by) for by in range(1, size)]


def join(*values):
    return lax.optimization_barrier(values)


def dp_factors():
    count = lax.axis_size("dp")
    core = 2
    row = 4 if count > 16 else 2
    return core, row, count // (core * row)


def gather_far(piece, direct):
    core, row, far = dp_factors()
    place = ("dp", core * row, far)
    value = piece.reshape(1, 1, 1, 1, *piece.shape)
    parts = [value]
    for by in range(1, far):
        parts.append(shift(value, *place, by) if direct else shift(parts[-1], *place))
    return in_order(parts, own_place(*place), 1)


def start_rings(values, places):
    core, row, far = dp_factors()
    stages = {"row": ("dp", core, row), "seq": ("seq", 1, lax.axis_size("seq"))}
    parts = []
    for value, place in zip(values, places, strict=True):
        parts.append(send_all(value, *stages[place]))
    return parts


def finish_rings(parts, places):
    core, row, far = dp_factors()
    stages = {"row": ("dp", core, row, 2), "seq": ("seq", 1, lax.axis_size("seq"), 0)}
    values = []
    for part, place in zip(parts, places, strict=True):
        axis, stride, size, dim = stages[place]
        values.append(in_order(part, own_place(axis, stride, size), dim))
    return values


NEAR = ("row", "seq")
LAST = ("seq", "row")


def exchange_cores(parts):
    return [(part, shift(part, "dp", 1, 2)) for part in parts]


def place_pieces(plan, count, core_ref, *refs):
    sources, outs = refs[:count], refs[count:]
    core = core_ref[0]
    for half, columns, out, out_rows in plan:
        width = columns.stop - columns.start
        for s in range(sources[0].shape[0]):
            for other in range(2):
                index = 1 - core if other else core
                outs[out][0, 0, index, out_rows, s * width : (s + 1) * width] = sources[
                    2 * half + other
                ][s, 0, 0, 0, :, columns]


def assemble(pairs, plan, outs):
    sources = [value for pair in pairs for value in pair]
    seq, far, row = sources[0].shape[:3]
    core = own_place("dp", 1, 2).astype(jnp.int32).reshape(1)
    size = 4 * sum(value.size for value in sources)
    results = pl.pallas_call(
        functools.partial(place_pieces, plan, len(sources)),
        grid=(far, row),
        out_shape=[
            jax.ShapeDtypeStruct((far, row, 2, rows, seq * width), jnp.bfloat16)
            for rows, width in outs
        ],
        in_specs=[pl.BlockSpec(memory_space=pltpu.SMEM)]
        + [
            pl.BlockSpec((seq, 1, 1, *value.shape[3:]), lambda f, r: (0, f, r, 0, 0, 0))
            for value in sources
        ],
        out_specs=[
            pl.BlockSpec((1, 1, 2, rows, seq * width), lambda f, r: (f, r, 0, 0, 0))
            for rows, width in outs
        ],
        compiler_params=pltpu.CompilerParams(vmem_limit_bytes=32 * 1024 * 1024),
        cost_estimate=pl.CostEstimate(flops=0, bytes_accessed=size, transcendentals=0),
    )(core, *sources)
    return [value.reshape(-1, value.shape[-1]) for value in results]


def pick(value, index, size, dim):
    width = value.shape[dim] // size
    if size == 2:
        return jnp.where(
            index == 0,
            lax.slice_in_dim(value, 0, width, axis=dim),
            lax.slice_in_dim(value, width, 2 * width, axis=dim),
        )
    return lax.dynamic_slice_in_dim(value, index * width, width, dim)


class Scatter:
    def __init__(self, value, names, kind=jnp.bfloat16):
        core, row, far = dp_factors()
        stages = {
            "core": ("dp", 1, core, 2),
            "row": ("dp", core, row, 1),
            "far": ("dp", core * row, far, 0),
            "seq": ("seq", 1, lax.axis_size("seq"), 4),
        }
        self.steps = [stages[name] for name in names]
        self.value, self.kind, self.left, self.moving = value.astype(kind), kind, 0, None

    def start(self, direct=False):
        axis, stride, size, dim = self.steps[0]
        own = own_place(axis, stride, size)
        if direct:
            self.left = 1
            self.moving = [
                shift(pick(self.value, (own + by) % size, size, dim), axis, stride, size, by)
                for by in range(1, size)
            ]
            return
        if self.left == 0:
            self.left = size - 1
            self.moving = [pick(self.value, (own + size - 1) % size, size, dim)]
        self.moving = [shift(self.moving[0], axis, stride, size)]

    def finish(self):
        axis, stride, size, dim = self.steps[0]
        self.left -= 1
        own = own_place(axis, stride, size)
        total = pick(self.value, (own + self.left) % size, size, dim).astype(jnp.float32)
        for value in self.moving:
            total = total + value.astype(jnp.float32)
        if self.left > 0:
            self.moving = [total.astype(self.kind)]
        else:
            self.steps.pop(0)
            self.value = total.astype(self.kind) if self.steps else total


class Total:
    def __init__(self, value):
        core, row, far = dp_factors()
        self.steps = [
            ("dp", 1, core),
            ("dp", core * row, far),
            ("dp", core, row),
            ("seq", 1, lax.axis_size("seq")),
        ]
        self.value = value

    def start(self):
        self.moving = send_all(self.value, *self.steps.pop(0))[1:]

    def finish(self):
        for value in self.moving:
            self.value = self.value + value


def meet(chains, *values):
    moving = [chain.moving for chain in chains]
    moving, values = join(moving, values)
    for chain, value in zip(chains, moving, strict=True):
        chain.moving = value
        chain.finish()
    return values


def start_all(chains):
    for chain in chains:
        chain.start()


def settle(chains, *values):
    sums, values = join([chain.value for chain in chains], values)
    for chain, value in zip(chains, sums, strict=True):
        chain.value = value
    return values


SEQ_FIRST = ("core", "seq", "row", "far")
ROW_FIRST = ("core", "row", "seq", "far")


CHUNK = 64
PAIR = 128
FRONT = HEADS // KV_HEADS * HEAD_DIM + 2 * HEAD_DIM
SPLIT = (INNER + CHANNELS + SSM_HEADS) // 2


def dot_high(left, right):
    return jnp.dot(left, right, precision=HIGH, preferred_element_type=jnp.float32)


def first_lanes(rows):
    return lax.broadcasted_iota(jnp.int32, (rows, PAIR), 1) < PAIR // 2


def turn(value, cosine, sine):
    half = HEAD_DIM // 2
    lane = lax.broadcasted_iota(jnp.int32, value.shape, 1)
    other = jnp.where(
        lane % HEAD_DIM < half,
        pltpu.roll(value, PAIR - half, 1),
        pltpu.roll(value, half, 1),
    )
    return value * cosine + other * sine


def twice(value):
    rolled = pltpu.roll(value, PAIR // 2, 1)
    low_half = first_lanes(value.shape[0])
    return jnp.where(low_half, value, rolled), jnp.where(low_half, rolled, value)


def stacked(pairs):
    low_half = first_lanes(pairs[0].shape[0])
    parts = []
    for pair in pairs:
        parts.append(jnp.where(low_half, pair, 0.0))
        parts.append(jnp.where(low_half, 0.0, pair))
    return jnp.concatenate(parts, axis=0).astype(jnp.bfloat16)


def softmax_block(queries, keys, seg_col, seg_row, first_row):
    rows, wide = seg_col.shape[0], keys.shape[0]
    scores = dot_right_t(queries, keys) * HEAD_DIM ** (-0.5)
    query_at = lax.broadcasted_iota(jnp.int32, (rows, wide), 0) + first_row
    key_at = lax.broadcasted_iota(jnp.int32, (rows, wide), 1)
    allowed = (seg_col == seg_row[:, :wide]) & (key_at <= query_at)
    offset = jnp.where(allowed, 0.0, -1e30)
    scores = scores + jnp.concatenate([offset] * (queries.shape[0] // rows), axis=0)
    scores = jnp.exp(scores - jnp.max(scores, axis=1, keepdims=True))
    return scores / jnp.sum(scores, axis=1, keepdims=True)


def attention_forward(*refs):
    parts, refs = refs[: 3 * KV_HEADS], refs[3 * KV_HEADS :]
    cos_ref, sin_ref, seg_col_ref, seg_row_ref, turned_ref, out_ref = refs
    count, row_count = turned_ref.shape[0], out_ref.shape[0]
    halo = count - row_count
    block = min(row_count, 128)
    cosine, sine = cos_ref[...], sin_ref[...]
    seg_row = seg_row_ref[...]
    group = HEADS // KV_HEADS * HEAD_DIM
    for kv_head in range(KV_HEADS):
        part_refs = parts[3 * kv_head : 3 * kv_head + 3]
        base = kv_head * (group + 2 * HEAD_DIM)
        for at in range(0, group, PAIR):
            turned_ref[:, base + at : base + at + PAIR] = turn(
                part_refs[at // PAIR][...], cosine, sine
            ).astype(jnp.bfloat16)
        at = base + group
        both = part_refs[2][...]
        both = jnp.where(first_lanes(count), turn(both, cosine, sine), both).astype(jnp.bfloat16)
        turned_ref[:, at : at + PAIR] = both
        keys, values = twice(both.astype(jnp.float32))
        keys, values = keys.astype(jnp.bfloat16), values.astype(jnp.bfloat16)
        for start in range(0, row_count, block):
            first = halo + start
            queries = stacked(
                [
                    turned_ref[first : first + block, at : at + PAIR].astype(jnp.float32)
                    for at in range(base, base + group, PAIR)
                ]
            )
            wide = first + block
            probs = softmax_block(
                queries, keys[:wide], seg_col_ref[first : first + block], seg_row, first
            ).astype(jnp.bfloat16)
            result = dot_plain(probs, values[:wide])
            low_half = first_lanes(block)
            for k in range(group // PAIR):
                pair = jnp.where(
                    low_half,
                    result[2 * k * block : (2 * k + 1) * block],
                    result[(2 * k + 1) * block : (2 * k + 2) * block],
                )
                at = kv_head * group + k * PAIR
                out_ref[start : start + block, at : at + PAIR] = pair.astype(jnp.bfloat16)


def attention_backward(
    turned_ref, grad_ref, cos_ref, sin_ref, seg_col_ref, seg_row_ref, out_ref, key_ref, value_ref
):
    count, row_count = turned_ref.shape[0], grad_ref.shape[0]
    halo = count - row_count
    block = min(row_count, 128)
    cosine, sine = cos_ref[...], sin_ref[...]
    seg_row = seg_row_ref[...]
    group = HEADS // KV_HEADS * HEAD_DIM
    scale = HEAD_DIM ** (-0.5)
    for kv_head in range(KV_HEADS):
        base = kv_head * (group + 2 * HEAD_DIM)
        at = base + group
        keys, values = twice(turned_ref[:, at : at + PAIR].astype(jnp.float32))
        keys, values = keys.astype(jnp.bfloat16), values.astype(jnp.bfloat16)
        key_ref[...] = jnp.zeros_like(key_ref)
        value_ref[...] = jnp.zeros_like(value_ref)
        for start in range(0, row_count, block):
            first = halo + start
            queries = stacked(
                [
                    turned_ref[first : first + block, at : at + PAIR].astype(jnp.float32)
                    for at in range(base, base + group, PAIR)
                ]
            )
            grads = stacked(
                [
                    grad_ref[
                        start : start + block, kv_head * group + at : kv_head * group + at + PAIR
                    ].astype(jnp.float32)
                    for at in range(0, group, PAIR)
                ]
            )
            wide = first + block
            probs = softmax_block(
                queries, keys[:wide], seg_col_ref[first : first + block], seg_row, first
            )
            prob_grad = dot_right_t(grads, values[:wide])
            mean = jnp.sum(probs * prob_grad, axis=1, keepdims=True)
            score_grad = (probs * (prob_grad - mean)).astype(jnp.bfloat16)
            result = dot_plain(score_grad, keys[:wide]) * scale
            key_ref[:wide] += dot_left_t(score_grad, queries)
            value_ref[:wide] += dot_left_t(probs.astype(jnp.bfloat16), grads)
            low_half = first_lanes(block)
            for k in range(group // PAIR):
                pair = jnp.where(
                    low_half,
                    result[2 * k * block : (2 * k + 1) * block],
                    result[(2 * k + 1) * block : (2 * k + 2) * block],
                )
                pair = turn(
                    pair, cosine[first : first + block], -sine[first : first + block]
                )
                out_ref[first : first + block, base + k * PAIR : base + (k + 1) * PAIR] = (
                    pair.astype(jnp.bfloat16)
                )
        key_grad, value_grad = key_ref[...], value_ref[...]
        key_grad = (key_grad + pltpu.roll(key_grad, PAIR // 2, 1)) * scale
        value_grad = value_grad + pltpu.roll(value_grad, PAIR // 2, 1)
        both = jnp.where(first_lanes(count), turn(key_grad, cosine, -sine), value_grad)
        out_ref[:, at : at + PAIR] = both.astype(jnp.bfloat16)
        out_ref[:halo, base : base + group] = jnp.zeros((halo, group), jnp.bfloat16)


def column_halves(ref):
    half = ref.shape[1] // 2
    return ref.at[:, :half], ref.at[:, half:]


def load_conv(first_ref, second_ref, conv_ref, split):
    count = first_ref.shape[0]
    early = split - INNER
    conv_ref[:8] = jnp.zeros((8, CHANNELS), jnp.float32)
    channels = jnp.concatenate(
        [
            first_ref[:, FRONT + INNER : FRONT + split],
            second_ref[:, FRONT : FRONT + CHANNELS - early],
        ],
        axis=1,
    )
    conv_ref[8 : count + 8] = channels.astype(jnp.bfloat16).astype(jnp.float32)


def conv_chunk(conv_ref, seg_ref, taps_ref, base):
    rows = conv_ref[pl.ds(base, CHUNK + 8), :]
    segs = seg_ref[pl.ds(base, CHUNK + 8), :]
    own = segs[8:]
    total = jnp.broadcast_to(taps_ref[CONV : CONV + 1, :], (CHUNK, CHANNELS))
    for offset in range(CONV):
        at = 8 - (CONV - 1) + offset
        same = segs[at : at + CHUNK] == own
        total = total + jnp.where(same, rows[at : at + CHUNK] * taps_ref[offset : offset + 1], 0.0)
    return total, segs


def steps_of(second_ref, heads_ref, base):
    raw = second_ref[pl.ds(base, CHUNK), FRONT + SPLIT - SSM_HEADS : FRONT + SPLIT]
    raw = raw + heads_ref[0:1, :SSM_HEADS]
    step = jnp.maximum(raw, 0.0) + jnp.log1p(jnp.exp(-jnp.abs(raw)))
    rate = -step * heads_ref[1:2, :SSM_HEADS]
    early = lax.broadcasted_iota(jnp.int32, (CHUNK, CHUNK), 0)
    late = lax.broadcasted_iota(jnp.int32, (CHUNK, CHUNK), 1)
    total = dot_high((late <= early).astype(jnp.float32), rate)
    source = lax.broadcasted_iota(jnp.int32, (CHUNK, PAIR), 0)
    target = lax.broadcasted_iota(jnp.int32, (CHUNK, PAIR), 1) % CHUNK
    across = lax.dot_general(
        rate,
        (source <= target).astype(jnp.float32),
        (((0,), (0,)), ((), ())),
        precision=HIGH,
        preferred_element_type=jnp.float32,
    )
    return raw, step, rate, total, across


def chunk_masks(segs, seg_row):
    own, before, last = segs[8:], segs[7:8], segs[CHUNK + 7 :]
    at = lax.broadcasted_iota(jnp.int32, (CHUNK, PAIR), 0)
    source = lax.broadcasted_iota(jnp.int32, (CHUNK, PAIR), 1) % CHUNK
    allowed = (own == seg_row) & (source <= at)
    entry = (own == before).astype(jnp.float32)
    tail = (own == last).astype(jnp.float32)
    carry = (last == before).astype(jnp.float32)
    return allowed, entry, tail, carry


def per_pair(columns, k, low_half):
    return jnp.where(low_half, columns[:, 2 * k : 2 * k + 1], columns[:, 2 * k + 1 : 2 * k + 2])


def row_pair(rows, k, low_half):
    return jnp.where(
        low_half[:1], rows[2 * k : 2 * k + 1], rows[2 * k + 1 : 2 * k + 2]
    )


def diagonal(value, low_half):
    zero = jnp.zeros_like(value)
    return jnp.concatenate([jnp.where(low_half, value, zero), jnp.where(low_half, zero, value)])


def mixer_forward(
    proj_ref, taps_ref, heads_ref, wide_ref, seg_ref, seg_row_ref,
    out_ref, mix_ref, states_ref, conv_ref, state_ref, gated_ref,
):
    first_ref, second_ref = column_halves(proj_ref)
    count, row_count = first_ref.shape[0], out_ref.shape[0]
    low = jnp.bfloat16
    load_conv(first_ref, second_ref, conv_ref, SPLIT)
    state_ref[...] = jnp.zeros_like(state_ref)
    low_half = first_lanes(CHUNK)

    def body(c, _):
        base = pl.multiple_of(c * CHUNK, CHUNK)
        store = pl.multiple_of(jnp.maximum(c - 1, 0) * CHUNK, CHUNK)
        total, segs = conv_chunk(conv_ref, seg_ref, taps_ref, base)
        mixed = (total * jax.nn.sigmoid(total)).astype(low)
        inner = mixed[:, :INNER].astype(jnp.float32)
        state_in, state_out = mixed[:, INNER : INNER + STATE], mixed[:, INNER + STATE :]
        _, step, _, cumul, across = steps_of(second_ref, heads_ref, base)
        allowed, entry, tail, carry = chunk_masks(segs, seg_row_ref[pl.ds(c, 1), :])
        shared = dot_right_t(state_out, jnp.concatenate([state_in, state_in]))
        shared = jnp.where(allowed, shared, 0.0)
        state = state_ref[...]
        state_low = state.astype(low)
        states_ref[pl.ds(c, 1)] = state_low[None]
        incoming = dot_plain(state_out, state_low)
        squares = jnp.zeros((CHUNK, PAIR), jnp.float32)
        fresh, kept = [], []
        for k in range(SSM_HEADS // 2):
            lanes = slice(k * PAIR, (k + 1) * PAIR)
            sums = per_pair(cumul, k, low_half)
            decay = jnp.exp(jnp.minimum(sums - row_pair(across, k, low_half), 0.0))
            weights = (decay * shared).astype(low)
            value = inner[:, lanes]
            stepped = value * per_pair(step, k, low_half)
            local = dot_plain(weights, diagonal(stepped.astype(low), low_half))
            end = sums[CHUNK - 1 :]
            mix = (
                local
                + incoming[:, lanes] * (jnp.exp(sums) * entry)
                + wide_ref[0:1, lanes] * value
            )
            fresh.append((stepped * (jnp.exp(end - sums) * tail)).astype(low))
            kept.append(jnp.exp(end) * carry)
            gate = first_ref[
                pl.ds(base, CHUNK), FRONT + k * PAIR : FRONT + (k + 1) * PAIR
            ]
            gated = mix * gate * jax.nn.sigmoid(gate)
            mix_ref[pl.ds(store, CHUNK), lanes] = mix
            gated_ref[:, lanes] = gated
            squares = squares + gated * gated
        state_ref[...] = state * jnp.concatenate(kept, axis=1) + dot_left_t(
            state_in, jnp.concatenate(fresh, axis=1)
        )
        norm = lax.rsqrt(jnp.sum(squares, axis=1, keepdims=True) / INNER + EPS)
        out_ref[pl.ds(store, CHUNK), :] = (gated_ref[...] * norm * wide_ref[1:2, :]).astype(low)
        return 0

    lax.fori_loop(0, count // CHUNK, body, 0)


def mixer_backward(
    proj_ref, mix_ref, states_ref, grad_ref, attention_ref, taps_ref, heads_ref, wide_ref, seg_ref, seg_row_ref,
    both_ref, sums_ref,
    conv_ref, pre_ref, adjoint_ref, mixgrad_ref, innergrad_ref,
):
    first_ref, second_ref = column_halves(proj_ref)
    out_ref, other_ref = column_halves(both_ref)
    count, row_count = first_ref.shape[0], mix_ref.shape[0]
    low = jnp.bfloat16
    load_conv(first_ref, second_ref, conv_ref, SPLIT)
    adjoint_ref[...] = jnp.zeros_like(adjoint_ref)
    pre_ref[...] = jnp.zeros_like(pre_ref)
    sums_ref[...] = jnp.zeros_like(sums_ref)
    low_half = first_lanes(CHUNK)
    chunks = count // CHUNK

    def body(turn_at, _):
        c = chunks - 1 - turn_at
        base = pl.multiple_of(c * CHUNK, CHUNK)
        store = pl.multiple_of(jnp.maximum(c - 1, 0) * CHUNK, CHUNK)
        real = (c > 0).astype(jnp.float32)

        gate = first_ref[pl.ds(base, CHUNK), FRONT : FRONT + INNER]
        mix = mix_ref[pl.ds(store, CHUNK), :]
        norm_grad = grad_ref[pl.ds(store, CHUNK), :].astype(jnp.float32) * real
        sig = jax.nn.sigmoid(gate)
        silu = gate * sig
        gated = mix * silu
        norm = lax.rsqrt(jnp.mean(gated * gated, axis=1, keepdims=True) + EPS)
        scaled = norm_grad * wide_ref[1:2, :]
        sums_ref[5:6, :INNER] += jnp.sum(norm_grad * gated * norm, axis=0, keepdims=True)
        pull = jnp.mean(gated * scaled, axis=1, keepdims=True) * (norm * norm * norm)
        gated_grad = norm * scaled - gated * pull
        mix_grad = gated_grad * silu
        mixgrad_ref[...] = mix_grad
        gate_grad = (gated_grad * mix * (sig * (1.0 + gate * (1.0 - sig)))).astype(low)

        total, segs = conv_chunk(conv_ref, seg_ref, taps_ref, base)
        sig = jax.nn.sigmoid(total)
        mixed = (total * sig).astype(low)
        slope = sig * (1.0 + total * (1.0 - sig))
        inner = mixed[:, :INNER].astype(jnp.float32)
        state_in, state_out = mixed[:, INNER : INNER + STATE], mixed[:, INNER + STATE :]
        sums_ref[6:7, :INNER] += jnp.sum(mix_grad * inner, axis=0, keepdims=True)
        raw, step, rate, cumul, across = steps_of(second_ref, heads_ref, base)
        allowed, entry, tail, carry = chunk_masks(segs, seg_row_ref[pl.ds(c, 1), :])
        twice_in = jnp.concatenate([state_in, state_in])
        shared = jnp.where(allowed, dot_right_t(state_out, twice_in), 0.0)
        state = states_ref[pl.ds(c, 1)][0]
        adjoint = adjoint_ref[...]
        adjoint_low = adjoint.astype(low)
        incoming = dot_plain(state_out, state)
        reached = dot_plain(state_in, adjoint_low)
        products = jnp.sum(adjoint * state.astype(jnp.float32), axis=0, keepdims=True)
        head_lane = lax.broadcasted_iota(jnp.int32, (CHUNK, SSM_HEADS), 1)
        head_row = lax.broadcasted_iota(jnp.int32, (SSM_HEADS, PAIR), 0)
        head_low = lax.broadcasted_iota(jnp.int32, (SSM_HEADS, PAIR), 1) < CHUNK
        last_row = lax.broadcasted_iota(jnp.int32, (CHUNK, PAIR), 0) == CHUNK - 1
        sum_grad = jnp.zeros((CHUNK, SSM_HEADS), jnp.float32)
        step_grad = jnp.zeros((CHUNK, SSM_HEADS), jnp.float32)
        columns = jnp.zeros((SSM_HEADS, PAIR), jnp.float32)
        shared_grad = jnp.zeros((CHUNK, PAIR), jnp.float32)
        leaving, fresh, kept = [], [], []
        for k in range(SSM_HEADS // 2):
            lanes = slice(k * PAIR, (k + 1) * PAIR)
            grad = mixgrad_ref[:, lanes]
            grad_low = grad.astype(low)
            sums = per_pair(cumul, k, low_half)
            decay = jnp.exp(jnp.minimum(sums - row_pair(across, k, low_half), 0.0))
            weights = decay * shared
            value = inner[:, lanes]
            steps = per_pair(step, k, low_half)
            stepped = value * steps
            end = sums[CHUNK - 1 :]
            grown = jnp.exp(sums) * entry
            faded = jnp.exp(end - sums) * tail
            passed = jnp.exp(end) * carry
            leaving.append((grad * grown).astype(low))
            fresh.append((stepped * faded).astype(low))
            kept.append(passed)
            weight_grad = dot_right_t(grad_low, diagonal(stepped.astype(low), low_half))
            local = dot_left_t(weights.astype(low), grad_low)
            local = jnp.where(low_half, local[:CHUNK], local[CHUNK:])
            shared_grad = shared_grad + weight_grad * decay
            gap_grad = weight_grad * weights
            into = reached[:, lanes] * faded
            moved = into * stepped
            at_end = jnp.sum(moved, axis=0, keepdims=True) + products[:, lanes] * passed
            sum_terms = (
                gap_grad
                + grad * incoming[:, lanes] * grown
                - moved
                + jnp.where(last_row, at_end, 0.0)
            )
            stepped_grad = into + local
            innergrad_ref[:, lanes] = stepped_grad * steps + wide_ref[0:1, lanes] * grad
            step_terms = stepped_grad * value
            for half in range(2):
                head = 2 * k + half
                chosen = low_half if half == 0 else ~low_half
                sum_grad = sum_grad + jnp.where(
                    head_lane == head,
                    jnp.sum(jnp.where(chosen, sum_terms, 0.0), axis=1, keepdims=True),
                    0.0,
                )
                step_grad = step_grad + jnp.where(
                    head_lane == head,
                    jnp.sum(jnp.where(chosen, step_terms, 0.0), axis=1, keepdims=True),
                    0.0,
                )
            column = jnp.sum(gap_grad, axis=0, keepdims=True)
            mine = ((head_row == 2 * k) & head_low) | ((head_row == 2 * k + 1) & ~head_low)
            columns = columns + jnp.where(mine, column, 0.0)
        leaving = jnp.concatenate(leaving, axis=1)
        fresh = jnp.concatenate(fresh, axis=1)
        shared_grad = jnp.where(allowed, shared_grad, 0.0).astype(low)
        out_grad = dot_right_t(leaving, state) + dot_plain(shared_grad, twice_in)
        in_grad = dot_left_t(shared_grad, state_out)
        in_grad = in_grad[:CHUNK] + in_grad[CHUNK:] + dot_right_t(fresh, adjoint_low)
        adjoint_ref[...] = adjoint * jnp.concatenate(kept, axis=1) + dot_left_t(state_out, leaving)

        place = lax.broadcasted_iota(jnp.int32, (CHUNK, PAIR), 0)
        lane = lax.broadcasted_iota(jnp.int32, (CHUNK, PAIR), 1) % CHUNK
        sum_grad = sum_grad - lax.dot_general(
            (place == lane).astype(jnp.float32),
            columns,
            (((1,), (1,)), ((), ())),
            precision=HIGH,
            preferred_element_type=jnp.float32,
        )
        early = lax.broadcasted_iota(jnp.int32, (CHUNK, CHUNK), 0)
        late = lax.broadcasted_iota(jnp.int32, (CHUNK, CHUNK), 1)
        rate_grad = dot_high((late >= early).astype(jnp.float32), sum_grad)
        raw_grad = (step_grad - rate_grad * heads_ref[1:2, :SSM_HEADS]) * jax.nn.sigmoid(raw)
        sums_ref[7:8, :SSM_HEADS] += jnp.sum(raw_grad, axis=0, keepdims=True)
        sums_ref[8:9, :SSM_HEADS] += jnp.sum(rate_grad * rate, axis=0, keepdims=True)

        pre = jnp.concatenate([innergrad_ref[...], in_grad, out_grad], axis=1) * slope
        sums_ref[CONV : CONV + 1, :] += jnp.sum(pre, axis=0, keepdims=True)
        rows = conv_ref[pl.ds(base, CHUNK + 8), :]
        own = segs[8:]
        for offset in range(CONV):
            at = 8 - (CONV - 1) + offset
            same = segs[at : at + CHUNK] == own
            sums_ref[offset : offset + 1, :] += jnp.sum(
                jnp.where(same, pre * rows[at : at + CHUNK], 0.0), axis=0, keepdims=True
            )
        later = jnp.concatenate([pre, pre_ref[...]])
        later_segs = seg_ref[pl.ds(base + 8, CHUNK + 8), :]
        conv_grad = jnp.zeros((CHUNK, CHANNELS), jnp.float32)
        for offset in range(CONV):
            at = CONV - 1 - offset
            same = later_segs[at : at + CHUNK] == own
            conv_grad = conv_grad + jnp.where(
                same, later[at : at + CHUNK] * taps_ref[offset : offset + 1], 0.0
            )
        conv_grad = conv_grad.astype(low)
        early = SPLIT - INNER
        rest = jnp.zeros((CHUNK, out_ref.shape[1] - FRONT - SPLIT), low)
        out_ref[pl.ds(base, CHUNK), :] = jnp.concatenate(
            [attention_ref[pl.ds(base, CHUNK), :FRONT], gate_grad, conv_grad[:, :early], rest],
            axis=1,
        )
        other_ref[pl.ds(base, CHUNK), :] = jnp.concatenate(
            [
                attention_ref[pl.ds(base, CHUNK), FRONT:],
                conv_grad[:, early:],
                raw_grad.astype(low),
                rest,
            ],
            axis=1,
        )
        pre_ref[...] = pre[:8]
        return 0

    lax.fori_loop(0, chunks, body, 0)


def call(kernel, outs, scratch, flops, *args, blocks=()):
    size = sum(a.size * a.dtype.itemsize for a in args)
    whole = pl.BlockSpec(memory_space=pltpu.VMEM)
    specs = [
        pl.BlockSpec((args[0].shape[0], PAIR), functools.partial(lambda at, _: (0, at), at))
        for at in blocks
    ]
    return pl.pallas_call(
        kernel,
        grid=(1,) if blocks else (),
        out_shape=[jax.ShapeDtypeStruct(shape, kind) for shape, kind in outs],
        in_specs=specs + [whole] * (len(args) - len(blocks)),
        out_specs=[whole] * len(outs),
        scratch_shapes=[pltpu.VMEM(shape, jnp.float32) for shape in scratch],
        compiler_params=pltpu.CompilerParams(vmem_limit_bytes=56 * 1024 * 1024),
        cost_estimate=pl.CostEstimate(flops=flops, bytes_accessed=size, transcendentals=0),
    )(*args)


def shards_halo(
    tokens,
    segments,
    input_gain,
    mixer_in,
    conv_weight,
    conv_bias,
    step_bias,
    decay_log,
    skip_gain,
    mixer_gain,
    mixer_out,
    w_query,
    w_key,
    w_value,
    w_output,
    hidden_gain,
    w_gate,
    w_up,
    w_down,
    cotangent,
):
    row_count, width = tokens.shape
    halo = max(row_count // 8, 2)
    count = row_count + halo
    seq_rank = lax.axis_index("seq")
    dp_count = lax.axis_size("dp")
    low = jnp.bfloat16

    small = jnp.concatenate(
        [input_gain, conv_weight.reshape(-1), conv_bias, mixer_gain, hidden_gain]
    )
    rows = w_query.shape[0]
    small = jnp.pad(small, (0, -small.shape[0] % rows)).reshape(rows, -1)
    small_width = small.shape[1]
    half_q, half_k = w_query.shape[1], w_key.shape[1]
    front = half_q + 2 * half_k
    split = mixer_in.shape[1]
    first_piece = jnp.concatenate([w_query, w_key, w_value, mixer_in, small], axis=1)
    first_piece = jnp.pad(first_piece, ((0, 0), (0, -first_piece.shape[1] % 128)))
    first_width = first_piece.shape[1]
    half_ff, half_width = w_gate.shape[1], mixer_out.shape[1]
    out_piece = jnp.concatenate([mixer_out, w_output])
    second_piece = jnp.concatenate(
        [w_gate, w_up]
        + [
            value[at : at + rows]
            for value in (out_piece, w_down)
            for at in range(0, value.shape[0], rows)
        ],
        axis=1,
    )
    first_far = gather_far(first_piece, True)
    both = slice(0, rows // 2), slice(rows // 2, rows)

    def halves(value):
        return [value[:, :, :, :, half] for half in both]

    first_near = finish_rings(start_rings(halves(first_far), NEAR), NEAR)
    second_piece, first_near = join(second_piece, first_near)
    second_far = gather_far(second_piece, False)
    first_last = finish_rings(start_rings(first_near, LAST), LAST)
    (weights_one,) = assemble(
        exchange_cores(first_last),
        [(half, slice(0, first_width), 0, both[half]) for half in range(2)],
        [(rows, first_width)],
    )
    second_far, weights_one = join(second_far, weights_one)
    second_near = start_rings(halves(second_far), NEAR)

    smalls = jnp.stack(
        [
            weights_one[:, at + front + split : at + front + split + small_width]
            for at in (0, first_width)
        ]
    )
    smalls = smalls.reshape(2, dp_count, -1)
    smalls = smalls.transpose(1, 0, 2).reshape(2 * dp_count, -1)
    sizes = [
        input_gain.shape[0],
        conv_weight.size,
        conv_bias.shape[0],
        mixer_gain.shape[0],
        hidden_gain.shape[0],
    ]
    places_at = [sum(sizes[:k]) for k in range(6)]
    gains = [
        smalls[:, places_at[k] : places_at[k + 1]].reshape(-1).astype(jnp.float32)
        for k in range(5)
    ]
    full_input_gain, full_conv_weight, full_conv_bias, full_mixer_gain, full_hidden_gain = gains
    full_conv_weight = full_conv_weight.reshape(-1, CONV)

    half_rows = rows // 2

    def half_sums(grad):
        return [
            Scatter(grad[:, :, :, :half_rows], SEQ_FIRST),
            Scatter(grad[:, :, :, half_rows:], ROW_FIRST),
        ]

    def row_major(value):
        return with_layout_constraint(value, Layout(tuple(range(value.ndim))))

    def weight_grad(left, right):
        core, row, far = dp_factors()
        grad = row_major(dot_left_t(left, right).astype(low))
        return grad.reshape(far, row, core, -1, right.shape[1])


    seg_all = segments[0]
    tail = lax.ppermute(tokens[row_count - halo :], "seq", [(0, 1)])
    hidden_ext = jnp.concatenate([tail, tokens]).astype(jnp.float32)
    padded_seg = jnp.concatenate([jnp.full((halo,), -1, jnp.int32), seg_all])
    seg_ext = lax.dynamic_slice_in_dim(padded_seg, seq_rank * row_count, count)
    padded_places = jnp.concatenate([jnp.zeros((halo,), jnp.int32), doc_places(seg_all)])
    places = lax.dynamic_slice_in_dim(padded_places, seq_rank * row_count, count)
    seg_rows = seg_ext[halo:]

    normed, norm_pull = jax.vjp(rms_scale, hidden_ext, full_input_gain)
    normed_low = normed.astype(low)
    normed_own = normed_low[halo:]
    f32 = jnp.float32
    seg_col, seg_row = seg_ext[:, None], seg_ext[None, :]
    half = HEAD_DIM // 2
    lane = jnp.arange(PAIR)
    angle = places.astype(f32)[:, None] * (THETA ** (-(lane % half).astype(f32) / half))[None, :]
    cosine = jnp.cos(angle)
    sine = jnp.sin(angle) * jnp.where(lane % HEAD_DIM < half, -1.0, 1.0)[None, :]
    projected = row_major(dot_plain(normed_low, weights_one))
    second_near, projected = join(second_near, projected)
    second_near = finish_rings(second_near, NEAR)
    base_out = 2 * half_ff
    base_down = base_out + 2 * half_width
    second_near, projected = join(
        [
            [value[..., :base_down] for value in second_near],
            [value[..., base_down:] for value in second_near],
        ],
        projected,
    )
    second_last = start_rings(second_near[0], LAST)
    blocks = [at + k for at in (0, first_width // PAIR) for k in range(front // PAIR)]
    turned, attended_low = call(
        attention_forward,
        [((count, 2 * front), low), ((row_count, HEADS * HEAD_DIM), low)],
        [],
        10**9,
        *[projected] * len(blocks),
        cosine,
        sine,
        seg_col,
        seg_row,
        blocks=blocks,
    )
    projected, attended_low = join(projected, attended_low)

    chunks = count // CHUNK
    seg_conv = jnp.concatenate(
        [jnp.full((8,), -1, jnp.int32), seg_ext, jnp.full((8,), -9, jnp.int32)]
    )
    seg_conv = seg_conv[:, None]
    seg_chunks = jnp.concatenate([seg_ext.reshape(chunks, CHUNK)] * 2, axis=1)
    taps = jnp.concatenate([full_conv_weight.T, full_conv_bias[None]])
    heads = jnp.stack([step_bias, jnp.exp(decay_log)])
    wide = jnp.stack([jnp.repeat(skip_gain, SSM_DIM), full_mixer_gain])
    mixed_low, mix, states = call(
        mixer_forward,
        [
            ((row_count, INNER), low),
            ((row_count, INNER), f32),
            ((chunks, STATE, INNER), low),
        ],
        [(count + 8, CHANNELS), (STATE, INNER), (CHUNK, INNER)],
        10**9,
        projected,
        taps,
        heads,
        wide,
        seg_conv,
        seg_chunks,
    )
    second_last, mixed_low = join(second_last, mixed_low)
    second_last = finish_rings(second_last, LAST)
    second_near[1], second_last = join(second_near[1], second_last)
    third_last = start_rings(second_near[1], LAST)
    pieces, down_pieces = [], []
    for half in range(2):
        pieces.append((half, slice(0, base_out), 0, both[half]))
        for k in range(2):
            at = k * rows + half * (rows // 2)
            columns = slice(k * half_width, (k + 1) * half_width)
            down_pieces.append((half, columns, 0, slice(at, at + rows // 2)))
            columns = slice(base_out + k * half_width, base_out + (k + 1) * half_width)
            if at < mixer_out.shape[0]:
                pieces.append((half, columns, 1, slice(at, at + rows // 2)))
            else:
                at -= mixer_out.shape[0]
                pieces.append((half, columns, 2, slice(at, at + rows // 2)))
    gate_up, full_mixer_out, full_output = assemble(
        exchange_cores(second_last),
        pieces,
        [
            (rows, base_out),
            (mixer_out.shape[0], half_width),
            (w_output.shape[0], half_width),
        ],
    )
    hidden_mid = (
        hidden_ext[halo:]
        + dot_plain(attended_low, full_output)
        + dot_plain(mixed_low, full_mixer_out)
    )
    normed_two, norm_two_pull = jax.vjp(rms_scale, hidden_mid, full_hidden_gain)
    normed_two_low = normed_two.astype(low)
    third_last, normed_two_low = join(third_last, normed_two_low)
    third_cores = exchange_cores(finish_rings(third_last, LAST))
    gate_up_part = dot_plain(normed_two_low, gate_up)
    ffn = []
    for k in range(2):
        gate_part, up_part = (
            gate_up_part[:, at : at + half_ff]
            for at in (2 * k * half_ff, (2 * k + 1) * half_ff)
        )
        sigmoid_gate = jax.nn.sigmoid(gate_part)
        ffn.append((gate_part, up_part, sigmoid_gate))
    (full_down,) = assemble(third_cores, down_pieces, [(w_down.shape[0], half_width)])
    activated_low = jnp.concatenate([(g * s * u).astype(low) for g, u, s in ffn], axis=1)
    output = (hidden_mid + dot_plain(activated_low, full_down)).astype(low)

    grad_down = weight_grad(activated_low, cotangent)
    down = Scatter(grad_down, ROW_FIRST)
    down.start()
    act_grad = dot_right_t(cotangent, full_down)
    gate_up_grad = []
    for k in range(2):
        gate_grad, up_grad = ffn_backward_grads(
            act_grad[:, k * half_ff : (k + 1) * half_ff], *ffn[k]
        )
        gate_up_grad += [gate_grad, up_grad]
    gate_up_grad = jnp.concatenate(gate_up_grad, axis=1)
    (gate_up_grad,) = meet([down], gate_up_grad)
    down.start()
    grad_gate_up = weight_grad(normed_two_low, gate_up_grad)
    grad_gate_up, gate_up_grad = join(grad_gate_up, gate_up_grad)
    ffn_sums = half_sums(grad_gate_up)
    start_all(ffn_sums)
    normed_two_grad = row_major(
        dot_right_t(gate_up_grad, gate_up)
    )
    hidden_part, hidden_gain_grad = norm_two_pull(normed_two_grad)
    hidden_grad = cotangent.astype(jnp.float32) + hidden_part
    branch_low = hidden_grad.astype(low)
    (branch_low,) = meet(ffn_sums, branch_low)
    start_all(ffn_sums)

    grad_outs = jnp.concatenate(
        [
            weight_grad(mixed_low, branch_low),
            weight_grad(attended_low, branch_low),
        ],
        axis=3,
    )
    outs = Scatter(grad_outs, ROW_FIRST)
    outs.start()
    attended_grad = dot_right_t(branch_low, full_output).astype(low)
    norm_grad = row_major(dot_right_t(branch_low, full_mixer_out))
    (qkv_grad,) = call(
        attention_backward,
        [((count, 2 * front), low)],
        [(count, PAIR), (count, PAIR)],
        10**9,
        turned,
        attended_grad,
        cosine,
        sine,
        seg_col,
        seg_row,
    )
    others = [*ffn_sums, down, outs]
    qkv_grad, norm_grad = meet(others, qkv_grad, norm_grad)
    (qkv_grad,) = settle(others, qkv_grad)
    start_all(others)
    proj_grad, small_sums = call(
        mixer_backward,
        [
            ((count, 2 * first_width), low),
            ((16, CHANNELS), f32),
        ],
        [
            (count + 8, CHANNELS),
            (8, CHANNELS),
            (STATE, INNER),
            (CHUNK, INNER),
            (CHUNK, INNER),
        ],
        10**9,
        projected,
        mix,
        states,
        norm_grad,
        qkv_grad,
        taps,
        heads,
        wide,
        seg_conv,
        seg_chunks,
    )
    (proj_grad,) = meet(others, proj_grad)
    (proj_grad,) = settle(others, proj_grad)
    start_all(others)
    grad_first = weight_grad(normed_low, proj_grad)
    grad_first, proj_grad = meet(others, grad_first, proj_grad)
    first = half_sums(grad_first)
    start_all(first)
    normed_grad = row_major(dot_right_t(proj_grad, weights_one))
    normed_grad, small_sums, hidden_gain_grad = meet(
        first, normed_grad, small_sums, hidden_gain_grad
    )
    normed_grad, small_sums, hidden_gain_grad = settle(
        first, normed_grad, small_sums, hidden_gain_grad
    )
    start_all(first)
    input_part, input_gain_grad = norm_pull(normed_grad)
    returned = lax.ppermute(input_part[:halo].astype(low), "seq", [(1, 0)]).astype(jnp.float32)
    token_grad = hidden_grad + input_part[halo:]
    token_grad = token_grad + jnp.pad(returned, ((row_count - halo, 0), (0, 0)))

    gain_rows = jnp.stack([hidden_gain_grad, input_gain_grad])
    small = Total(small_sums + jnp.pad(gain_rows, ((9, 5), (0, CHANNELS - width))))
    small.start()
    meet([small])
    rings = others[:3]
    moving, outs.value, small.value = join(
        [chain.moving for chain in rings], outs.value, small.value
    )
    for chain, value in zip(rings, moving, strict=True):
        chain.moving = value
    start_all([small, *others])
    meet([*first, small, *others])
    start_all([*first, small, *others])
    meet([*first, small, *others])
    last = Scatter(jnp.concatenate([chain.value for chain in first], axis=3), ("far",))
    last.start(direct=True)
    start_all([small, outs])
    meet([last, small, outs])
    grad_down = down.value.reshape(-1, half_width)
    grad_gate_up = jnp.concatenate(
        [chain.value.reshape(half_rows, -1) for chain in ffn_sums]
    )
    grad_outs = outs.value.reshape(-1, half_width)
    grad_mixer_out = grad_outs[: mixer_out.shape[0]]
    grad_output = grad_outs[mixer_out.shape[0] :]
    grad_first = last.value.reshape(rows, first_width)
    sums = small.value
    place = lax.axis_index("dp") * 2 + seq_rank

    def own_part(row, size):
        return lax.dynamic_slice(sums, (row, place * size), (1, size)).reshape(-1)

    own_taps = lax.dynamic_slice(sums, (0, place * sizes[2]), (CONV, sizes[2]))
    skip_grad = jnp.sum(sums[6, :INNER].reshape(SSM_HEADS, SSM_DIM), axis=1)
    return (
        output,
        token_grad,
        own_part(10, sizes[0]),
        grad_first[:, front : front + split],
        own_taps.T,
        own_part(CONV, sizes[2]),
        sums[7, :SSM_HEADS],
        sums[8, :SSM_HEADS],
        skip_grad,
        own_part(5, sizes[3]),
        grad_mixer_out,
        grad_first[:, :half_q],
        grad_first[:, half_q : half_q + half_k],
        grad_first[:, half_q + half_k : front],
        grad_output,
        own_part(9, sizes[4]),
        grad_gate_up[:, :half_ff],
        grad_gate_up[:, half_ff:],
        grad_down,
    )


def solution(mesh):
    placed = (
        P(("dp", "seq"), None),
        P("dp", None),
        P(("dp", "seq")),
        P("dp", "seq"),
        P(("dp", "seq"), None),
        P(("dp", "seq")),
        P(),
        P(),
        P(),
        P(("dp", "seq")),
        P("dp", "seq"),
        P("dp", "seq"),
        P("dp", "seq"),
        P("dp", "seq"),
        P("dp", "seq"),
        P(("dp", "seq")),
        P("dp", "seq"),
        P("dp", "seq"),
        P("dp", "seq"),
        P(("dp", "seq"), None),
    )
    return jax.shard_map(
        shards_halo if mesh.shape["seq"] == 2 else shards_general,
        mesh=mesh,
        in_specs=placed,
        out_specs=(
            P(("dp", "seq"), None),
            P(("dp", "seq"), None),
            P(("dp", "seq")),
            P("dp", "seq"),
            P(("dp", "seq"), None),
            P(("dp", "seq")),
            P(),
            P(),
            P(),
            P(("dp", "seq")),
            P("dp", "seq"),
            P("dp", "seq"),
            P("dp", "seq"),
            P("dp", "seq"),
            P("dp", "seq"),
            P(("dp", "seq")),
            P("dp", "seq"),
            P("dp", "seq"),
            P("dp", "seq"),
        ),
        check_vma=False,
    )
```
